32 devices in a mesh: dp: 2 (over core), expert: 16 (over z, y, x).
Axes of the slice: x: 2, y: 2, z: 4, core: 2. Of those that a mesh axis runs over, the one named last changes fastest.
Arguments:
- tokens: bfloat16 [4096, 2048], P(('dp', 'expert')), parts along dimension 0, may hold values from -6 to 6
- cotangent: bfloat16 [4096, 2048], P(('dp', 'expert')), parts along dimension 0, may hold values from -6 to 6
- expert_ids: int32 [4096, 10], P(('dp', 'expert')), parts along dimension 0, may hold values from 0 to 31, all different within a row; in each aligned block of 128 rows (0 to 127, 128 to 255, ...) at most 48 rows name the same one
- probs: float32 [4096, 10], P(('dp', 'expert')), parts along dimension 0, may hold values from 0.05 to 0.5
- gate_weight: bfloat16 [64, 2048, 256], P(('dp', 'expert')), parts along dimension 0, may hold values from -0.125 to 0.125
- up_weight: bfloat16 [64, 2048, 256], P(('dp', 'expert')), parts along dimension 0, may hold values from -0.125 to 0.125
- down_weight: bfloat16 [64, 256, 2048], P(('dp', 'expert')), parts along dimension 0, may hold values from -0.375 to 0.375
Outputs:
- mixed: float32 [4096, 2048], P(('dp', 'expert')), parts along dimension 0
- input_grad: float32 [4096, 2048], P(('dp', 'expert')), parts along dimension 0
The draws below stay inside these ranges and needn't reach their ends.
There are 2 independent parts, one for each index of `dp`. The reference program is written for one: setup_inputs(seed, part) draws one part's arguments, and reference() takes and returns one part's arrays. A program takes and returns all parts, laid end to end along the dimension named above; each array names one. Nothing has to cross between parts.
Inputs may be any that keep to these rules, and one draw needn't show every extreme that they name: `expert_ids`: each row names 10 different experts. Within the 128 rows of one device no expert is named by more than 48 rows, and in some of these blocks one expert is named by exactly 48 rows; loads across experts are skewed.
All inputs are finite; a program needn't handle non-finite values.
Results may differ from the reference program's by a relative error of at most 0.0041.
Values may be sent and summed in bfloat16 or wider, within the bound.
No kernel may reach another device: no remote copies, remote signals or barrier semaphores. Data moves between devices by JAX's collectives and lax.ppermute only.
A program may use at most 128 MiB of HBM per device.

```python
import math
import jax
import jax.numpy as jnp
import numpy as np
from jax import lax

D = 2048
H = 256
TOP_K = 10
TOK_DEV = 128
EXPERTS = 32
TOKENS = 2048
CAP = 48
N_EXPERT = 16


def steps_of(own_key, shape, split, low, top_value):
    def one(axis_at, blocks):
        steps = jax.random.uniform(jax.random.fold_in(jax.random.fold_in(own_key, 6), axis_at), (blocks,), jnp.float32, low / len(split), top_value / len(split))
        return jnp.repeat(jnp.exp(steps), shape[axis_at] // blocks).reshape((-1,) + (1,) * (len(shape) - axis_at - 1))

    loudness = one(*split[0])
    for cut in split[1:]:
        loudness = loudness * one(*cut)
    return loudness


def deal_out(stream_key, own, number, rows, amount, top, reach, lean):
    order = jax.random.permutation(stream_key, amount)
    packed, ordinary = shares(amount, rows * top, reach, lean, True), shares(amount, rows * top, reach, lean, False)
    places = jnp.arange(amount)

    def named(lengths, offset_by):
        used = int((lengths > 0).sum())
        fixed = max(1, used // 4)
        passed = fixed + (places - fixed + offset_by * (used - fixed)) % max(1, amount - fixed)
        return jnp.zeros((amount,), jnp.int32).at[order[jnp.where(places < fixed, places, passed)]].set(jnp.asarray(lengths, jnp.int32))

    lengths = jnp.where(number % 4 == 0, named(packed, number // 4), named(ordinary, number - number // 4 - 1))
    mixed = jax.random.permutation(jax.random.fold_in(own, 3), amount)
    giver, taker = mixed[0:amount // 2 * 2:2], mixed[1:amount // 2 * 2:2]
    room = jnp.minimum(lengths[giver] - 1, reach - lengths[taker]) // 2
    room = jnp.where((giver == order[0]) | (taker == order[0]) | (lengths[taker] == 0), 0, jnp.maximum(room, 0))
    passed = jax.random.randint(jax.random.fold_in(own, 4), (amount // 2,), 0, 1 << 20) % (room + 1)
    lengths = lengths.at[giver].add(-passed).at[taker].add(passed)
    members = jnp.searchsorted(jnp.cumsum(lengths), jnp.arange(rows * top), side="right").astype(jnp.int32)
    grid = members.reshape(top, rows).T
    grid = grid[jax.random.permutation(jax.random.fold_in(own, 1), rows)]
    offset_by = jax.random.randint(jax.random.fold_in(own, 2), (rows, 1), 0, top)
    return jnp.take_along_axis(grid, (jnp.arange(top)[None, :] + offset_by) % top, axis=1)


def shares(amount, total, reach, skew, full):
    loads = [(1 << 20) // math.isqrt(standing ** skew) + 1 for standing in range(1, amount + 1)]
    largest = reach if full else min(reach, max(-(-total // amount), total * loads[0] // sum(loads)))
    least = 1 if total - largest >= amount - 1 else 0
    given, surplus = [largest] + [least] * (amount - 1), total - largest - least * (amount - 1)
    while surplus > 0:
        candidates = [i for i in range(1, amount) if given[i] < largest] or [i for i in range(1, amount) if given[i] < reach]
        whole, left = sum([loads[i] for i in candidates]), surplus
        for i in candidates:
            more = min(reach - given[i], max(1, left * loads[i] // whole), surplus)
            given[i] = given[i] + more
            surplus = surplus - more
    return np.array(given)


def normal_values(stream_key, dims, width, reach, cuts=(), kind=jnp.bfloat16):
    entries = jax.random.normal(stream_key, dims, jnp.float32) * width
    if len(cuts) > 0:
        entries = steps_of(stream_key, dims, cuts, -0.22, 0.18) * entries
    return jnp.clip(entries, min=-reach, max=reach).astype(kind)


def setup_inputs(seed: int = 0, part: int = 0) -> dict:
    keys = jax.random.split(jax.random.key(seed), 8)
    part_keys = jax.random.split(jax.random.fold_in(keys[7], part), 8)
    tokens = normal_values(part_keys[0], (TOKENS, D), 1.0, 6.0, ((0, 16),))
    cotangent = normal_values(part_keys[1], (TOKENS, D), 1.0, 6.0, ((0, 16),))
    expert_ids_keys = jax.random.split(jax.random.fold_in(part_keys[2], 1), TOKENS // TOK_DEV)
    expert_ids_turns = jax.random.permutation(jax.random.fold_in(part_keys[2], 3), TOKENS // TOK_DEV)
    expert_ids = jax.vmap(lambda own, number: deal_out(jax.random.fold_in(part_keys[2], 2), own, number, TOK_DEV, EXPERTS, TOP_K, CAP, 2))(expert_ids_keys, expert_ids_turns).reshape((TOKENS, TOP_K))
    probs = jnp.clip(jnp.exp(math.log(0.5) - 2.3025851 * jax.random.uniform(part_keys[3], (TOKENS, TOP_K), jnp.float32) ** steps_of(part_keys[3], (TOKENS, TOP_K), ((0, 16),), -0.2, 0.2)), 0.05, 0.5)
    gate_weight = normal_values(part_keys[4], (EXPERTS, D, H), D ** -0.5, 0.125, ((0, 16),))
    up_weight = normal_values(part_keys[5], (EXPERTS, D, H), D ** -0.5, 0.125, ((0, 16),))
    down_weight = normal_values(part_keys[6], (EXPERTS, H, D), H ** -0.5, 0.375, ((0, 16),))
    return {"tokens": tokens, "cotangent": cotangent, "expert_ids": expert_ids, "probs": probs, "gate_weight": gate_weight, "up_weight": up_weight, "down_weight": down_weight}


def expert_pass(row_block, grad_block, w_gate, w_up, w_down):
    gate_pre = jnp.dot(row_block, w_gate, preferred_element_type=jnp.float32)
    up_pre = jnp.dot(row_block, w_up, preferred_element_type=jnp.float32)
    sigmoid_gate = jax.nn.sigmoid(gate_pre)
    activ = (gate_pre * sigmoid_gate * up_pre).astype(jnp.bfloat16)
    expert_out = jnp.dot(activ, w_down, preferred_element_type=jnp.float32).astype(jnp.bfloat16)
    grad_act = jnp.dot(grad_block, w_down.T, preferred_element_type=jnp.float32)
    grad_gate = (grad_act * up_pre * sigmoid_gate * (1.0 + gate_pre * (1.0 - sigmoid_gate))).astype(jnp.bfloat16)
    grad_up = (grad_act * gate_pre * sigmoid_gate).astype(jnp.bfloat16)
    expert_back = (jnp.dot(grad_gate, w_gate.T, preferred_element_type=jnp.float32)
                   + jnp.dot(grad_up, w_up.T, preferred_element_type=jnp.float32)).astype(jnp.bfloat16)
    return expert_out, expert_back


def reference(tokens, cotangent, expert_ids, probs, gate_weight, up_weight, down_weight):
    row_count = TOKENS * TOP_K
    most_rows = N_EXPERT * CAP
    flat_ids = expert_ids.reshape(row_count).astype(jnp.int32)
    sort_order = jnp.argsort(flat_ids, stable=True).astype(jnp.int32)
    counts = jnp.zeros((EXPERTS,), jnp.int32).at[flat_ids].add(1)
    starts = (jnp.cumsum(counts) - counts).astype(jnp.int32)
    padded = jnp.concatenate([sort_order, jnp.zeros((most_rows,), jnp.int32)])
    flat_probs = probs.reshape(row_count)

    def expert_step(state_pair, expert):
        summed, grad_sum = state_pair
        row_index = lax.dynamic_slice_in_dim(padded, starts[expert], most_rows)
        live_mask = jnp.arange(most_rows, dtype=jnp.int32) < counts[expert]
        token_index = (row_index // TOP_K).astype(jnp.int32)
        weight = jnp.where(live_mask, flat_probs[row_index], jnp.zeros_like(flat_probs[row_index]))
        expert_out, expert_back = expert_pass(tokens[token_index], cotangent[token_index],
                                              gate_weight[expert], up_weight[expert], down_weight[expert])
        summed = summed.at[token_index].add(weight[:, None] * expert_out.astype(jnp.float32))
        grad_sum = grad_sum.at[token_index].add(weight[:, None] * expert_back.astype(jnp.float32))
        return (summed, grad_sum), None

    start_pair = (jnp.zeros((TOKENS, D), jnp.float32), jnp.zeros((TOKENS, D), jnp.float32))
    (mixed, input_grad), _ = lax.scan(expert_step, start_pair, jnp.arange(EXPERTS, dtype=jnp.int32))
    return mixed, input_grad
```

```python
import functools

import jax
import jax.numpy as jnp
from jax import lax
from jax.experimental import pallas as pl
from jax.experimental.pallas import tpu as pltpu
from jax.sharding import PartitionSpec as P

VMEM_BYTES = 48 * 2**20


def forward_kernel(first, *refs):
    if first:
        rows_ref, weight_ref, gate_ref, up_ref, down_ref, mixed_ref, by_gate_ref, by_up_ref = refs
        mixed = None
    else:
        rows_ref, weight_ref, gate_ref, up_ref, down_ref, so_far_ref, mixed_ref, by_gate_ref, by_up_ref = refs
        mixed = so_far_ref[...]
    local_count, _, hidden = gate_ref.shape
    rows = rows_ref[...]
    for e in range(local_count):
        cut = slice(e * hidden, (e + 1) * hidden)
        gate_pre = jnp.dot(rows, gate_ref[e], preferred_element_type=jnp.float32)
        up_pre = jnp.dot(rows, up_ref[e], preferred_element_type=jnp.float32)
        sig = jax.nn.sigmoid(gate_pre)
        silu = gate_pre * sig
        activ = (silu * up_pre).astype(jnp.bfloat16)
        by_gate_ref[:, cut] = up_pre * sig * (1.0 + gate_pre * (1.0 - sig))
        by_up_ref[:, cut] = silu
        out = jnp.dot(activ, down_ref[e], preferred_element_type=jnp.float32)
        out = out.astype(jnp.bfloat16).astype(jnp.float32) * weight_ref[:, e : e + 1]
        mixed = out if mixed is None else mixed + out
    mixed_ref[...] = mixed.astype(mixed_ref.dtype)


def backward_kernel(first, *refs):
    if first:
        grads_ref, weight_ref, by_gate_ref, by_up_ref, gate_ref, up_ref, down_ref, back_ref = refs
        total = None
    else:
        grads_ref, weight_ref, by_gate_ref, by_up_ref, gate_ref, up_ref, down_ref, so_far_ref, back_ref = refs
        total = so_far_ref[...]
    local_count, _, hidden = gate_ref.shape
    grads = grads_ref[...]
    nt = (((1,), (1,)), ((), ()))
    for e in range(local_count):
        cut = slice(e * hidden, (e + 1) * hidden)
        grad_act = lax.dot_general(grads, down_ref[e], nt, preferred_element_type=jnp.float32)
        grad_gate = (grad_act * by_gate_ref[:, cut]).astype(jnp.bfloat16)
        grad_up = (grad_act * by_up_ref[:, cut]).astype(jnp.bfloat16)
        back = lax.dot_general(grad_gate, gate_ref[e], nt, preferred_element_type=jnp.float32)
        back += lax.dot_general(grad_up, up_ref[e], nt, preferred_element_type=jnp.float32)
        back = back.astype(jnp.bfloat16).astype(jnp.float32) * weight_ref[:, e : e + 1]
        total = back if total is None else total + back
    back_ref[...] = total.astype(back_ref.dtype)


def row_tile(rows):
    return 256 if rows % 256 == 0 else rows


def whole(array):
    return pl.BlockSpec(array.shape, lambda i: (0,) * array.ndim)


def tiled(tile, columns):
    return pl.BlockSpec((tile, columns), lambda i: (i, 0))


def forward_dense(rows, weight, gate_weight, up_weight, down_weight, so_far=None):
    count, width = rows.shape
    experts, _, hidden = gate_weight.shape
    tile = row_tile(count)
    first = so_far is None
    sum_type = jnp.float32 if first else jnp.bfloat16
    return pl.pallas_call(
        functools.partial(forward_kernel, first),
        grid=(count // tile,),
        in_specs=[
            tiled(tile, width),
            tiled(tile, experts),
            whole(gate_weight),
            whole(up_weight),
            whole(down_weight),
        ]
        + ([] if first else [tiled(tile, width)]),
        out_specs=[tiled(tile, width), tiled(tile, experts * hidden), tiled(tile, experts * hidden)],
        out_shape=[
            jax.ShapeDtypeStruct((count, width), sum_type),
            jax.ShapeDtypeStruct((count, experts * hidden), jnp.float32),
            jax.ShapeDtypeStruct((count, experts * hidden), jnp.float32),
        ],
        compiler_params=pltpu.CompilerParams(vmem_limit_bytes=VMEM_BYTES),
        cost_estimate=pl.CostEstimate(
            flops=6 * count * experts * width * hidden,
            bytes_accessed=6 * count * width + 8 * count * experts * hidden + 6 * gate_weight.size,
            transcendentals=count * experts * hidden,
        ),
        name="forward_dense",
    )(rows, weight, gate_weight, up_weight, down_weight, *([] if first else [so_far]))


def backward_dense(grads, weight, by_gate, by_up, gate_weight, up_weight, down_weight, so_far=None):
    count, width = grads.shape
    experts, _, hidden = gate_weight.shape
    tile = row_tile(count)
    first = so_far is None
    sum_type = jnp.float32 if first else jnp.bfloat16
    return pl.pallas_call(
        functools.partial(backward_kernel, first),
        grid=(count // tile,),
        in_specs=[
            tiled(tile, width),
            tiled(tile, experts),
            tiled(tile, experts * hidden),
            tiled(tile, experts * hidden),
            whole(gate_weight),
            whole(up_weight),
            whole(down_weight),
        ]
        + ([] if first else [tiled(tile, width)]),
        out_specs=tiled(tile, width),
        out_shape=jax.ShapeDtypeStruct((count, width), sum_type),
        compiler_params=pltpu.CompilerParams(vmem_limit_bytes=VMEM_BYTES),
        cost_estimate=pl.CostEstimate(
            flops=6 * count * experts * width * hidden,
            bytes_accessed=6 * count * width + 8 * count * experts * hidden + 6 * gate_weight.size,
            transcendentals=0,
        ),
        name="backward_dense",
    )(grads, weight, by_gate, by_up, gate_weight, up_weight, down_weight, *([] if first else [so_far]))


def on_device_dense(tokens, cotangent, expert_ids, probs, gate_weight, up_weight, down_weight):
    local_count = gate_weight.shape[0]
    devices = lax.axis_size("expert")
    experts = local_count * devices
    teams = [list(range(side, devices, 2)) for side in range(2)]
    pairs = [(d, d ^ 1) for d in range(devices)]
    labels = lax.broadcasted_iota(jnp.int32, (1, 1, experts), 2)
    weight = jnp.sum(jnp.where(expert_ids[:, :, None] == labels, probs[:, :, None], 0.0), axis=1)

    def gather(values):
        return lax.all_gather(values, "expert", axis_index_groups=teams, axis=0, tiled=True)

    def reduce(values):
        summed = lax.psum_scatter(
            values, "expert", scatter_dimension=0, axis_index_groups=teams, tiled=True
        )
        return summed.astype(jnp.float32)

    other = [lax.ppermute(w, "expert", pairs) for w in (gate_weight, up_weight, down_weight)]
    all_rows = gather(tokens)
    all_weight = gather(weight)
    all_grads = gather(cotangent)
    me = lax.axis_index("expert")
    own_weight = lax.dynamic_slice_in_dim(all_weight, me * local_count, local_count, axis=1)
    other_weight = lax.dynamic_slice_in_dim(all_weight, (me ^ 1) * local_count, local_count, axis=1)
    own = (gate_weight, up_weight, down_weight)
    mixed, by_gate, by_up = forward_dense(all_rows, own_weight, *own)
    back = backward_dense(all_grads, own_weight, by_gate, by_up, *own)
    mixed, by_gate, by_up = forward_dense(all_rows, other_weight, *other, so_far=mixed)
    mixed = reduce(mixed)
    back = backward_dense(all_grads, other_weight, by_gate, by_up, *other, so_far=back)
    back = reduce(back)
    return (mixed, back)


def route_slots(expert_ids, local_count, device_count, capacity):
    experts = local_count * device_count
    row_count = expert_ids.shape[0] * expert_ids.shape[1]
    flat_ids = expert_ids.reshape(row_count)
    sort_order = jnp.argsort(flat_ids, stable=True)
    labels = lax.broadcasted_iota(jnp.int32, (1, experts), 1)
    counts = jnp.sum((flat_ids[:, None] == labels).astype(jnp.int32), axis=0)
    starts = jnp.cumsum(counts) - counts
    sorted_ids = flat_ids[sort_order]
    rank_within = jnp.arange(row_count, dtype=jnp.int32) - starts[sorted_ids]
    owner = sorted_ids // local_count
    local_slot = sorted_ids % local_count
    target = local_slot * (device_count * capacity) + owner * capacity + rank_within
    source_of = jnp.full((experts * capacity,), row_count, jnp.int32).at[target].set(sort_order)
    target_of = jnp.zeros((row_count,), jnp.int32).at[sort_order].set(target)
    return (source_of, target_of)


def pack_rows(values, source_of, top_count, local_count):
    token_count = values.shape[0]
    with_zero = jnp.concatenate([values, jnp.zeros((1, values.shape[1]), values.dtype)], axis=0)
    token_index = jnp.minimum(source_of // top_count, token_count)
    picked = with_zero[token_index]
    return picked.reshape(local_count, -1, values.shape[1])


def forward_part(received, gate_weight, up_weight, down_weight):
    gate_pre = jnp.einsum("erd,edh->erh", received, gate_weight, preferred_element_type=jnp.float32)
    up_pre = jnp.einsum("erd,edh->erh", received, up_weight, preferred_element_type=jnp.float32)
    sigmoid_gate = jax.nn.sigmoid(gate_pre)
    activ = (gate_pre * sigmoid_gate * up_pre).astype(jnp.bfloat16)
    expert_out = jnp.einsum("erh,ehd->erd", activ, down_weight, preferred_element_type=jnp.float32)
    return (expert_out.astype(jnp.bfloat16), gate_pre, up_pre, sigmoid_gate)


def backward_part(grad_rows, gate_pre, up_pre, sigmoid_gate, gate_weight, up_weight, down_weight):
    grad_act = jnp.einsum(
        "erd,ehd->erh", grad_rows, down_weight, preferred_element_type=jnp.float32
    )
    grad_gate = (grad_act * up_pre * sigmoid_gate * (1.0 + gate_pre * (1.0 - sigmoid_gate))).astype(
        jnp.bfloat16
    )
    grad_up = (grad_act * gate_pre * sigmoid_gate).astype(jnp.bfloat16)
    joined_grad = jnp.concatenate([grad_gate, grad_up], axis=2)
    joined_weight = jnp.concatenate([gate_weight, up_weight], axis=2)
    expert_back = jnp.einsum(
        "erh,edh->erd", joined_grad, joined_weight, preferred_element_type=jnp.float32
    )
    return expert_back.astype(jnp.bfloat16)


def combine_rows(returned, target_of, probs):
    token_count, top_count = probs.shape
    flat_back = returned.reshape(-1, returned.shape[2])
    picked = flat_back[target_of].reshape(token_count, top_count, returned.shape[2])
    return jnp.sum(picked.astype(jnp.float32) * probs[:, :, None], axis=1)


def on_device_routed(tokens, cotangent, expert_ids, probs, gate_weight, up_weight, down_weight):
    local_count = gate_weight.shape[0]
    device_count = lax.axis_size("expert")
    experts = local_count * device_count
    token_count, top_count = expert_ids.shape
    row_count = token_count * top_count
    capacity = row_count * 6 // (5 * experts)
    source_of, target_of = route_slots(expert_ids, local_count, device_count, capacity)
    send_rows = pack_rows(tokens, source_of, top_count, local_count)
    send_grads = pack_rows(cotangent, source_of, top_count, local_count)
    received = lax.all_to_all(send_rows, "expert", split_axis=1, concat_axis=1, tiled=True)
    expert_out, gate_pre, up_pre, sigmoid_gate = forward_part(
        received, gate_weight, up_weight, down_weight
    )
    returned_out = lax.all_to_all(expert_out, "expert", split_axis=1, concat_axis=1, tiled=True)
    received_grads = lax.all_to_all(send_grads, "expert", split_axis=1, concat_axis=1, tiled=True)
    expert_back = backward_part(
        received_grads, gate_pre, up_pre, sigmoid_gate, gate_weight, up_weight, down_weight
    )
    returned_back = lax.all_to_all(expert_back, "expert", split_axis=1, concat_axis=1, tiled=True)
    mixed = combine_rows(returned_out, target_of, probs)
    input_grad = combine_rows(returned_back, target_of, probs)
    return (mixed, input_grad)


def on_device(tokens, cotangent, expert_ids, probs, gate_weight, up_weight, down_weight):
    devices = lax.axis_size("expert")
    dense = devices % 2 == 0 and devices <= 2 * expert_ids.shape[1]
    body = on_device_dense if dense else on_device_routed
    return body(tokens, cotangent, expert_ids, probs, gate_weight, up_weight, down_weight)


def solution(mesh):
    in_specs = (
        P(("dp", "expert"), None),
        P(("dp", "expert"), None),
        P(("dp", "expert"), None),
        P(("dp", "expert"), None),
        P(("dp", "expert"), None, None),
        P(("dp", "expert"), None, None),
        P(("dp", "expert"), None, None),
    )
    out_specs = (P(("dp", "expert"), None), P(("dp", "expert"), None))
    return jax.shard_map(
        on_device, mesh=mesh, in_specs=in_specs, out_specs=out_specs, check_vma=False
    )
```

```python
import jax
import jax.numpy as jnp
from jax import lax
from jax.experimental import pallas as pl
from jax.experimental.pallas import tpu as pltpu
from jax.sharding import PartitionSpec as P

VMEM_BYTES = 48 * 2**20
CHUNKS = 4


def hidden_kernel(rows_ref, gate_ref, up_ref, activ_ref, by_gate_ref, by_up_ref):
    experts, _, hidden = gate_ref.shape
    rows = rows_ref[...]
    for e in range(experts):
        cut = slice(e * hidden, (e + 1) * hidden)
        gate_pre = jnp.dot(rows, gate_ref[e], preferred_element_type=jnp.float32)
        up_pre = jnp.dot(rows, up_ref[e], preferred_element_type=jnp.float32)
        sig = jax.nn.sigmoid(gate_pre)
        silu = gate_pre * sig
        activ_ref[:, cut] = (silu * up_pre).astype(jnp.bfloat16)
        by_gate_ref[:, cut] = up_pre * sig * (1.0 + gate_pre * (1.0 - sig))
        by_up_ref[:, cut] = silu


def split_store(total, keep_ref, send_ref):
    @pl.when(pl.program_id(0) == 0)
    def _():
        send_ref[...] = total.astype(send_ref.dtype)

    @pl.when(pl.program_id(0) == 1)
    def _():
        keep_ref[...] = total


def mix_kernel(weight_ref, own_ref, other_ref, own_down_ref, other_down_ref, keep_ref, send_ref):
    experts, hidden, _ = own_down_ref.shape
    total = None
    for side, (activ_ref, down_ref) in enumerate(((own_ref, own_down_ref), (other_ref, other_down_ref))):
        for e in range(experts):
            cut = slice(e * hidden, (e + 1) * hidden)
            at = side * experts + e
            out = jnp.dot(activ_ref[:, cut], down_ref[e], preferred_element_type=jnp.float32)
            out = out.astype(jnp.bfloat16).astype(jnp.float32) * weight_ref[:, at : at + 1]
            total = out if total is None else total + out
    split_store(total, keep_ref, send_ref)


def back_kernel(weight_ref, *refs):
    keep_ref, send_ref = refs[-2:]
    experts, _, hidden = refs[2].shape
    nt = (((1,), (1,)), ((), ()))
    total = None
    for side in range(2):
        by_gate_ref, by_up_ref, gate_ref, up_ref = refs[4 * side : 4 * side + 4]
        for e in range(experts):
            cut = slice(e * hidden, (e + 1) * hidden)
            at = side * experts + e
            back = lax.dot_general(by_gate_ref[:, cut], gate_ref[e], nt, preferred_element_type=jnp.float32)
            back += lax.dot_general(by_up_ref[:, cut], up_ref[e], nt, preferred_element_type=jnp.float32)
            back = back.astype(jnp.bfloat16).astype(jnp.float32) * weight_ref[:, at : at + 1]
            total = back if total is None else total + back
    split_store(total, keep_ref, send_ref)


def hidden_forward(rows, gate_weight, up_weight):
    count = rows.shape[0]
    experts, width, hidden = gate_weight.shape
    tile = 256 if count % 256 == 0 else count
    columns = experts * hidden
    weights = pl.BlockSpec((experts, width, hidden), lambda i: (0, 0, 0))
    out = pl.BlockSpec((tile, columns), lambda i: (i, 0))
    return pl.pallas_call(
        hidden_kernel,
        grid=(count // tile,),
        in_specs=[pl.BlockSpec((tile, width), lambda i: (i, 0)), weights, weights],
        out_specs=[out, out, out],
        out_shape=[
            jax.ShapeDtypeStruct((count, columns), jnp.bfloat16),
            jax.ShapeDtypeStruct((count, columns), jnp.float32),
            jax.ShapeDtypeStruct((count, columns), jnp.float32),
        ],
        compiler_params=pltpu.CompilerParams(vmem_limit_bytes=VMEM_BYTES),
        cost_estimate=pl.CostEstimate(
            flops=4 * count * width * columns,
            bytes_accessed=2 * count * width + 10 * count * columns + 4 * gate_weight.size,
            transcendentals=count * columns,
        ),
        name="hidden_forward",
    )(rows, gate_weight, up_weight)


def halves_call(kernel, name, count, columns, flops, in_specs, operands):
    half = count // 2
    return pl.pallas_call(
        kernel,
        grid=(2,),
        in_specs=in_specs,
        out_specs=[pl.BlockSpec((half, columns), lambda i: (0, 0))] * 2,
        out_shape=[
            jax.ShapeDtypeStruct((half, columns), jnp.float32),
            jax.ShapeDtypeStruct((half, columns), jnp.bfloat16),
        ],
        compiler_params=pltpu.CompilerParams(vmem_limit_bytes=VMEM_BYTES),
        cost_estimate=pl.CostEstimate(
            flops=flops,
            bytes_accessed=sum(2 * x.size for x in operands) // 2 + 6 * half * columns,
            transcendentals=0,
        ),
        name=name,
    )(*operands)


def half_rows(array):
    return pl.BlockSpec((array.shape[0] // 2, array.shape[1]), lambda i: (1 - i, 0))


def mix_columns(weight, own, other, own_down, other_down, at):
    experts, hidden, columns = other_down.shape
    count = own.shape[0]
    specs = [
        half_rows(weight),
        half_rows(own),
        half_rows(other),
        pl.BlockSpec((experts, hidden, columns), lambda i: (0, 0, at)),
        pl.BlockSpec((experts, hidden, columns), lambda i: (0, 0, 0)),
    ]
    flops = 4 * count * experts * hidden * columns
    return halves_call(
        mix_kernel, "mix_columns", count, columns, flops, specs, (weight, own, other, own_down, other_down)
    )


def back_columns(weight, own, own_weights, other, other_weights, at, columns):
    experts, _, hidden = own_weights[0].shape
    count = weight.shape[0]
    weights = pl.BlockSpec((experts, columns, hidden), lambda i: (0, at, 0))
    specs = [half_rows(weight)]
    for grads in (own, other):
        specs += [half_rows(grads[0]), half_rows(grads[1]), weights, weights]
    flops = 8 * count * experts * hidden * columns
    return halves_call(
        back_kernel,
        "back_columns",
        count,
        columns,
        flops,
        specs,
        (weight, *own, *own_weights, *other, *other_weights),
    )


def on_device_dense(tokens, cotangent, expert_ids, probs, gate_weight, up_weight, down_weight):
    local_count, hidden, width = down_weight.shape
    devices = lax.axis_size("expert")
    layers = devices // 4
    experts = local_count * devices
    block = tokens.shape[0]
    columns = width // CHUNKS
    me = lax.axis_index("expert")

    def after(values, *others):
        return lax.optimization_barrier((values, *others))[0]

    def to_twin(values):
        return lax.ppermute(values, "expert", [(d, d ^ 1) for d in range(devices)])

    def to_side(values):
        return lax.ppermute(values, "expert", [(d, d ^ 2) for d in range(devices)])

    def to_layer(values, step):
        return lax.ppermute(values, "expert", [(d, (d + 4 * step) % devices) for d in range(devices)])

    def gather(values):
        near = [values] + [to_layer(values, -k) for k in range(1, layers)]
        return near, jnp.concatenate(near + [to_side(v) for v in near], axis=0)

    def reduce_start(keep, send):
        come = to_side(send).astype(jnp.float32)
        total = keep + come
        own = total[:block]
        return [own] + [
            to_layer(total[k * block : (k + 1) * block].astype(jnp.bfloat16), k) for k in range(1, layers)
        ]

    def reduce_end(parts):
        return jnp.concatenate([sum(p.astype(jnp.float32) for p in part) for part in parts], axis=1)

    labels = lax.broadcasted_iota(jnp.int32, (1, 1, experts), 2)
    weight = jnp.sum(jnp.where(expert_ids[:, :, None] == labels, probs[:, :, None], 0.0), axis=1)
    first = lax.reduce_precision(weight, 8, 7)
    second = lax.reduce_precision(weight - first, 8, 7)
    third = weight - first - second
    spare = jnp.zeros((block, -3 * experts % 128), jnp.bfloat16)
    terms = [t.astype(jnp.bfloat16) for t in (first, second, third)]
    rows = jnp.concatenate([tokens] + terms + [spare], axis=1)

    near, all_rows = gather(rows)
    other_gate = to_twin(gate_weight)
    other_up = to_twin(up_weight)
    other_down = []
    for c in range(CHUNKS):
        piece = down_weight[:, :, c * columns : (c + 1) * columns]
        other_down.append(to_twin(after(piece, other_gate if 2 * c < CHUNKS else other_up)))
    _, all_grads = gather(after(cotangent, near[layers // 2]))

    terms = [
        all_rows[:, width + t * experts : width + (t + 1) * experts].astype(jnp.float32) for t in range(3)
    ]
    all_weight = terms[0] + terms[1] + terms[2]
    weight = jnp.concatenate(
        [
            lax.dynamic_slice_in_dim(all_weight, owner * local_count, local_count, axis=1)
            for owner in (me, me ^ 1)
        ],
        axis=1,
    )

    def grad_act(grads, down):
        flat = down.reshape(local_count * hidden, down.shape[2])
        return lax.dot_general(grads, flat, (((1,), (1,)), ((), ())), preferred_element_type=jnp.float32)

    activ, by_gate, by_up = hidden_forward(all_rows, gate_weight, up_weight)
    other_activ, other_by_gate, other_by_up = hidden_forward(all_rows, other_gate, other_up)
    grad = grad_act(all_grads, down_weight)
    own_grads = [(grad * by).astype(jnp.bfloat16) for by in (by_gate, by_up)]
    mixed = []
    other_grad = None
    for c in range(CHUNKS):
        keep, send = mix_columns(weight, activ, other_activ, down_weight, other_down[c], c)
        mixed.append(reduce_start(keep, send))
        term = grad_act(all_grads[:, c * columns : (c + 1) * columns], other_down[c])
        other_grad = term if other_grad is None else other_grad + term
    other_grads = [(other_grad * by).astype(jnp.bfloat16) for by in (other_by_gate, other_by_up)]
    back = []
    for c in range(CHUNKS):
        keep, send = back_columns(
            weight, own_grads, (gate_weight, up_weight), other_grads, (other_gate, other_up), c, columns
        )
        back.append(reduce_start(keep, send))
    return (reduce_end(mixed), reduce_end(back))


def route_slots(expert_ids, local_count, device_count, capacity):
    experts = local_count * device_count
    row_count = expert_ids.shape[0] * expert_ids.shape[1]
    flat_ids = expert_ids.reshape(row_count)
    sort_order = jnp.argsort(flat_ids, stable=True)
    labels = lax.broadcasted_iota(jnp.int32, (1, experts), 1)
    counts = jnp.sum((flat_ids[:, None] == labels).astype(jnp.int32), axis=0)
    starts = jnp.cumsum(counts) - counts
    sorted_ids = flat_ids[sort_order]
    rank_within = jnp.arange(row_count, dtype=jnp.int32) - starts[sorted_ids]
    owner = sorted_ids // local_count
    local_slot = sorted_ids % local_count
    target = local_slot * (device_count * capacity) + owner * capacity + rank_within
    source_of = jnp.full((experts * capacity,), row_count, jnp.int32).at[target].set(sort_order)
    target_of = jnp.zeros((row_count,), jnp.int32).at[sort_order].set(target)
    return (source_of, target_of)


def pack_rows(values, source_of, top_count, local_count):
    token_count = values.shape[0]
    with_zero = jnp.concatenate([values, jnp.zeros((1, values.shape[1]), values.dtype)], axis=0)
    token_index = jnp.minimum(source_of // top_count, token_count)
    picked = with_zero[token_index]
    return picked.reshape(local_count, -1, values.shape[1])


def forward_part(received, gate_weight, up_weight, down_weight):
    gate_pre = jnp.einsum("erd,edh->erh", received, gate_weight, preferred_element_type=jnp.float32)
    up_pre = jnp.einsum("erd,edh->erh", received, up_weight, preferred_element_type=jnp.float32)
    sigmoid_gate = jax.nn.sigmoid(gate_pre)
    activ = (gate_pre * sigmoid_gate * up_pre).astype(jnp.bfloat16)
    expert_out = jnp.einsum("erh,ehd->erd", activ, down_weight, preferred_element_type=jnp.float32)
    return (expert_out.astype(jnp.bfloat16), gate_pre, up_pre, sigmoid_gate)


def backward_part(grad_rows, gate_pre, up_pre, sigmoid_gate, gate_weight, up_weight, down_weight):
    grad_act = jnp.einsum(
        "erd,ehd->erh", grad_rows, down_weight, preferred_element_type=jnp.float32
    )
    grad_gate = (grad_act * up_pre * sigmoid_gate * (1.0 + gate_pre * (1.0 - sigmoid_gate))).astype(
        jnp.bfloat16
    )
    grad_up = (grad_act * gate_pre * sigmoid_gate).astype(jnp.bfloat16)
    joined_grad = jnp.concatenate([grad_gate, grad_up], axis=2)
    joined_weight = jnp.concatenate([gate_weight, up_weight], axis=2)
    expert_back = jnp.einsum(
        "erh,edh->erd", joined_grad, joined_weight, preferred_element_type=jnp.float32
    )
    return expert_back.astype(jnp.bfloat16)


def combine_rows(returned, target_of, probs):
    token_count, top_count = probs.shape
    flat_back = returned.reshape(-1, returned.shape[2])
    picked = flat_back[target_of].reshape(token_count, top_count, returned.shape[2])
    return jnp.sum(picked.astype(jnp.float32) * probs[:, :, None], axis=1)


def on_device_routed(tokens, cotangent, expert_ids, probs, gate_weight, up_weight, down_weight):
    local_count = gate_weight.shape[0]
    device_count = lax.axis_size("expert")
    experts = local_count * device_count
    token_count, top_count = expert_ids.shape
    row_count = token_count * top_count
    capacity = row_count * 6 // (5 * experts)
    source_of, target_of = route_slots(expert_ids, local_count, device_count, capacity)
    send_rows = pack_rows(tokens, source_of, top_count, local_count)
    send_grads = pack_rows(cotangent, source_of, top_count, local_count)
    received = lax.all_to_all(send_rows, "expert", split_axis=1, concat_axis=1, tiled=True)
    expert_out, gate_pre, up_pre, sigmoid_gate = forward_part(
        received, gate_weight, up_weight, down_weight
    )
    returned_out = lax.all_to_all(expert_out, "expert", split_axis=1, concat_axis=1, tiled=True)
    received_grads = lax.all_to_all(send_grads, "expert", split_axis=1, concat_axis=1, tiled=True)
    expert_back = backward_part(
        received_grads, gate_pre, up_pre, sigmoid_gate, gate_weight, up_weight, down_weight
    )
    returned_back = lax.all_to_all(expert_back, "expert", split_axis=1, concat_axis=1, tiled=True)
    mixed = combine_rows(returned_out, target_of, probs)
    input_grad = combine_rows(returned_back, target_of, probs)
    return (mixed, input_grad)


def on_device(tokens, cotangent, expert_ids, probs, gate_weight, up_weight, down_weight):
    devices = lax.axis_size("expert")
    dense = devices % 4 == 0 and devices <= 2 * expert_ids.shape[1]
    body = on_device_dense if dense else on_device_routed
    return body(tokens, cotangent, expert_ids, probs, gate_weight, up_weight, down_weight)


def solution(mesh):
    in_specs = (
        P(("dp", "expert"), None),
        P(("dp", "expert"), None),
        P(("dp", "expert"), None),
        P(("dp", "expert"), None),
        P(("dp", "expert"), None, None),
        P(("dp", "expert"), None, None),
        P(("dp", "expert"), None, None),
    )
    out_specs = (P(("dp", "expert"), None), P(("dp", "expert"), None))
    return jax.shard_map(
        on_device, mesh=mesh, in_specs=in_specs, out_specs=out_specs, check_vma=False
    )
```

```python
import jax
import jax.numpy as jnp
from jax import lax
from jax.experimental import pallas as pl
from jax.experimental.pallas import tpu as pltpu
from jax.sharding import PartitionSpec as P

VMEM_BYTES = 48 * 2**20


def hidden_kernel(rows_ref, gate_ref, up_ref, activ_ref, by_gate_ref, by_up_ref):
    experts, _, hidden = gate_ref.shape
    rows = rows_ref[...]
    for e in range(experts):
        cut = slice(e * hidden, (e + 1) * hidden)
        gate_pre = jnp.dot(rows, gate_ref[e], preferred_element_type=jnp.float32)
        up_pre = jnp.dot(rows, up_ref[e], preferred_element_type=jnp.float32)
        sig = jax.nn.sigmoid(gate_pre)
        silu = gate_pre * sig
        activ_ref[:, cut] = (silu * up_pre).astype(jnp.bfloat16)
        by_gate_ref[:, cut] = up_pre * sig * (1.0 + gate_pre * (1.0 - sig))
        by_up_ref[:, cut] = silu


def split_store(total, keep_ref, send_ref):
    @pl.when(pl.program_id(0) == 0)
    def _():
        send_ref[...] = total.astype(send_ref.dtype)

    @pl.when(pl.program_id(0) == 1)
    def _():
        keep_ref[...] = total


def mix_kernel(weight_ref, own_ref, other_ref, own_down_ref, other_down_ref, keep_ref, send_ref):
    experts, hidden, _ = own_down_ref.shape
    total = None
    for side, (activ_ref, down_ref) in enumerate(((own_ref, own_down_ref), (other_ref, other_down_ref))):
        for e in range(experts):
            cut = slice(e * hidden, (e + 1) * hidden)
            at = side * experts + e
            out = jnp.dot(activ_ref[:, cut], down_ref[e], preferred_element_type=jnp.float32)
            out = out.astype(jnp.bfloat16).astype(jnp.float32) * weight_ref[:, at : at + 1]
            total = out if total is None else total + out
    split_store(total, keep_ref, send_ref)


def back_kernel(weight_ref, *refs):
    keep_ref, send_ref = refs[-2:]
    experts, _, hidden = refs[2].shape
    nt = (((1,), (1,)), ((), ()))
    total = None
    for side in range(2):
        by_gate_ref, by_up_ref, gate_ref, up_ref = refs[4 * side : 4 * side + 4]
        for e in range(experts):
            cut = slice(e * hidden, (e + 1) * hidden)
            at = side * experts + e
            back = lax.dot_general(by_gate_ref[:, cut], gate_ref[e], nt, preferred_element_type=jnp.float32)
            back += lax.dot_general(by_up_ref[:, cut], up_ref[e], nt, preferred_element_type=jnp.float32)
            back = back.astype(jnp.bfloat16).astype(jnp.float32) * weight_ref[:, at : at + 1]
            total = back if total is None else total + back
    split_store(total, keep_ref, send_ref)


def hidden_forward(rows, gate_weight, up_weight):
    count = rows.shape[0]
    experts, width, hidden = gate_weight.shape
    tile = 256 if count % 256 == 0 else count
    columns = experts * hidden
    weights = pl.BlockSpec((experts, width, hidden), lambda i: (0, 0, 0))
    out = pl.BlockSpec((tile, columns), lambda i: (i, 0))
    return pl.pallas_call(
        hidden_kernel,
        grid=(count // tile,),
        in_specs=[pl.BlockSpec((tile, width), lambda i: (i, 0)), weights, weights],
        out_specs=[out, out, out],
        out_shape=[
            jax.ShapeDtypeStruct((count, columns), jnp.bfloat16),
            jax.ShapeDtypeStruct((count, columns), jnp.float32),
            jax.ShapeDtypeStruct((count, columns), jnp.float32),
        ],
        compiler_params=pltpu.CompilerParams(vmem_limit_bytes=VMEM_BYTES),
        cost_estimate=pl.CostEstimate(
            flops=4 * count * width * columns,
            bytes_accessed=2 * count * width + 10 * count * columns + 4 * gate_weight.size,
            transcendentals=count * columns,
        ),
        name="hidden_forward",
    )(rows, gate_weight, up_weight)


def halves_call(kernel, name, count, columns, flops, in_specs, operands):
    half = count // 2
    return pl.pallas_call(
        kernel,
        grid=(2,),
        in_specs=in_specs,
        out_specs=[pl.BlockSpec((half, columns), lambda i: (0, 0))] * 2,
        out_shape=[
            jax.ShapeDtypeStruct((half, columns), jnp.float32),
            jax.ShapeDtypeStruct((half, columns), jnp.bfloat16),
        ],
        compiler_params=pltpu.CompilerParams(vmem_limit_bytes=VMEM_BYTES),
        cost_estimate=pl.CostEstimate(
            flops=flops,
            bytes_accessed=sum(2 * x.size for x in operands) // 2 + 6 * half * columns,
            transcendentals=0,
        ),
        name=name,
    )(*operands)


def half_rows(array):
    return pl.BlockSpec((array.shape[0] // 2, array.shape[1]), lambda i: (1 - i, 0))


def mix_columns(weight, own, other, own_down, other_down, at):
    experts, hidden, columns = other_down.shape
    count = own.shape[0]
    specs = [
        half_rows(weight),
        half_rows(own),
        half_rows(other),
        pl.BlockSpec((experts, hidden, columns), lambda i: (0, 0, at)),
        pl.BlockSpec((experts, hidden, columns), lambda i: (0, 0, 0)),
    ]
    flops = 4 * count * experts * hidden * columns
    return halves_call(
        mix_kernel, "mix_columns", count, columns, flops, specs, (weight, own, other, own_down, other_down)
    )


def back_columns(weight, own, own_weights, other, other_weights, at, columns):
    experts, _, hidden = own_weights[0].shape
    count = weight.shape[0]
    weights = pl.BlockSpec((experts, columns, hidden), lambda i: (0, at, 0))
    specs = [half_rows(weight)]
    for grads in (own, other):
        specs += [half_rows(grads[0]), half_rows(grads[1]), weights, weights]
    flops = 8 * count * experts * hidden * columns
    return halves_call(
        back_kernel,
        "back_columns",
        count,
        columns,
        flops,
        specs,
        (weight, *own, *own_weights, *other, *other_weights),
    )


def cut_columns(width, eighths):
    eighth = width // 8
    return [(lo * eighth, hi * eighth) for lo, hi in eighths]


def join_columns(chunks, parts):
    return jnp.concatenate([part for _, part in sorted(zip(chunks, parts), key=lambda p: p[0])], axis=1)


def after(values, *others):
    return lax.optimization_barrier((values, *others))[0]


class Queue:
    def __init__(self, depth):
        self.depth = depth
        self.results = []

    def send(self, values, pairs, *others):
        waits = list(others) + self.results[: max(0, len(self.results) - self.depth + 1)]
        if waits:
            values = after(values, *waits)
        self.results.append(lax.ppermute(values, "expert", pairs))
        return self.results[-1]


def on_device_dense(tokens, cotangent, expert_ids, probs, gate_weight, up_weight, down_weight):
    local_count, hidden, width = down_weight.shape
    devices = lax.axis_size("expert")
    layers = devices // 4
    experts = local_count * devices
    block = tokens.shape[0]
    chunks = cut_columns(width, ((4, 8), (0, 3), (3, 4)))
    back_chunks = cut_columns(width, ((0, 3), (3, 6), (6, 8)))
    me = lax.axis_index("expert")
    to_twin = [(d, d ^ 1) for d in range(devices)]
    to_side = [(d, d ^ 2) for d in range(devices)]
    to_layer = [[(d, (d + 4 * k) % devices) for d in range(devices)] for k in range(layers)]
    hops = sorted(range(1, layers), key=lambda k: min(k, layers - k))
    twins, sides, across = Queue(2), Queue(2), Queue(2)

    labels = lax.broadcasted_iota(jnp.int32, (1, 1, experts), 2)
    weight = jnp.sum(jnp.where(expert_ids[:, :, None] == labels, probs[:, :, None], 0.0), axis=1)
    first = lax.reduce_precision(weight, 8, 7)
    second = lax.reduce_precision(weight - first, 8, 7)
    third = weight - first - second
    spare = jnp.zeros((block, -3 * experts % 128), jnp.bfloat16)
    terms = [t.astype(jnp.bfloat16) for t in (first, second, third)]
    rows = jnp.concatenate([tokens] + terms + [spare], axis=1)

    other_gate = twins.send(gate_weight, to_twin)
    near_rows, far_rows = {0: rows}, {}
    near_grads, far_grads = {0: cotangent}, {}
    for k in hops:
        near_rows[k] = across.send(rows, to_layer[-k])
    for k in hops:
        near_grads[k] = across.send(cotangent, to_layer[-k])
    early = [0] + hops[:-1]
    for k in early:
        far_rows[k] = sides.send(near_rows[k], to_side)
    other_up = twins.send(up_weight, to_twin, far_rows[early[-1]])
    far_grads[0] = sides.send(cotangent, to_side)
    far_rows[hops[-1]] = sides.send(near_rows[hops[-1]], to_side)
    for k in hops:
        far_grads[k] = sides.send(near_grads[k], to_side)
    all_rows = jnp.concatenate(
        [near_rows[k] for k in range(layers)] + [far_rows[k] for k in range(layers)], axis=0
    )
    all_grads = jnp.concatenate(
        [near_grads[k] for k in range(layers)] + [far_grads[k] for k in range(layers)], axis=0
    )

    terms = [
        all_rows[:, width + t * experts : width + (t + 1) * experts].astype(jnp.float32) for t in range(3)
    ]
    all_weight = terms[0] + terms[1] + terms[2]
    weight = jnp.concatenate(
        [
            lax.dynamic_slice_in_dim(all_weight, owner * local_count, local_count, axis=1)
            for owner in (me, me ^ 1)
        ],
        axis=1,
    )

    def grad_act(grads, down):
        flat = down.reshape(local_count * hidden, down.shape[2])
        return lax.dot_general(grads, flat, (((1,), (1,)), ((), ())), preferred_element_type=jnp.float32)

    def reduce(keep, send):
        total = keep + sides.send(send, to_side).astype(jnp.float32)
        parts = [total[:block]]
        for k in hops:
            piece = total[k * block : (k + 1) * block].astype(jnp.bfloat16)
            parts.append(across.send(piece, to_layer[k]))
        return sum(p.astype(jnp.float32) for p in parts)

    activ, by_gate, by_up = hidden_forward(all_rows, gate_weight, up_weight)
    other_activ, other_by_gate, other_by_up = hidden_forward(all_rows, other_gate, other_up)
    grad = grad_act(all_grads, down_weight)
    own_grads = [(grad * by).astype(jnp.bfloat16) for by in (by_gate, by_up)]
    mixed = []
    other_grad = None
    other_down = [
        twins.send(down_weight[:, :, lo:hi], to_twin, far_rows[hops[-1]]) for lo, hi in chunks[:2]
    ]
    last = other_activ
    for c, (lo, hi) in enumerate(chunks):
        down = after(other_down[c], last)
        halves = mix_columns(weight, activ, other_activ, down_weight, down, lo // (hi - lo))
        last = halves[1]
        mixed.append(reduce(*halves))
        for ahead in chunks[c + 2 : c + 3]:
            other_down.append(twins.send(down_weight[:, :, ahead[0] : ahead[1]], to_twin, last))
        term = grad_act(all_grads[:, lo:hi], down)
        other_grad = term if other_grad is None else other_grad + term
    other_grads = [(other_grad * by).astype(jnp.bfloat16) for by in (other_by_gate, other_by_up)]
    own_weights, other_weights = (gate_weight, up_weight), (other_gate, other_up)
    back = []
    for lo, hi in back_chunks:
        columns = hi - lo
        halves = back_columns(
            after(weight, last), own_grads, own_weights, other_grads, other_weights, lo // columns, columns
        )
        last = halves[1]
        back.append(reduce(*halves))
    return (join_columns(chunks, mixed), join_columns(back_chunks, back))


def route_slots(expert_ids, local_count, device_count, capacity):
    experts = local_count * device_count
    row_count = expert_ids.shape[0] * expert_ids.shape[1]
    flat_ids = expert_ids.reshape(row_count)
    sort_order = jnp.argsort(flat_ids, stable=True)
    labels = lax.broadcasted_iota(jnp.int32, (1, experts), 1)
    counts = jnp.sum((flat_ids[:, None] == labels).astype(jnp.int32), axis=0)
    starts = jnp.cumsum(counts) - counts
    sorted_ids = flat_ids[sort_order]
    rank_within = jnp.arange(row_count, dtype=jnp.int32) - starts[sorted_ids]
    owner = sorted_ids // local_count
    local_slot = sorted_ids % local_count
    target = local_slot * (device_count * capacity) + owner * capacity + rank_within
    source_of = jnp.full((experts * capacity,), row_count, jnp.int32).at[target].set(sort_order)
    target_of = jnp.zeros((row_count,), jnp.int32).at[sort_order].set(target)
    return (source_of, target_of)


def pack_rows(values, source_of, top_count, local_count):
    token_count = values.shape[0]
    with_zero = jnp.concatenate([values, jnp.zeros((1, values.shape[1]), values.dtype)], axis=0)
    token_index = jnp.minimum(source_of // top_count, token_count)
    picked = with_zero[token_index]
    return picked.reshape(local_count, -1, values.shape[1])


def forward_part(received, gate_weight, up_weight, down_weight):
    gate_pre = jnp.einsum("erd,edh->erh", received, gate_weight, preferred_element_type=jnp.float32)
    up_pre = jnp.einsum("erd,edh->erh", received, up_weight, preferred_element_type=jnp.float32)
    sigmoid_gate = jax.nn.sigmoid(gate_pre)
    activ = (gate_pre * sigmoid_gate * up_pre).astype(jnp.bfloat16)
    expert_out = jnp.einsum("erh,ehd->erd", activ, down_weight, preferred_element_type=jnp.float32)
    return (expert_out.astype(jnp.bfloat16), gate_pre, up_pre, sigmoid_gate)


def backward_part(grad_rows, gate_pre, up_pre, sigmoid_gate, gate_weight, up_weight, down_weight):
    grad_act = jnp.einsum(
        "erd,ehd->erh", grad_rows, down_weight, preferred_element_type=jnp.float32
    )
    grad_gate = (grad_act * up_pre * sigmoid_gate * (1.0 + gate_pre * (1.0 - sigmoid_gate))).astype(
        jnp.bfloat16
    )
    grad_up = (grad_act * gate_pre * sigmoid_gate).astype(jnp.bfloat16)
    joined_grad = jnp.concatenate([grad_gate, grad_up], axis=2)
    joined_weight = jnp.concatenate([gate_weight, up_weight], axis=2)
    expert_back = jnp.einsum(
        "erh,edh->erd", joined_grad, joined_weight, preferred_element_type=jnp.float32
    )
    return expert_back.astype(jnp.bfloat16)


def combine_rows(returned, target_of, probs):
    token_count, top_count = probs.shape
    flat_back = returned.reshape(-1, returned.shape[2])
    picked = flat_back[target_of].reshape(token_count, top_count, returned.shape[2])
    return jnp.sum(picked.astype(jnp.float32) * probs[:, :, None], axis=1)


def on_device_routed(tokens, cotangent, expert_ids, probs, gate_weight, up_weight, down_weight):
    local_count = gate_weight.shape[0]
    device_count = lax.axis_size("expert")
    experts = local_count * device_count
    token_count, top_count = expert_ids.shape
    row_count = token_count * top_count
    capacity = row_count * 6 // (5 * experts)
    source_of, target_of = route_slots(expert_ids, local_count, device_count, capacity)
    send_rows = pack_rows(tokens, source_of, top_count, local_count)
    send_grads = pack_rows(cotangent, source_of, top_count, local_count)
    received = lax.all_to_all(send_rows, "expert", split_axis=1, concat_axis=1, tiled=True)
    expert_out, gate_pre, up_pre, sigmoid_gate = forward_part(
        received, gate_weight, up_weight, down_weight
    )
    returned_out = lax.all_to_all(expert_out, "expert", split_axis=1, concat_axis=1, tiled=True)
    received_grads = lax.all_to_all(send_grads, "expert", split_axis=1, concat_axis=1, tiled=True)
    expert_back = backward_part(
        received_grads, gate_pre, up_pre, sigmoid_gate, gate_weight, up_weight, down_weight
    )
    returned_back = lax.all_to_all(expert_back, "expert", split_axis=1, concat_axis=1, tiled=True)
    mixed = combine_rows(returned_out, target_of, probs)
    input_grad = combine_rows(returned_back, target_of, probs)
    return (mixed, input_grad)


def on_device(tokens, cotangent, expert_ids, probs, gate_weight, up_weight, down_weight):
    devices = lax.axis_size("expert")
    dense = devices % 4 == 0 and devices <= 2 * expert_ids.shape[1]
    body = on_device_dense if dense else on_device_routed
    return body(tokens, cotangent, expert_ids, probs, gate_weight, up_weight, down_weight)


def solution(mesh):
    in_specs = (
        P(("dp", "expert"), None),
        P(("dp", "expert"), None),
        P(("dp", "expert"), None),
        P(("dp", "expert"), None),
        P(("dp", "expert"), None, None),
        P(("dp", "expert"), None, None),
        P(("dp", "expert"), None, None),
    )
    out_specs = (P(("dp", "expert"), None), P(("dp", "expert"), None))
    return jax.shard_map(
        on_device, mesh=mesh, in_specs=in_specs, out_specs=out_specs, check_vma=False
    )
```

```python
import jax
import jax.numpy as jnp
from jax import lax
from jax.experimental import pallas as pl
from jax.experimental.pallas import tpu as pltpu
from jax.sharding import PartitionSpec as P

VMEM_BYTES = 48 * 2**20
AT_ONCE = pl.CostEstimate(flops=1, bytes_accessed=1, transcendentals=0)


def hidden_kernel(rows_ref, weight_ref, gate_ref, up_ref, activ_ref, by_ref):
    experts, _, hidden = gate_ref.shape
    rows = rows_ref[...]
    for e in range(experts):
        cut = slice(e * hidden, (e + 1) * hidden)
        cut_up = slice((experts + e) * hidden, (experts + e + 1) * hidden)
        gate_pre = jnp.dot(rows, gate_ref[e], preferred_element_type=jnp.float32)
        up_pre = jnp.dot(rows, up_ref[e], preferred_element_type=jnp.float32)
        sig = jax.nn.sigmoid(gate_pre)
        factor = sig * weight_ref[:, e : e + 1]
        silu = gate_pre * factor
        activ_ref[:, cut] = (silu * up_pre).astype(jnp.bfloat16)
        by_ref[:, cut] = up_pre * factor * (1.0 + gate_pre * (1.0 - sig))
        by_ref[:, cut_up] = silu


def hidden_forward(rows, weight, gate_weight, up_weight):
    count = rows.shape[0]
    experts, width, hidden = gate_weight.shape
    tile = 256 if count % 256 == 0 else count
    columns = experts * hidden
    weights = pl.BlockSpec((experts, width, hidden), lambda i: (0, 0, 0))
    return pl.pallas_call(
        hidden_kernel,
        grid=(count // tile,),
        in_specs=[
            pl.BlockSpec((tile, width), lambda i: (i, 0)),
            pl.BlockSpec((tile, experts), lambda i: (i, 0)),
            weights,
            weights,
        ],
        out_specs=[
            pl.BlockSpec((tile, columns), lambda i: (i, 0)),
            pl.BlockSpec((tile, 2 * columns), lambda i: (i, 0)),
        ],
        out_shape=[
            jax.ShapeDtypeStruct((count, columns), jnp.bfloat16),
            jax.ShapeDtypeStruct((count, 2 * columns), jnp.float32),
        ],
        compiler_params=pltpu.CompilerParams(vmem_limit_bytes=VMEM_BYTES),
        cost_estimate=AT_ONCE,
        name="hidden_forward",
    )(rows, weight, gate_weight, up_weight)


def columns_kernel(own_ref, other_ref, own_weight_ref, other_weight_ref, keep_ref, send_ref):
    total = jnp.dot(own_ref[...], own_weight_ref[...], preferred_element_type=jnp.float32)
    total += jnp.dot(other_ref[...], other_weight_ref[...], preferred_element_type=jnp.float32)

    @pl.when(pl.program_id(0) == 0)
    def _():
        send_ref[...] = total.astype(send_ref.dtype)

    @pl.when(pl.program_id(0) == 1)
    def _():
        keep_ref[...] = total


def sum_columns(name, own, other, own_weight, other_weight, own_at, other_at, columns):
    half, depth = own.shape[0] // 2, own.shape[1]
    rows = pl.BlockSpec((half, depth), lambda i: (1 - i, 0))
    return pl.pallas_call(
        columns_kernel,
        grid=(2,),
        in_specs=[
            rows,
            rows,
            pl.BlockSpec((depth, columns), lambda i: (0, own_at)),
            pl.BlockSpec((depth, columns), lambda i: (0, other_at)),
        ],
        out_specs=[pl.BlockSpec((half, columns), lambda i: (0, 0))] * 2,
        out_shape=[
            jax.ShapeDtypeStruct((half, columns), jnp.float32),
            jax.ShapeDtypeStruct((half, columns), jnp.bfloat16),
        ],
        compiler_params=pltpu.CompilerParams(vmem_limit_bytes=VMEM_BYTES),
        cost_estimate=AT_ONCE,
        name=name,
    )(own, other, own_weight, other_weight)


def cut_columns(width, eighths):
    eighth = width // 8
    return [(lo * eighth, hi * eighth) for lo, hi in eighths]


def join_columns(chunks, parts):
    return jnp.concatenate([part for _, part in sorted(zip(chunks, parts), key=lambda p: p[0])], axis=1)


def after(values, *others):
    return lax.optimization_barrier((values, *others))[0]


def send_round(sends, waits=()):
    values, _ = lax.optimization_barrier(([v for v, _ in sends], list(waits)))
    return [lax.ppermute(v, "expert", pairs) for v, (_, pairs) in zip(values, sends)]


def on_device_dense(tokens, cotangent, expert_ids, probs, gate_weight, up_weight, down_weight):
    local_count, hidden, width = down_weight.shape
    devices = lax.axis_size("expert")
    layers = devices // 4
    experts = local_count * devices
    block = tokens.shape[0]
    chunks = cut_columns(width, ((6, 8), (0, 3), (3, 6)))
    back_chunks = cut_columns(width, ((0, 3), (3, 6), (6, 8)))
    me = lax.axis_index("expert")
    twin = [(d, d ^ 1) for d in range(devices)]
    side = [(d, d ^ 2) for d in range(devices)]
    layer = [[(d, (d + 4 * k) % devices) for d in range(devices)] for k in range(layers)]
    hops = list(range(1, layers))
    ends, middle = [hops[0], hops[-1]], hops[1:-1]

    labels = lax.broadcasted_iota(jnp.int32, (1, 1, experts), 2)
    weight = jnp.sum(jnp.where(expert_ids[:, :, None] == labels, probs[:, :, None], 0.0), axis=1)
    first = lax.reduce_precision(weight, 8, 7)
    second = lax.reduce_precision(weight - first, 8, 7)
    third = weight - first - second
    spare = jnp.zeros((block, -3 * experts % 128), jnp.bfloat16)
    terms = [t.astype(jnp.bfloat16) for t in (first, second, third)]
    rows = jnp.concatenate([tokens] + terms + [spare], axis=1)

    def turn(weights):
        return weights.transpose(0, 2, 1).reshape(local_count * hidden, width)

    near_rows, far_rows = {0: rows}, {}
    near_grads, far_grads = {0: cotangent}, {}
    down = down_weight.reshape(local_count * hidden, width)
    downs = [down[:, lo:hi] for lo, hi in chunks]
    got = send_round(
        [(gate_weight, twin), (rows, side), (cotangent, side)] + [(rows, layer[-k]) for k in ends]
    )
    other_gate, far_rows[0], far_grads[0], near_rows[ends[0]], near_rows[ends[1]] = got
    own_turned = jnp.concatenate([turn(gate_weight), turn(up_weight)], axis=0)
    got = send_round(
        [(up_weight, twin)] + [(near_rows[k], side) for k in ends] + [(rows, layer[-k]) for k in middle],
        got[1:] + [own_turned],
    )
    other_up, far_rows[ends[0]], far_rows[ends[1]] = got[:3]
    near_rows.update(zip(middle, got[3:]))
    got = send_round(
        [(downs[0], twin)] + [(cotangent, layer[-k]) for k in ends] + [(near_rows[k], side) for k in middle],
        got[1:] + [other_gate],
    )
    other_down = got[:1]
    near_grads[ends[0]], near_grads[ends[1]] = got[1:3]
    far_rows.update(zip(middle, got[3:]))
    all_rows = jnp.concatenate(
        [near_rows[k] for k in range(layers)] + [far_rows[k] for k in range(layers)], axis=0
    )
    other_turned = turn(other_gate)
    got = send_round(
        [(near_grads[k], side) for k in ends] + [(cotangent, layer[-k]) for k in middle], got[1:]
    )
    far_grads[ends[0]], far_grads[ends[1]] = got[:2]
    near_grads.update(zip(middle, got[2:]))
    terms = [
        all_rows[:, width + t * experts : width + (t + 1) * experts].astype(jnp.float32) for t in range(3)
    ]
    all_weight = terms[0] + terms[1] + terms[2]
    own_weight, other_weight = (
        lax.dynamic_slice_in_dim(all_weight, owner * local_count, local_count, axis=1)
        for owner in (me, me ^ 1)
    )
    activ, by = hidden_forward(all_rows, own_weight, gate_weight, up_weight)
    ready = got + [other_up, activ, other_turned, other_weight]
    got = send_round([(downs[1], twin)] + [(near_grads[k], side) for k in middle], ready)
    other_down += got[:1]
    far_grads.update(zip(middle, got[1:]))
    other_up = after(other_up, *ready)
    all_grads = jnp.concatenate(
        [near_grads[k] for k in range(layers)] + [far_grads[k] for k in range(layers)], axis=0
    )

    def grad_act(grads, down):
        return lax.dot_general(grads, down, (((1,), (1,)), ((), ())), preferred_element_type=jnp.float32)

    def spread(grad, by):
        return (jnp.concatenate([grad, grad], axis=1) * by).astype(jnp.bfloat16)

    def mix(c):
        lo, hi = chunks[c]
        return sum_columns(
            "mix_columns", activ, other_activ, down, other_down[c], lo // (hi - lo), 0, hi - lo
        )

    def back(c):
        lo, hi = back_chunks[c]
        at = lo // (hi - lo)
        return sum_columns(
            "back_columns", own_grads, other_grads, own_turned, other_turned, at, at, hi - lo
        )

    def across(total):
        return [
            (total[k * block : (k + 1) * block].astype(jnp.bfloat16), layer[k]) for k in hops
        ]

    def finish(total, parts):
        return total[:block] + sum(p.astype(jnp.float32) for p in parts)

    other_activ, other_by = hidden_forward(all_rows, other_weight, other_gate, other_up)
    other_down[0] = after(other_down[0], other_activ)
    keep, send = mix(0)
    got = send_round([(downs[2], twin), (send, side)], [all_grads])
    other_down += got[:1]
    own_grads = spread(grad_act(all_grads, down), by)
    other_turned = jnp.concatenate([other_turned, turn(other_up)], axis=0)
    totals, parts = [keep + got[1].astype(jnp.float32)], []

    other_down[1] = after(other_down[1], send)
    keep, send = mix(1)
    got = send_round([(send, side)] + across(totals[0]), [own_grads, other_turned])
    totals.append(keep + got[0].astype(jnp.float32))
    parts.append(got[1:])

    other_down[2] = after(other_down[2], send)
    keep, send = mix(2)
    got = send_round([(send, side)] + across(totals[1]), got)
    totals.append(keep + got[0].astype(jnp.float32))
    parts.append(got[1:])
    other_grad = sum(grad_act(all_grads[:, lo:hi], down) for (lo, hi), down in zip(chunks, other_down))
    other_grads = spread(other_grad, other_by)

    for c in range(len(back_chunks)):
        keep, send = back(c)
        got = send_round([(send, side)] + across(totals[-1]), got)
        totals.append(keep + got[0].astype(jnp.float32))
        parts.append(got[1:])
    parts.append(send_round(across(totals[-1]), got))
    sums = [finish(total, part) for total, part in zip(totals, parts)]
    count = len(chunks)
    return (join_columns(chunks, sums[:count]), join_columns(back_chunks, sums[count:]))


def route_slots(expert_ids, local_count, device_count, capacity):
    experts = local_count * device_count
    row_count = expert_ids.shape[0] * expert_ids.shape[1]
    flat_ids = expert_ids.reshape(row_count)
    sort_order = jnp.argsort(flat_ids, stable=True)
    labels = lax.broadcasted_iota(jnp.int32, (1, experts), 1)
    counts = jnp.sum((flat_ids[:, None] == labels).astype(jnp.int32), axis=0)
    starts = jnp.cumsum(counts) - counts
    sorted_ids = flat_ids[sort_order]
    rank_within = jnp.arange(row_count, dtype=jnp.int32) - starts[sorted_ids]
    owner = sorted_ids // local_count
    local_slot = sorted_ids % local_count
    target = local_slot * (device_count * capacity) + owner * capacity + rank_within
    source_of = jnp.full((experts * capacity,), row_count, jnp.int32).at[target].set(sort_order)
    target_of = jnp.zeros((row_count,), jnp.int32).at[sort_order].set(target)
    return (source_of, target_of)


def pack_rows(values, source_of, top_count, local_count):
    token_count = values.shape[0]
    with_zero = jnp.concatenate([values, jnp.zeros((1, values.shape[1]), values.dtype)], axis=0)
    token_index = jnp.minimum(source_of // top_count, token_count)
    picked = with_zero[token_index]
    return picked.reshape(local_count, -1, values.shape[1])


def forward_part(received, gate_weight, up_weight, down_weight):
    gate_pre = jnp.einsum("erd,edh->erh", received, gate_weight, preferred_element_type=jnp.float32)
    up_pre = jnp.einsum("erd,edh->erh", received, up_weight, preferred_element_type=jnp.float32)
    sigmoid_gate = jax.nn.sigmoid(gate_pre)
    activ = (gate_pre * sigmoid_gate * up_pre).astype(jnp.bfloat16)
    expert_out = jnp.einsum("erh,ehd->erd", activ, down_weight, preferred_element_type=jnp.float32)
    return (expert_out.astype(jnp.bfloat16), gate_pre, up_pre, sigmoid_gate)


def backward_part(grad_rows, gate_pre, up_pre, sigmoid_gate, gate_weight, up_weight, down_weight):
    grad_act = jnp.einsum(
        "erd,ehd->erh", grad_rows, down_weight, preferred_element_type=jnp.float32
    )
    grad_gate = (grad_act * up_pre * sigmoid_gate * (1.0 + gate_pre * (1.0 - sigmoid_gate))).astype(
        jnp.bfloat16
    )
    grad_up = (grad_act * gate_pre * sigmoid_gate).astype(jnp.bfloat16)
    joined_grad = jnp.concatenate([grad_gate, grad_up], axis=2)
    joined_weight = jnp.concatenate([gate_weight, up_weight], axis=2)
    expert_back = jnp.einsum(
        "erh,edh->erd", joined_grad, joined_weight, preferred_element_type=jnp.float32
    )
    return expert_back.astype(jnp.bfloat16)


def combine_rows(returned, target_of, probs):
    token_count, top_count = probs.shape
    flat_back = returned.reshape(-1, returned.shape[2])
    picked = flat_back[target_of].reshape(token_count, top_count, returned.shape[2])
    return jnp.sum(picked.astype(jnp.float32) * probs[:, :, None], axis=1)


def on_device_routed(tokens, cotangent, expert_ids, probs, gate_weight, up_weight, down_weight):
    local_count = gate_weight.shape[0]
    device_count = lax.axis_size("expert")
    experts = local_count * device_count
    token_count, top_count = expert_ids.shape
    row_count = token_count * top_count
    capacity = row_count * 6 // (5 * experts)
    source_of, target_of = route_slots(expert_ids, local_count, device_count, capacity)
    send_rows = pack_rows(tokens, source_of, top_count, local_count)
    send_grads = pack_rows(cotangent, source_of, top_count, local_count)
    received = lax.all_to_all(send_rows, "expert", split_axis=1, concat_axis=1, tiled=True)
    expert_out, gate_pre, up_pre, sigmoid_gate = forward_part(
        received, gate_weight, up_weight, down_weight
    )
    returned_out = lax.all_to_all(expert_out, "expert", split_axis=1, concat_axis=1, tiled=True)
    received_grads = lax.all_to_all(send_grads, "expert", split_axis=1, concat_axis=1, tiled=True)
    expert_back = backward_part(
        received_grads, gate_pre, up_pre, sigmoid_gate, gate_weight, up_weight, down_weight
    )
    returned_back = lax.all_to_all(expert_back, "expert", split_axis=1, concat_axis=1, tiled=True)
    mixed = combine_rows(returned_out, target_of, probs)
    input_grad = combine_rows(returned_back, target_of, probs)
    return (mixed, input_grad)


def on_device(tokens, cotangent, expert_ids, probs, gate_weight, up_weight, down_weight):
    devices = lax.axis_size("expert")
    dense = devices % 4 == 0 and 16 <= devices <= 2 * expert_ids.shape[1]
    body = on_device_dense if dense else on_device_routed
    return body(tokens, cotangent, expert_ids, probs, gate_weight, up_weight, down_weight)


def solution(mesh):
    in_specs = (
        P(("dp", "expert"), None),
        P(("dp", "expert"), None),
        P(("dp", "expert"), None),
        P(("dp", "expert"), None),
        P(("dp", "expert"), None, None),
        P(("dp", "expert"), None, None),
        P(("dp", "expert"), None, None),
    )
    out_specs = (P(("dp", "expert"), None), P(("dp", "expert"), None))
    return jax.shard_map(
        on_device, mesh=mesh, in_specs=in_specs, out_specs=out_specs, check_vma=False
    )
```

```python
import functools

import jax
import jax.numpy as jnp
from jax import lax
from jax.experimental import pallas as pl
from jax.experimental.pallas import tpu as pltpu
from jax.sharding import PartitionSpec as P

VMEM_BYTES = 32 * 2**20
AT_ONCE = pl.CostEstimate(flops=1, bytes_accessed=1, transcendentals=0)


def compiler_params():
    return pltpu.CompilerParams(vmem_limit_bytes=VMEM_BYTES)


def fetch_rows(block_refs, buffer, sems):
    step = pl.program_id(0)
    count = len(block_refs) // pl.num_programs(0)

    @pl.when(step == 0)
    def _():
        for j, ref in enumerate(block_refs):
            pltpu.make_async_copy(ref, buffer.at[j], sems.at[j]).start()

    for j in range(len(block_refs)):

        @pl.when(step == j // count)
        def _(j=j):
            pltpu.make_async_copy(block_refs[j], buffer.at[j], sems.at[j]).wait()

    rows = buffer[pl.ds(step * count, count)]
    return rows.reshape(count * rows.shape[1], rows.shape[2])


def hidden_kernel(blocks, all_experts, owner_ref, gate_ref, up_ref, *refs):
    activ_ref, by_ref, buffer, sems = refs[blocks:]
    experts, width, hidden = gate_ref.shape
    rows = fetch_rows(refs[:blocks], buffer, sems)
    terms = rows[:, width:].astype(jnp.float32)
    rows = rows[:, :width]
    lanes = lax.broadcasted_iota(jnp.int32, terms.shape, 1)
    for e in range(experts):
        cut = slice(e * hidden, (e + 1) * hidden)
        cut_up = slice((experts + e) * hidden, (experts + e + 1) * hidden)
        label = owner_ref[0] * experts + e
        named = (lanes == label) | (lanes == label + all_experts) | (lanes == label + 2 * all_experts)
        weight = jnp.sum(jnp.where(named, terms, 0.0), axis=1, keepdims=True)
        gate_pre = jnp.dot(rows, gate_ref[e], preferred_element_type=jnp.float32)
        up_pre = jnp.dot(rows, up_ref[e], preferred_element_type=jnp.float32)
        sig = jax.nn.sigmoid(gate_pre)
        factor = sig * weight
        silu = gate_pre * factor
        activ_ref[:, cut] = (silu * up_pre).astype(jnp.bfloat16)
        by_ref[:, cut] = up_pre * factor * (1.0 + gate_pre * (1.0 - sig))
        by_ref[:, cut_up] = silu


def hidden_forward(row_blocks, owner, gate_weight, up_weight, all_experts):
    blocks = len(row_blocks)
    block, row_width = row_blocks[0].shape
    experts, width, hidden = gate_weight.shape
    count, columns, tile = blocks * block, experts * hidden, 2 * block
    weights = pl.BlockSpec((experts, width, hidden), lambda i: (0, 0, 0))
    return pl.pallas_call(
        functools.partial(hidden_kernel, blocks, all_experts),
        grid=(blocks // 2,),
        in_specs=[pl.BlockSpec(memory_space=pltpu.SMEM), weights, weights]
        + [pl.BlockSpec(memory_space=pl.ANY)] * blocks,
        out_specs=[
            pl.BlockSpec((tile, columns), lambda i: (i, 0)),
            pl.BlockSpec((tile, 2 * columns), lambda i: (i, 0)),
        ],
        out_shape=[
            jax.ShapeDtypeStruct((count, columns), jnp.bfloat16),
            jax.ShapeDtypeStruct((count, 2 * columns), jnp.float32),
        ],
        scratch_shapes=[
            pltpu.VMEM((blocks, block, row_width), jnp.bfloat16),
            pltpu.SemaphoreType.DMA((blocks,)),
        ],
        compiler_params=compiler_params(),
        cost_estimate=AT_ONCE,
        name="hidden_forward",
    )(owner.reshape(1), gate_weight, up_weight, *row_blocks)


NT = (((1,), (1,)), ((), ()))


def grads_kernel(blocks, chunks, by_ref, *refs):
    down_refs, block_refs = refs[: len(chunks)], refs[len(chunks) : len(chunks) + blocks]
    out_ref, buffer, sems = refs[len(chunks) + blocks :]
    rows = fetch_rows(block_refs, buffer, sems)
    total = None
    for (lo, hi), down_ref in zip(chunks, down_refs):
        term = lax.dot_general(rows[:, lo:hi], down_ref[...], NT, preferred_element_type=jnp.float32)
        total = term if total is None else total + term
    columns = total.shape[1]
    out_ref[:, :columns] = (total * by_ref[:, :columns]).astype(jnp.bfloat16)
    out_ref[:, columns:] = (total * by_ref[:, columns:]).astype(jnp.bfloat16)


def hidden_grads(grad_blocks, by, downs, chunks):
    blocks = len(grad_blocks)
    block, width = grad_blocks[0].shape
    tile = 2 * block
    rows = pl.BlockSpec((tile, by.shape[1]), lambda i: (i, 0))
    return pl.pallas_call(
        functools.partial(grads_kernel, blocks, tuple(chunks)),
        grid=(blocks // 2,),
        in_specs=[rows]
        + [pl.BlockSpec(d.shape, lambda i: (0, 0)) for d in downs]
        + [pl.BlockSpec(memory_space=pl.ANY)] * blocks,
        out_specs=rows,
        out_shape=jax.ShapeDtypeStruct(by.shape, jnp.bfloat16),
        scratch_shapes=[
            pltpu.VMEM((blocks, block, width), jnp.bfloat16),
            pltpu.SemaphoreType.DMA((blocks,)),
        ],
        compiler_params=compiler_params(),
        cost_estimate=AT_ONCE,
        name="hidden_grads",
    )(by, *downs, *grad_blocks)


def store_half(total, keep_ref, send_ref):
    @pl.when(pl.program_id(0) == 0)
    def _():
        send_ref[...] = total.astype(send_ref.dtype)

    @pl.when(pl.program_id(0) == 1)
    def _():
        keep_ref[...] = total


def mix_kernel(own_ref, other_ref, own_down_ref, other_down_ref, keep_ref, send_ref):
    total = jnp.dot(own_ref[...], own_down_ref[...], preferred_element_type=jnp.float32)
    total += jnp.dot(other_ref[...], other_down_ref[...], preferred_element_type=jnp.float32)
    store_half(total, keep_ref, send_ref)


def back_kernel(own_ref, other_ref, *refs):
    weight_refs, (keep_ref, send_ref) = refs[:-2], refs[-2:]
    experts, _, hidden = weight_refs[0].shape
    total = None
    for at, weight_ref in enumerate(weight_refs):
        grads_ref = (own_ref, other_ref)[at // 2]
        for e in range(experts):
            first = (at % 2 * experts + e) * hidden
            term = lax.dot_general(
                grads_ref[:, first : first + hidden], weight_ref[e], NT, preferred_element_type=jnp.float32
            )
            total = term if total is None else total + term
    store_half(total, keep_ref, send_ref)


def sum_columns(kernel, name, columns, own, other, weights, weight_specs):
    half, depth = own.shape[0] // 2, own.shape[1]
    rows = pl.BlockSpec((half, depth), lambda i: (1 - i, 0))
    return pl.pallas_call(
        kernel,
        grid=(2,),
        in_specs=[rows, rows] + weight_specs,
        out_specs=[pl.BlockSpec((half, columns), lambda i: (0, 0))] * 2,
        out_shape=[
            jax.ShapeDtypeStruct((half, columns), jnp.float32),
            jax.ShapeDtypeStruct((half, columns), jnp.bfloat16),
        ],
        compiler_params=compiler_params(),
        cost_estimate=AT_ONCE,
        name=name,
    )(own, other, *weights)


def mix_columns(own, other, own_down, other_down, at):
    depth, columns = other_down.shape
    specs = [
        pl.BlockSpec((depth, columns), lambda i: (0, at)),
        pl.BlockSpec((depth, columns), lambda i: (0, 0)),
    ]
    return sum_columns(mix_kernel, "mix_columns", columns, own, other, [own_down, other_down], specs)


def back_columns(own, other, weights, at, columns):
    experts, _, hidden = weights[0].shape
    specs = [pl.BlockSpec((experts, columns, hidden), lambda i: (0, at, 0))] * len(weights)
    return sum_columns(back_kernel, "back_columns", columns, own, other, weights, specs)


def add_kernel(keep_ref, come_ref, own_ref, *piece_refs):
    block = own_ref.shape[0]
    own_ref[...] = keep_ref[:block, :] + come_ref[:block, :].astype(jnp.float32)
    for k, piece_ref in enumerate(piece_refs, 1):
        cut = slice(k * block, (k + 1) * block)
        total = keep_ref[cut, :] + come_ref[cut, :].astype(jnp.float32)
        piece_ref[...] = total.astype(piece_ref.dtype)


def add_sides(keep, come, layers):
    block, columns = keep.shape[0] // layers, keep.shape[1]
    pieces = [jax.ShapeDtypeStruct((block, columns), jnp.bfloat16)] * (layers - 1)
    return pl.pallas_call(
        add_kernel,
        out_shape=[jax.ShapeDtypeStruct((block, columns), jnp.float32)] + pieces,
        compiler_params=compiler_params(),
        cost_estimate=AT_ONCE,
        name="add_sides",
    )(keep, come)


def finish_kernel(chunks, layers, *refs):
    out_ref = refs[-1]
    for c, (lo, hi) in enumerate(chunks):
        own_ref, *piece_refs = refs[c * layers : (c + 1) * layers]
        total = own_ref[...]
        for piece_ref in piece_refs:
            total += piece_ref[...].astype(jnp.float32)
        out_ref[:, lo:hi] = total


def finish(chunks, parts, width):
    return pl.pallas_call(
        functools.partial(finish_kernel, tuple(chunks), len(parts[0])),
        out_shape=jax.ShapeDtypeStruct((parts[0][0].shape[0], width), jnp.float32),
        compiler_params=compiler_params(),
        cost_estimate=AT_ONCE,
        name="finish",
    )(*[p for part in parts for p in part])


def cut_columns(width, eighths):
    eighth = width // 8
    return [(lo * eighth, hi * eighth) for lo, hi in eighths]


def after(values, *others):
    return lax.optimization_barrier((values, *others))[0]


def send_all(sends, *waits):
    values, _ = lax.optimization_barrier(([v for v, _ in sends], waits))
    return [lax.ppermute(v, "expert", pairs) for v, (_, pairs) in zip(values, sends)]


def on_device_dense(tokens, cotangent, expert_ids, probs, gate_weight, up_weight, down_weight):
    local_count, hidden, width = down_weight.shape
    devices = lax.axis_size("expert")
    layers = devices // 4
    experts = local_count * devices
    block = tokens.shape[0]
    chunks = cut_columns(width, ((6, 8), (0, 3), (3, 6)))
    back_chunks = cut_columns(width, ((0, 3), (3, 6), (6, 8)))
    me = lax.axis_index("expert")
    twin = [(d, d ^ 1) for d in range(devices)]
    side = [(d, d ^ 2) for d in range(devices)]
    layer = [[(d, (d + 4 * k) % devices) for d in range(devices)] for k in range(layers)]

    labels = lax.broadcasted_iota(jnp.int32, (1, 1, experts), 2)
    weight = jnp.sum(jnp.where(expert_ids[:, :, None] == labels, probs[:, :, None], 0.0), axis=1)
    first = lax.reduce_precision(weight, 8, 7)
    second = lax.reduce_precision(weight - first, 8, 7)
    third = weight - first - second
    spare = jnp.zeros((block, -3 * experts % 128), jnp.bfloat16)
    terms = [t.astype(jnp.bfloat16) for t in (first, second, third)]
    row = jnp.concatenate([tokens] + terms + [spare], axis=1)
    grad = cotangent
    down = down_weight.reshape(local_count * hidden, width)
    downs = [down[:, lo:hi] for lo, hi in chunks]

    one, last, *middle = [1, layers - 1, *range(2, layers - 1)]
    rows, far_rows, grads, far_grads = {0: row}, {}, {0: grad}, {}
    other_gate, rows[one], far_rows[0] = send_all([(gate_weight, twin), (row, layer[-one]), (row, side)])
    rows[last], far_grads[0] = send_all([(row, layer[-last]), (grad, side)])
    got = send_all([(rows[one], side)] + [(row, layer[-k]) for k in middle], far_rows[0])
    far_rows[one] = got[0]
    rows.update(zip(middle, got[1:]))
    other_up, far_rows[last] = send_all([(up_weight, twin), (rows[last], side)], far_grads[0])
    got = send_all(
        [(grad, layer[-one])] + [(rows[k], side) for k in middle], far_rows[one]
    )
    grads[one] = got[0]
    far_rows.update(zip(middle, got[1:]))
    down_0, grads[last] = send_all([(downs[0], twin), (grad, layer[-last])], far_rows[last], other_gate)
    got = send_all(
        [(grads[one], side)] + [(grad, layer[-k]) for k in middle], *far_rows.values()
    )
    far_grads[one] = got[0]
    grads.update(zip(middle, got[1:]))
    row_blocks = [rows[k] for k in range(layers)] + [far_rows[k] for k in range(layers)]
    activ, by = hidden_forward(row_blocks, me, gate_weight, up_weight, experts)
    (far_grads[last],) = send_all([(grads[last], side)], activ)
    waits = [other_up, far_grads[one]]
    got = send_all([(downs[1], twin)] + [(grads[k], side) for k in middle], *waits)
    down_1 = got[0]
    far_grads.update(zip(middle, got[1:]))

    other_up = after(other_up, *waits)
    other_activ, other_by = hidden_forward(row_blocks, me ^ 1, other_gate, other_up, experts)

    def mix(c, other_down, *waits):
        lo, hi = chunks[c]
        return mix_columns(activ, other_activ, down, after(other_down, *waits), lo // (hi - lo))

    def across(pieces):
        return [(piece, layer[k]) for k, piece in enumerate(pieces, 1)]

    keep_0, send = mix(0, down_0, other_activ)
    come_0, down_2 = send_all([(send, side), (downs[2], twin)], far_grads[last])
    grad_blocks = [grads[k] for k in range(layers)] + [far_grads[k] for k in range(layers)]
    own_grads = hidden_grads(grad_blocks, by, [down], [(0, width)])

    keep_1, send = mix(1, down_1, send)
    own_0, *pieces = add_sides(keep_0, come_0, layers)
    come_1, *parts_0 = send_all([(send, side)] + across(pieces), own_grads)

    keep_2, send = mix(2, down_2, send)
    own_1, *pieces = add_sides(keep_1, come_1, layers)
    come_2, *parts_1 = send_all([(send, side)] + across(pieces), *parts_0)

    other_grads = hidden_grads(grad_blocks, other_by, [down_0, down_1, down_2], chunks)
    weights = [gate_weight, up_weight, other_gate, other_up]

    def back(c):
        lo, hi = back_chunks[c]
        return back_columns(own_grads, other_grads, weights, lo // (hi - lo), hi - lo)

    keep_3, send = back(0)
    (come_3,) = send_all([(send, side)])

    keep_4, send = back(1)
    own_2, *pieces = add_sides(keep_2, come_2, layers)
    come_4, *parts_2 = send_all([(send, side)] + across(pieces), *parts_1)

    keep_5, send = back(2)
    own_3, *pieces = add_sides(keep_3, come_3, layers)
    come_5, *parts_3 = send_all([(send, side)] + across(pieces), *parts_2)

    own_4, *pieces = add_sides(keep_4, come_4, layers)
    parts_4 = send_all(across(pieces), *parts_3)

    own_5, *pieces = add_sides(keep_5, after(come_5, own_4), layers)
    parts_5 = send_all(across(pieces))

    mixed = finish(chunks, [(own_0, *parts_0), (own_1, *parts_1), (own_2, *parts_2)], width)
    back_sum = finish(back_chunks, [(own_3, *parts_3), (own_4, *parts_4), (own_5, *parts_5)], width)
    return (mixed, back_sum)


def route_slots(expert_ids, local_count, device_count, capacity):
    experts = local_count * device_count
    row_count = expert_ids.shape[0] * expert_ids.shape[1]
    flat_ids = expert_ids.reshape(row_count)
    sort_order = jnp.argsort(flat_ids, stable=True)
    labels = lax.broadcasted_iota(jnp.int32, (1, experts), 1)
    counts = jnp.sum((flat_ids[:, None] == labels).astype(jnp.int32), axis=0)
    starts = jnp.cumsum(counts) - counts
    sorted_ids = flat_ids[sort_order]
    rank_within = jnp.arange(row_count, dtype=jnp.int32) - starts[sorted_ids]
    owner = sorted_ids // local_count
    local_slot = sorted_ids % local_count
    target = local_slot * (device_count * capacity) + owner * capacity + rank_within
    source_of = jnp.full((experts * capacity,), row_count, jnp.int32).at[target].set(sort_order)
    target_of = jnp.zeros((row_count,), jnp.int32).at[sort_order].set(target)
    return (source_of, target_of)


def pack_rows(values, source_of, top_count, local_count):
    token_count = values.shape[0]
    with_zero = jnp.concatenate([values, jnp.zeros((1, values.shape[1]), values.dtype)], axis=0)
    token_index = jnp.minimum(source_of // top_count, token_count)
    picked = with_zero[token_index]
    return picked.reshape(local_count, -1, values.shape[1])


def forward_part(received, gate_weight, up_weight, down_weight):
    gate_pre = jnp.einsum("erd,edh->erh", received, gate_weight, preferred_element_type=jnp.float32)
    up_pre = jnp.einsum("erd,edh->erh", received, up_weight, preferred_element_type=jnp.float32)
    sigmoid_gate = jax.nn.sigmoid(gate_pre)
    activ = (gate_pre * sigmoid_gate * up_pre).astype(jnp.bfloat16)
    expert_out = jnp.einsum("erh,ehd->erd", activ, down_weight, preferred_element_type=jnp.float32)
    return (expert_out.astype(jnp.bfloat16), gate_pre, up_pre, sigmoid_gate)


def backward_part(grad_rows, gate_pre, up_pre, sigmoid_gate, gate_weight, up_weight, down_weight):
    grad_act = jnp.einsum(
        "erd,ehd->erh", grad_rows, down_weight, preferred_element_type=jnp.float32
    )
    grad_gate = (grad_act * up_pre * sigmoid_gate * (1.0 + gate_pre * (1.0 - sigmoid_gate))).astype(
        jnp.bfloat16
    )
    grad_up = (grad_act * gate_pre * sigmoid_gate).astype(jnp.bfloat16)
    joined_grad = jnp.concatenate([grad_gate, grad_up], axis=2)
    joined_weight = jnp.concatenate([gate_weight, up_weight], axis=2)
    expert_back = jnp.einsum(
        "erh,edh->erd", joined_grad, joined_weight, preferred_element_type=jnp.float32
    )
    return expert_back.astype(jnp.bfloat16)


def combine_rows(returned, target_of, probs):
    token_count, top_count = probs.shape
    flat_back = returned.reshape(-1, returned.shape[2])
    picked = flat_back[target_of].reshape(token_count, top_count, returned.shape[2])
    return jnp.sum(picked.astype(jnp.float32) * probs[:, :, None], axis=1)


def on_device_routed(tokens, cotangent, expert_ids, probs, gate_weight, up_weight, down_weight):
    local_count = gate_weight.shape[0]
    device_count = lax.axis_size("expert")
    experts = local_count * device_count
    token_count, top_count = expert_ids.shape
    row_count = token_count * top_count
    capacity = row_count * 6 // (5 * experts)
    source_of, target_of = route_slots(expert_ids, local_count, device_count, capacity)
    send_rows = pack_rows(tokens, source_of, top_count, local_count)
    send_grads = pack_rows(cotangent, source_of, top_count, local_count)
    received = lax.all_to_all(send_rows, "expert", split_axis=1, concat_axis=1, tiled=True)
    expert_out, gate_pre, up_pre, sigmoid_gate = forward_part(
        received, gate_weight, up_weight, down_weight
    )
    returned_out = lax.all_to_all(expert_out, "expert", split_axis=1, concat_axis=1, tiled=True)
    received_grads = lax.all_to_all(send_grads, "expert", split_axis=1, concat_axis=1, tiled=True)
    expert_back = backward_part(
        received_grads, gate_pre, up_pre, sigmoid_gate, gate_weight, up_weight, down_weight
    )
    returned_back = lax.all_to_all(expert_back, "expert", split_axis=1, concat_axis=1, tiled=True)
    mixed = combine_rows(returned_out, target_of, probs)
    input_grad = combine_rows(returned_back, target_of, probs)
    return (mixed, input_grad)


def on_device(tokens, cotangent, expert_ids, probs, gate_weight, up_weight, down_weight):
    devices = lax.axis_size("expert")
    dense = devices % 4 == 0 and 16 <= devices <= 2 * expert_ids.shape[1]
    body = on_device_dense if dense else on_device_routed
    return body(tokens, cotangent, expert_ids, probs, gate_weight, up_weight, down_weight)


def solution(mesh):
    in_specs = (
        P(("dp", "expert"), None),
        P(("dp", "expert"), None),
        P(("dp", "expert"), None),
        P(("dp", "expert"), None),
        P(("dp", "expert"), None, None),
        P(("dp", "expert"), None, None),
        P(("dp", "expert"), None, None),
    )
    out_specs = (P(("dp", "expert"), None), P(("dp", "expert"), None))
    return jax.shard_map(
        on_device, mesh=mesh, in_specs=in_specs, out_specs=out_specs, check_vma=False
    )
```

```python
import functools

import jax
import jax.numpy as jnp
from jax import lax
from jax.experimental import pallas as pl
from jax.experimental.pallas import tpu as pltpu
from jax.sharding import PartitionSpec as P

VMEM_BYTES = 18 * 2**20
AT_ONCE = pl.CostEstimate(flops=1, bytes_accessed=1, transcendentals=0)


def resident(shape, index):
    return pl.BlockSpec(shape, index, pipeline_mode=pl.Buffered(1))


def compiler_params():
    return pltpu.CompilerParams(vmem_limit_bytes=VMEM_BYTES)


def fetch_rows(block_refs, buffer, sems):
    step = pl.program_id(0)
    count = len(block_refs) // pl.num_programs(0)

    @pl.when(step == 0)
    def _():
        for j, ref in enumerate(block_refs):
            pltpu.make_async_copy(ref, buffer.at[j], sems.at[j]).start()

    for j in range(len(block_refs)):

        @pl.when(step == j // count)
        def _(j=j):
            pltpu.make_async_copy(block_refs[j], buffer.at[j], sems.at[j]).wait()

    rows = buffer[pl.ds(step * count, count)]
    return rows.reshape(count * rows.shape[1], rows.shape[2])


def hidden_kernel(blocks, all_experts, owner_ref, gate_ref, up_ref, *refs):
    activ_ref, by_ref, buffer, sems = refs[blocks:]
    experts, width, hidden = gate_ref.shape
    rows = fetch_rows(refs[:blocks], buffer, sems)
    terms = rows[:, width:].astype(jnp.float32)
    rows = rows[:, :width]
    lanes = lax.broadcasted_iota(jnp.int32, terms.shape, 1)
    for e in range(experts):
        cut = slice(e * hidden, (e + 1) * hidden)
        cut_up = slice((experts + e) * hidden, (experts + e + 1) * hidden)
        label = owner_ref[0] * experts + e
        named = (lanes == label) | (lanes == label + all_experts) | (lanes == label + 2 * all_experts)
        weight = jnp.sum(jnp.where(named, terms, 0.0), axis=1, keepdims=True)
        gate_pre = jnp.dot(rows, gate_ref[e], preferred_element_type=jnp.float32)
        up_pre = jnp.dot(rows, up_ref[e], preferred_element_type=jnp.float32)
        sig = jax.nn.sigmoid(gate_pre)
        factor = sig * weight
        silu = gate_pre * factor
        activ_ref[:, cut] = (silu * up_pre).astype(jnp.bfloat16)
        by_ref[:, cut] = up_pre * factor * (1.0 + gate_pre * (1.0 - sig))
        by_ref[:, cut_up] = silu


def hidden_forward(row_blocks, owner, gate_weight, up_weight, all_experts):
    blocks = len(row_blocks)
    block, row_width = row_blocks[0].shape
    experts, width, hidden = gate_weight.shape
    count, columns, tile = blocks * block, experts * hidden, 2 * block
    weights = resident((experts, width, hidden), lambda i: (0, 0, 0))
    return pl.pallas_call(
        functools.partial(hidden_kernel, blocks, all_experts),
        grid=(blocks // 2,),
        in_specs=[pl.BlockSpec(memory_space=pltpu.SMEM), weights, weights]
        + [pl.BlockSpec(memory_space=pl.ANY)] * blocks,
        out_specs=[
            pl.BlockSpec((tile, columns), lambda i: (i, 0)),
            pl.BlockSpec((tile, 2 * columns), lambda i: (i, 0)),
        ],
        out_shape=[
            jax.ShapeDtypeStruct((count, columns), jnp.bfloat16),
            jax.ShapeDtypeStruct((count, 2 * columns), jnp.float32),
        ],
        scratch_shapes=[
            pltpu.VMEM((blocks, block, row_width), jnp.bfloat16),
            pltpu.SemaphoreType.DMA((blocks,)),
        ],
        compiler_params=compiler_params(),
        cost_estimate=AT_ONCE,
        name="hidden_forward",
    )(owner.reshape(1), gate_weight, up_weight, *row_blocks)


NT = (((1,), (1,)), ((), ()))


def grads_kernel(blocks, cuts, has_by, has_before, *refs):
    refs = list(refs)
    by_ref = refs.pop(0) if has_by else None
    before_ref = refs.pop(0) if has_before else None
    down_refs, block_refs = refs[: len(cuts)], refs[len(cuts) : len(cuts) + blocks]
    out_ref, buffer, sems = refs[len(cuts) + blocks :]
    rows = fetch_rows(block_refs, buffer, sems)
    total = before_ref[...] if has_before else None
    for (lo, hi), down_ref in zip(cuts, down_refs):
        term = lax.dot_general(rows[:, lo:hi], down_ref[...], NT, preferred_element_type=jnp.float32)
        total = term if total is None else total + term
    if has_by:
        columns = total.shape[1]
        out_ref[:, :columns] = (total * by_ref[:, :columns]).astype(jnp.bfloat16)
        out_ref[:, columns:] = (total * by_ref[:, columns:]).astype(jnp.bfloat16)
    else:
        out_ref[...] = total


def hidden_grads(grad_blocks, downs, cuts, by=None, before=None):
    blocks = len(grad_blocks)
    block, width = grad_blocks[0].shape
    columns = downs[0].shape[0]
    tile = 2 * block

    def rows(count):
        return pl.BlockSpec((tile, count), lambda i: (i, 0))

    given = [x for x in (by, before) if x is not None]
    out_columns, out_type = (columns, jnp.float32) if by is None else (2 * columns, jnp.bfloat16)
    return pl.pallas_call(
        functools.partial(grads_kernel, blocks, tuple(cuts), by is not None, before is not None),
        grid=(blocks // 2,),
        in_specs=[rows(x.shape[1]) for x in given]
        + [resident(d.shape, lambda i: (0, 0)) for d in downs]
        + [pl.BlockSpec(memory_space=pl.ANY)] * blocks,
        out_specs=rows(out_columns),
        out_shape=jax.ShapeDtypeStruct((blocks * block, out_columns), out_type),
        scratch_shapes=[
            pltpu.VMEM((blocks, block, width), jnp.bfloat16),
            pltpu.SemaphoreType.DMA((blocks,)),
        ],
        compiler_params=compiler_params(),
        cost_estimate=AT_ONCE,
        name="hidden_grads",
    )(*given, *downs, *grad_blocks)


def store_half(total, keep_ref, send_ref):
    @pl.when(pl.program_id(0) == 0)
    def _():
        send_ref[...] = total.astype(send_ref.dtype)

    @pl.when(pl.program_id(0) == 1)
    def _():
        keep_ref[...] = total


def mix_kernel(own_ref, other_ref, own_down_ref, other_down_ref, keep_ref, send_ref):
    total = jnp.dot(own_ref[...], own_down_ref[...], preferred_element_type=jnp.float32)
    total += jnp.dot(other_ref[...], other_down_ref[...], preferred_element_type=jnp.float32)
    store_half(total, keep_ref, send_ref)


def back_kernel(own_ref, other_ref, *refs):
    weight_refs, (keep_ref, send_ref) = refs[:-2], refs[-2:]
    experts, _, hidden = weight_refs[0].shape
    total = None
    for at, weight_ref in enumerate(weight_refs):
        grads_ref = (own_ref, other_ref)[at // 2]
        for e in range(experts):
            first = (at % 2 * experts + e) * hidden
            term = lax.dot_general(
                grads_ref[:, first : first + hidden], weight_ref[e], NT, preferred_element_type=jnp.float32
            )
            total = term if total is None else total + term
    store_half(total, keep_ref, send_ref)


def sum_columns(kernel, name, columns, own, other, weights, weight_specs):
    half, depth = own.shape[0] // 2, own.shape[1]
    rows = pl.BlockSpec((half, depth), lambda i: (1 - i, 0))
    return pl.pallas_call(
        kernel,
        grid=(2,),
        in_specs=[rows, rows] + weight_specs,
        out_specs=[pl.BlockSpec((half, columns), lambda i: (0, 0))] * 2,
        out_shape=[
            jax.ShapeDtypeStruct((half, columns), jnp.float32),
            jax.ShapeDtypeStruct((half, columns), jnp.bfloat16),
        ],
        compiler_params=compiler_params(),
        cost_estimate=AT_ONCE,
        name=name,
    )(own, other, *weights)


def mix_columns(own, other, own_down, other_down, at):
    depth, columns = other_down.shape
    specs = [
        resident((depth, columns), lambda i: (0, at)),
        resident((depth, columns), lambda i: (0, 0)),
    ]
    return sum_columns(mix_kernel, "mix_columns", columns, own, other, [own_down, other_down], specs)


def back_columns(own, other, weights, at, columns):
    experts, _, hidden = weights[0].shape
    specs = [resident((experts, columns, hidden), lambda i: (0, at, 0))] * len(weights)
    return sum_columns(back_kernel, "back_columns", columns, own, other, weights, specs)


def add_kernel(keep_ref, come_ref, *out_refs):
    block = out_refs[0].shape[0]
    for k, out_ref in enumerate(out_refs):
        cut = slice(k * block, (k + 1) * block)
        total = keep_ref[cut, :] + come_ref[cut, :].astype(jnp.float32)
        out_ref[...] = total.astype(out_ref.dtype)


def add_sides(keep, come, types):
    block, columns = keep.shape[0] // len(types), keep.shape[1]
    return pl.pallas_call(
        add_kernel,
        out_shape=[jax.ShapeDtypeStruct((block, columns), t) for t in types],
        compiler_params=compiler_params(),
        cost_estimate=AT_ONCE,
        name="add_sides",
    )(keep, come)


def add_piece(piece, come):
    return pl.pallas_call(
        add_kernel,
        out_shape=jax.ShapeDtypeStruct(piece.shape, jnp.bfloat16),
        compiler_params=compiler_params(),
        cost_estimate=AT_ONCE,
        name="add_piece",
    )(piece, come)


def finish_kernel(chunks, layers, *refs):
    out_ref = refs[-1]
    for c, (lo, hi) in enumerate(chunks):
        own_ref, *piece_refs = refs[c * layers : (c + 1) * layers]
        total = own_ref[...]
        for piece_ref in piece_refs:
            total += piece_ref[...].astype(jnp.float32)
        out_ref[:, lo:hi] = total


def finish(chunks, parts, width):
    return pl.pallas_call(
        functools.partial(finish_kernel, tuple(chunks), len(parts[0])),
        out_shape=jax.ShapeDtypeStruct((parts[0][0].shape[0], width), jnp.float32),
        compiler_params=compiler_params(),
        cost_estimate=AT_ONCE,
        name="finish",
    )(*[p for part in parts for p in part])


def cut_columns(width, eighths):
    eighth = width // 8
    return [(lo * eighth, hi * eighth) for lo, hi in eighths]


def after(values, *others):
    return lax.optimization_barrier((values, *others))[0]


def send_all(sends, *waits):
    values, _ = lax.optimization_barrier(([v for v, _ in sends], waits))
    return [lax.ppermute(v, "expert", pairs) for v, (_, pairs) in zip(values, sends)]


def on_device_dense(tokens, cotangent, expert_ids, probs, gate_weight, up_weight, down_weight):
    local_count, hidden, width = down_weight.shape
    devices = lax.axis_size("expert")
    layers = devices // 4
    experts = local_count * devices
    block = tokens.shape[0]
    chunks = cut_columns(width, ((6, 8), (0, 3), (3, 6)))
    back_chunks = cut_columns(width, ((0, 3), (3, 6), (6, 8)))
    me = lax.axis_index("expert")
    twin = [(d, d ^ 1) for d in range(devices)]
    side = [(d, d ^ 2) for d in range(devices)]
    layer = [[(d, (d + 4 * k) % devices) for d in range(devices)] for k in range(layers)]

    labels = lax.broadcasted_iota(jnp.int32, (1, 1, experts), 2)
    weight = jnp.sum(jnp.where(expert_ids[:, :, None] == labels, probs[:, :, None], 0.0), axis=1)
    first = lax.reduce_precision(weight, 8, 7)
    second = lax.reduce_precision(weight - first, 8, 7)
    third = weight - first - second
    spare = jnp.zeros((block, -3 * experts % 128), jnp.bfloat16)
    terms = [t.astype(jnp.bfloat16) for t in (first, second, third)]
    row = jnp.concatenate([tokens] + terms + [spare], axis=1)
    grad = cotangent
    down = down_weight.reshape(local_count * hidden, width)
    downs = [down[:, lo:hi] for lo, hi in chunks]

    one, last, *middle = [1, layers - 1, *range(2, layers - 1)]
    rows, far_rows, grads, far_grads = {0: row}, {}, {0: grad}, {}
    other_gate, rows[one], far_rows[0] = send_all([(gate_weight, twin), (row, layer[-one]), (row, side)])
    rows[last], far_grads[0] = send_all([(row, layer[-last]), (grad, side)])
    (far_rows[one],) = send_all([(rows[one], side)], far_rows[0])
    for k in middle:
        (rows[k],) = send_all([(rows[k - 1], layer[-one])], far_rows[0])
    other_up, far_rows[last] = send_all([(up_weight, twin), (rows[last], side)], far_grads[0])
    got = send_all([(grad, layer[-one])] + [(rows[k], side) for k in middle], far_rows[one])
    grads[one] = got[0]
    far_rows.update(zip(middle, got[1:]))
    down_0, grads[last] = send_all([(downs[0], twin), (grad, layer[-last])], far_rows[last], other_gate)
    (far_grads[one],) = send_all([(grads[one], side)], *far_rows.values())
    for k in middle:
        (grads[k],) = send_all([(grads[k - 1], layer[-one])], *far_rows.values())
    (far_grads[last],) = send_all([(grads[last], side)], *far_rows.values())
    for k in middle:
        (far_grads[k],) = send_all([(grads[k], side)], far_grads[one])
    row_blocks = [rows[k] for k in range(layers)] + [far_rows[k] for k in range(layers)]
    own = after(me, far_grads[one])
    activ, by = hidden_forward(row_blocks, own, gate_weight, up_weight, experts)
    other_up = after(other_up, activ)
    other_activ, other_by = hidden_forward(row_blocks, me ^ 1, other_gate, other_up, experts)

    (down_1,) = send_all([(downs[1], twin)], down_0, activ, other_activ, *far_grads.values())

    def mix(c, other_down, *waits):
        lo, hi = chunks[c]
        return mix_columns(activ, other_activ, down, after(other_down, *waits), lo // (hi - lo))

    types = [jnp.float32, jnp.float32] + [jnp.bfloat16] * (layers - 2)

    def send_on(pieces, *waits):
        (far,) = send_all([(pieces[-1], layer[last])], *waits)
        come = None
        for k in reversed(middle):
            piece = pieces[k - 1] if come is None else add_piece(pieces[k - 1], come)
            (come,) = send_all([(piece, layer[one])], *waits)
        return far, come

    def send_last(pieces, come, far):
        piece = pieces[0].astype(jnp.bfloat16) if come is None else add_piece(pieces[0], come)
        return send_all([(piece, layer[one])], far)[0]

    keep_0, send = mix(0, down_0, other_activ)
    come_0, down_2 = send_all([(send, side), (downs[2], twin)], far_grads[last])
    grad_blocks = [grads[k] for k in range(layers)] + [far_grads[k] for k in range(layers)]
    own_grads = hidden_grads(grad_blocks, [down], [(0, width)], by=by)

    keep_1, send = mix(1, down_1, send)
    own_0, *pieces = add_sides(keep_0, come_0, types)
    (come_1,) = send_all([(send, side)], own_0, own_grads)
    far_0, next_0 = send_on(pieces)
    near_0 = send_last(pieces, next_0, far_0)
    other_grad = hidden_grads(grad_blocks, [down_0, down_1], chunks[:2])

    keep_2, send = mix(2, down_2, send, other_grad, near_0)
    own_1, *pieces = add_sides(keep_1, come_1, types)
    (come_2,) = send_all([(send, side)], own_1)
    far_1, next_1 = send_on(pieces, near_0)

    other_by = after(other_by, next_1)
    other_grads = hidden_grads(grad_blocks, [down_2], chunks[2:], by=other_by, before=other_grad)
    weights = [gate_weight, up_weight, other_gate, other_up]

    def back(c):
        lo, hi = back_chunks[c]
        return back_columns(own_grads, other_grads, weights, lo // (hi - lo), hi - lo)

    near_1 = send_last(pieces, next_1, far_1)
    keep_3, send = back(0)
    (come_3,) = send_all([(send, side)])

    keep_4, send = back(1)
    own_2, *pieces = add_sides(keep_2, come_2, types)
    (come_4,) = send_all([(send, side)], own_2)
    far_2, next_2 = send_on(pieces, near_1)
    near_2 = send_last(pieces, next_2, far_2)

    keep_5, send = back(2)
    own_3, *pieces = add_sides(keep_3, come_3, types)
    (come_5,) = send_all([(send, side)], own_3)
    far_3, next_3 = send_on(pieces, near_2)
    near_3 = send_last(pieces, next_3, far_3)

    mixed = finish(chunks, [(own_0, far_0, near_0), (own_1, far_1, near_1), (own_2, far_2, near_2)], width)
    own_4, *pieces = add_sides(keep_4, after(come_4, mixed), types)
    far_4, next_4 = send_on(pieces, near_3)
    near_4 = send_last(pieces, next_4, far_4)

    own_5, *pieces = add_sides(keep_5, after(come_5, own_4), types)
    far_5, next_5 = send_on(pieces, near_4)
    near_5 = send_last(pieces, next_5, far_5)
    back_parts = [(own_3, far_3, near_3), (own_4, far_4, near_4), (own_5, far_5, near_5)]
    return (mixed, finish(back_chunks, back_parts, width))


def route_slots(expert_ids, local_count, device_count, capacity):
    experts = local_count * device_count
    row_count = expert_ids.shape[0] * expert_ids.shape[1]
    flat_ids = expert_ids.reshape(row_count)
    sort_order = jnp.argsort(flat_ids, stable=True)
    labels = lax.broadcasted_iota(jnp.int32, (1, experts), 1)
    counts = jnp.sum((flat_ids[:, None] == labels).astype(jnp.int32), axis=0)
    starts = jnp.cumsum(counts) - counts
    sorted_ids = flat_ids[sort_order]
    rank_within = jnp.arange(row_count, dtype=jnp.int32) - starts[sorted_ids]
    owner = sorted_ids // local_count
    local_slot = sorted_ids % local_count
    target = local_slot * (device_count * capacity) + owner * capacity + rank_within
    source_of = jnp.full((experts * capacity,), row_count, jnp.int32).at[target].set(sort_order)
    target_of = jnp.zeros((row_count,), jnp.int32).at[sort_order].set(target)
    return (source_of, target_of)


def pack_rows(values, source_of, top_count, local_count):
    token_count = values.shape[0]
    with_zero = jnp.concatenate([values, jnp.zeros((1, values.shape[1]), values.dtype)], axis=0)
    token_index = jnp.minimum(source_of // top_count, token_count)
    picked = with_zero[token_index]
    return picked.reshape(local_count, -1, values.shape[1])


def forward_part(received, gate_weight, up_weight, down_weight):
    gate_pre = jnp.einsum("erd,edh->erh", received, gate_weight, preferred_element_type=jnp.float32)
    up_pre = jnp.einsum("erd,edh->erh", received, up_weight, preferred_element_type=jnp.float32)
    sigmoid_gate = jax.nn.sigmoid(gate_pre)
    activ = (gate_pre * sigmoid_gate * up_pre).astype(jnp.bfloat16)
    expert_out = jnp.einsum("erh,ehd->erd", activ, down_weight, preferred_element_type=jnp.float32)
    return (expert_out.astype(jnp.bfloat16), gate_pre, up_pre, sigmoid_gate)


def backward_part(grad_rows, gate_pre, up_pre, sigmoid_gate, gate_weight, up_weight, down_weight):
    grad_act = jnp.einsum(
        "erd,ehd->erh", grad_rows, down_weight, preferred_element_type=jnp.float32
    )
    grad_gate = (grad_act * up_pre * sigmoid_gate * (1.0 + gate_pre * (1.0 - sigmoid_gate))).astype(
        jnp.bfloat16
    )
    grad_up = (grad_act * gate_pre * sigmoid_gate).astype(jnp.bfloat16)
    joined_grad = jnp.concatenate([grad_gate, grad_up], axis=2)
    joined_weight = jnp.concatenate([gate_weight, up_weight], axis=2)
    expert_back = jnp.einsum(
        "erh,edh->erd", joined_grad, joined_weight, preferred_element_type=jnp.float32
    )
    return expert_back.astype(jnp.bfloat16)


def combine_rows(returned, target_of, probs):
    token_count, top_count = probs.shape
    flat_back = returned.reshape(-1, returned.shape[2])
    picked = flat_back[target_of].reshape(token_count, top_count, returned.shape[2])
    return jnp.sum(picked.astype(jnp.float32) * probs[:, :, None], axis=1)


def on_device_routed(tokens, cotangent, expert_ids, probs, gate_weight, up_weight, down_weight):
    local_count = gate_weight.shape[0]
    device_count = lax.axis_size("expert")
    experts = local_count * device_count
    token_count, top_count = expert_ids.shape
    row_count = token_count * top_count
    capacity = row_count * 6 // (5 * experts)
    source_of, target_of = route_slots(expert_ids, local_count, device_count, capacity)
    send_rows = pack_rows(tokens, source_of, top_count, local_count)
    send_grads = pack_rows(cotangent, source_of, top_count, local_count)
    received = lax.all_to_all(send_rows, "expert", split_axis=1, concat_axis=1, tiled=True)
    expert_out, gate_pre, up_pre, sigmoid_gate = forward_part(
        received, gate_weight, up_weight, down_weight
    )
    returned_out = lax.all_to_all(expert_out, "expert", split_axis=1, concat_axis=1, tiled=True)
    received_grads = lax.all_to_all(send_grads, "expert", split_axis=1, concat_axis=1, tiled=True)
    expert_back = backward_part(
        received_grads, gate_pre, up_pre, sigmoid_gate, gate_weight, up_weight, down_weight
    )
    returned_back = lax.all_to_all(expert_back, "expert", split_axis=1, concat_axis=1, tiled=True)
    mixed = combine_rows(returned_out, target_of, probs)
    input_grad = combine_rows(returned_back, target_of, probs)
    return (mixed, input_grad)


def on_device(tokens, cotangent, expert_ids, probs, gate_weight, up_weight, down_weight):
    devices = lax.axis_size("expert")
    dense = devices % 4 == 0 and 12 <= devices <= 2 * expert_ids.shape[1]
    body = on_device_dense if dense else on_device_routed
    return body(tokens, cotangent, expert_ids, probs, gate_weight, up_weight, down_weight)


def solution(mesh):
    in_specs = (
        P(("dp", "expert"), None),
        P(("dp", "expert"), None),
        P(("dp", "expert"), None),
        P(("dp", "expert"), None),
        P(("dp", "expert"), None, None),
        P(("dp", "expert"), None, None),
        P(("dp", "expert"), None, None),
    )
    out_specs = (P(("dp", "expert"), None), P(("dp", "expert"), None))
    return jax.shard_map(
        on_device, mesh=mesh, in_specs=in_specs, out_specs=out_specs, check_vma=False
    )
```

```python
import functools

import jax
import jax.numpy as jnp
from jax import lax
from jax.experimental import pallas as pl
from jax.experimental.pallas import tpu as pltpu
from jax.sharding import PartitionSpec as P

VMEM_BYTES = 18 * 2**20
VMEM_BYTES_FETCH = 56 * 2**20
AT_ONCE = pl.CostEstimate(flops=1, bytes_accessed=1, transcendentals=0)


def resident(shape, index):
    return pl.BlockSpec(shape, index, pipeline_mode=pl.Buffered(1))


def compiler_params(vmem_bytes=VMEM_BYTES):
    return pltpu.CompilerParams(vmem_limit_bytes=vmem_bytes)


def fetch_rows(block_refs, buffer, sems):
    step = pl.program_id(0)
    count = len(block_refs) // pl.num_programs(0)

    @pl.when(step == 0)
    def _():
        for j, ref in enumerate(block_refs):
            pltpu.make_async_copy(ref, buffer.at[j], sems.at[j]).start()

    for j in range(len(block_refs)):

        @pl.when(step == j // count)
        def _(j=j):
            pltpu.make_async_copy(block_refs[j], buffer.at[j], sems.at[j]).wait()

    rows = buffer[pl.ds(step * count, count)]
    return rows.reshape(count * rows.shape[1], rows.shape[2])


def hidden_kernel(blocks, all_experts, owner_ref, gate_ref, up_ref, *refs):
    activ_ref, by_ref, buffer, sems = refs[blocks:]
    experts, width, hidden = gate_ref.shape
    rows = fetch_rows(refs[:blocks], buffer, sems)
    terms = rows[:, width:].astype(jnp.float32)
    rows = rows[:, :width]
    lanes = lax.broadcasted_iota(jnp.int32, terms.shape, 1)
    for e in range(experts):
        cut = slice(e * hidden, (e + 1) * hidden)
        cut_up = slice((experts + e) * hidden, (experts + e + 1) * hidden)
        label = owner_ref[0] * experts + e
        named = (lanes == label) | (lanes == label + all_experts) | (lanes == label + 2 * all_experts)
        weight = jnp.sum(jnp.where(named, terms, 0.0), axis=1, keepdims=True)
        gate_pre = jnp.dot(rows, gate_ref[e], preferred_element_type=jnp.float32)
        up_pre = jnp.dot(rows, up_ref[e], preferred_element_type=jnp.float32)
        sig = jax.nn.sigmoid(gate_pre)
        factor = sig * weight
        silu = gate_pre * factor
        activ_ref[:, cut] = (silu * up_pre).astype(jnp.bfloat16)
        by_ref[:, cut] = up_pre * factor * (1.0 + gate_pre * (1.0 - sig))
        by_ref[:, cut_up] = silu


def hidden_forward(row_blocks, owner, gate_weight, up_weight, all_experts):
    blocks = len(row_blocks)
    block, row_width = row_blocks[0].shape
    experts, width, hidden = gate_weight.shape
    count, columns, tile = blocks * block, experts * hidden, 2 * block
    weights = resident((experts, width, hidden), lambda i: (0, 0, 0))
    return pl.pallas_call(
        functools.partial(hidden_kernel, blocks, all_experts),
        grid=(blocks // 2,),
        in_specs=[pl.BlockSpec(memory_space=pltpu.SMEM), weights, weights]
        + [pl.BlockSpec(memory_space=pl.ANY)] * blocks,
        out_specs=[
            pl.BlockSpec((tile, columns), lambda i: (i, 0)),
            pl.BlockSpec((tile, 2 * columns), lambda i: (i, 0)),
        ],
        out_shape=[
            jax.ShapeDtypeStruct((count, columns), jnp.bfloat16),
            jax.ShapeDtypeStruct((count, 2 * columns), jnp.float32),
        ],
        scratch_shapes=[
            pltpu.VMEM((blocks, block, row_width), jnp.bfloat16),
            pltpu.SemaphoreType.DMA((blocks,)),
        ],
        compiler_params=compiler_params(VMEM_BYTES_FETCH),
        cost_estimate=AT_ONCE,
        name="hidden_forward",
    )(owner.reshape(1), gate_weight, up_weight, *row_blocks)


NT = (((1,), (1,)), ((), ()))


def grads_kernel(blocks, cuts, has_by, has_before, *refs):
    refs = list(refs)
    by_ref = refs.pop(0) if has_by else None
    before_ref = refs.pop(0) if has_before else None
    down_refs, block_refs = refs[: len(cuts)], refs[len(cuts) : len(cuts) + blocks]
    out_ref, buffer, sems = refs[len(cuts) + blocks :]
    rows = fetch_rows(block_refs, buffer, sems)
    total = before_ref[...] if has_before else None
    for (lo, hi), down_ref in zip(cuts, down_refs):
        term = lax.dot_general(rows[:, lo:hi], down_ref[...], NT, preferred_element_type=jnp.float32)
        total = term if total is None else total + term
    if has_by:
        columns = total.shape[1]
        out_ref[:, :columns] = (total * by_ref[:, :columns]).astype(jnp.bfloat16)
        out_ref[:, columns:] = (total * by_ref[:, columns:]).astype(jnp.bfloat16)
    else:
        out_ref[...] = total


def hidden_grads(grad_blocks, downs, cuts, by=None, before=None):
    blocks = len(grad_blocks)
    block, width = grad_blocks[0].shape
    columns = downs[0].shape[0]
    tile = 2 * block

    def rows(count):
        return pl.BlockSpec((tile, count), lambda i: (i, 0))

    given = [x for x in (by, before) if x is not None]
    out_columns, out_type = (columns, jnp.float32) if by is None else (2 * columns, jnp.bfloat16)
    return pl.pallas_call(
        functools.partial(grads_kernel, blocks, tuple(cuts), by is not None, before is not None),
        grid=(blocks // 2,),
        in_specs=[rows(x.shape[1]) for x in given]
        + [resident(d.shape, lambda i: (0, 0)) for d in downs]
        + [pl.BlockSpec(memory_space=pl.ANY)] * blocks,
        out_specs=rows(out_columns),
        out_shape=jax.ShapeDtypeStruct((blocks * block, out_columns), out_type),
        scratch_shapes=[
            pltpu.VMEM((blocks, block, width), jnp.bfloat16),
            pltpu.SemaphoreType.DMA((blocks,)),
        ],
        compiler_params=compiler_params(),
        cost_estimate=AT_ONCE,
        name="hidden_grads",
    )(*given, *downs, *grad_blocks)


def store_half(total, keep_ref, send_ref):
    @pl.when(pl.program_id(0) == 0)
    def _():
        send_ref[...] = total.astype(send_ref.dtype)

    @pl.when(pl.program_id(0) == 1)
    def _():
        keep_ref[...] = total


def mix_kernel(own_ref, other_ref, own_down_ref, other_down_ref, keep_ref, send_ref):
    total = jnp.dot(own_ref[...], own_down_ref[...], preferred_element_type=jnp.float32)
    total += jnp.dot(other_ref[...], other_down_ref[...], preferred_element_type=jnp.float32)
    store_half(total, keep_ref, send_ref)


def back_kernel(own_ref, other_ref, *refs):
    weight_refs, (keep_ref, send_ref) = refs[:-2], refs[-2:]
    experts, _, hidden = weight_refs[0].shape
    total = None
    for at, weight_ref in enumerate(weight_refs):
        grads_ref = (own_ref, other_ref)[at // 2]
        for e in range(experts):
            first = (at % 2 * experts + e) * hidden
            term = lax.dot_general(
                grads_ref[:, first : first + hidden], weight_ref[e], NT, preferred_element_type=jnp.float32
            )
            total = term if total is None else total + term
    store_half(total, keep_ref, send_ref)


def sum_columns(kernel, name, columns, own, other, weights, weight_specs):
    half, depth = own.shape[0] // 2, own.shape[1]
    rows = pl.BlockSpec((half, depth), lambda i: (1 - i, 0))
    return pl.pallas_call(
        kernel,
        grid=(2,),
        in_specs=[rows, rows] + weight_specs,
        out_specs=[pl.BlockSpec((half, columns), lambda i: (0, 0))] * 2,
        out_shape=[
            jax.ShapeDtypeStruct((half, columns), jnp.float32),
            jax.ShapeDtypeStruct((half, columns), jnp.bfloat16),
        ],
        compiler_params=compiler_params(),
        cost_estimate=AT_ONCE,
        name=name,
    )(own, other, *weights)


def mix_columns(own, other, own_down, other_down, at):
    depth, columns = other_down.shape
    specs = [
        resident((depth, columns), lambda i: (0, at)),
        resident((depth, columns), lambda i: (0, 0)),
    ]
    return sum_columns(mix_kernel, "mix_columns", columns, own, other, [own_down, other_down], specs)


def back_columns(own, other, weights, at, columns):
    experts, _, hidden = weights[0].shape
    specs = [resident((experts, columns, hidden), lambda i: (0, at, 0))] * len(weights)
    return sum_columns(back_kernel, "back_columns", columns, own, other, weights, specs)


def add_kernel(keep_ref, come_ref, *out_refs):
    block = out_refs[0].shape[0]
    for k, out_ref in enumerate(out_refs):
        cut = slice(k * block, (k + 1) * block)
        total = keep_ref[cut, :] + come_ref[cut, :].astype(jnp.float32)
        out_ref[...] = total.astype(out_ref.dtype)


def add_sides(keep, come, types):
    block, columns = keep.shape[0] // len(types), keep.shape[1]
    return pl.pallas_call(
        add_kernel,
        out_shape=[jax.ShapeDtypeStruct((block, columns), t) for t in types],
        compiler_params=compiler_params(),
        cost_estimate=AT_ONCE,
        name="add_sides",
    )(keep, come)


def add_piece(piece, come):
    return pl.pallas_call(
        add_kernel,
        out_shape=jax.ShapeDtypeStruct(piece.shape, jnp.bfloat16),
        compiler_params=compiler_params(),
        cost_estimate=AT_ONCE,
        name="add_piece",
    )(piece, come)


def finish_kernel(chunks, counts, *refs):
    out_ref = refs[-1]
    refs = list(refs[:-1])
    for (lo, hi), count in zip(chunks, counts):
        own_ref, *piece_refs = refs[:count]
        del refs[:count]
        total = own_ref[...]
        for piece_ref in piece_refs:
            total += piece_ref[...].astype(jnp.float32)
        out_ref[:, lo:hi] = total


def finish(chunks, parts, width):
    return pl.pallas_call(
        functools.partial(finish_kernel, tuple(chunks), tuple(map(len, parts))),
        out_shape=jax.ShapeDtypeStruct((parts[0][0].shape[0], width), jnp.float32),
        compiler_params=compiler_params(),
        cost_estimate=AT_ONCE,
        name="finish",
    )(*[p for part in parts for p in part])


def cut_columns(width, eighths):
    eighth = width // 8
    return [(lo * eighth, hi * eighth) for lo, hi in eighths]


def after(values, *others):
    return lax.optimization_barrier((values, *others))[0]


def send_all(sends, *waits):
    values, _ = lax.optimization_barrier(([v for v, _ in sends], waits))
    return [lax.ppermute(v, "expert", pairs) for v, (_, pairs) in zip(values, sends)]


def on_device_dense(tokens, cotangent, expert_ids, probs, gate_weight, up_weight, down_weight):
    local_count, hidden, width = down_weight.shape
    devices = lax.axis_size("expert")
    layers = devices // 4
    experts = local_count * devices
    block = tokens.shape[0]
    chunks = cut_columns(width, ((0, 3), (3, 6), (6, 8)))
    back_chunks = cut_columns(width, ((4, 8), (0, 3), (3, 4)))
    me = lax.axis_index("expert")
    twin = [(d, d ^ 1) for d in range(devices)]
    side = [(d, d ^ 2) for d in range(devices)]
    layer = [[(d, (d + 4 * k) % devices) for d in range(devices)] for k in range(layers)]

    labels = lax.broadcasted_iota(jnp.int32, (1, 1, experts), 2)
    weight = jnp.sum(jnp.where(expert_ids[:, :, None] == labels, probs[:, :, None], 0.0), axis=1)
    first = lax.reduce_precision(weight, 8, 7)
    second = lax.reduce_precision(weight - first, 8, 7)
    third = weight - first - second
    spare = jnp.zeros((block, -3 * experts % 128), jnp.bfloat16)
    terms = [t.astype(jnp.bfloat16) for t in (first, second, third)]
    row = jnp.concatenate([tokens] + terms + [spare], axis=1)
    grad = cotangent
    down = down_weight.reshape(local_count * hidden, width)
    downs = [down[:, lo:hi] for lo, hi in chunks]

    one, last, *middle = [1, layers - 1, *range(2, layers - 1)]
    rows, far_rows, grads, far_grads = {0: row}, {}, {0: grad}, {}
    other_gate, rows[one], far_rows[0] = send_all([(gate_weight, twin), (row, layer[-one]), (row, side)])
    rows[last], far_grads[0] = send_all([(row, layer[-last]), (grad, side)])
    (far_rows[one],) = send_all([(rows[one], side)], far_rows[0])
    for k in middle:
        (rows[k],) = send_all([(rows[k - 1], layer[-one])], far_rows[0])
    other_up, far_rows[last] = send_all([(up_weight, twin), (rows[last], side)], far_grads[0])
    got = send_all([(grad, layer[-one])] + [(rows[k], side) for k in middle], far_rows[one])
    grads[one] = got[0]
    far_rows.update(zip(middle, got[1:]))
    down_0, grads[last] = send_all([(downs[0], twin), (grad, layer[-last])], far_rows[last], other_gate)
    (far_grads[one],) = send_all([(grads[one], side)], *far_rows.values())
    for k in middle:
        (grads[k],) = send_all([(grads[k - 1], layer[-one])], *far_rows.values())
    (far_grads[last],) = send_all([(grads[last], side)], *far_rows.values())
    row_blocks = [rows[k] for k in range(layers)] + [far_rows[k] for k in range(layers)]
    activ, by = hidden_forward(row_blocks, me, gate_weight, up_weight, experts)
    for k in middle:
        (far_grads[k],) = send_all([(grads[k], side)], far_grads[one], activ)
    other_up = after(other_up, activ)
    other_activ, other_by = hidden_forward(row_blocks, me ^ 1, other_gate, other_up, experts)

    (down_1,) = send_all([(downs[1], twin)], down_0, activ, other_activ)

    def mix(c, other_down, *waits):
        lo, hi = chunks[c]
        return mix_columns(activ, other_activ, down, after(other_down, *waits), lo // (hi - lo))

    types = [jnp.float32, jnp.float32] + [jnp.bfloat16] * (layers - 2)

    def send_on(pieces, *waits):
        (far,) = send_all([(pieces[-1], layer[last])], *waits)
        come = None
        for k in reversed(middle):
            piece = pieces[k - 1] if come is None else add_piece(pieces[k - 1], come)
            (come,) = send_all([(piece, layer[one])], *waits)
        return far, come

    def send_last(pieces, come, far):
        piece = pieces[0].astype(jnp.bfloat16) if come is None else add_piece(pieces[0], come)
        return send_all([(piece, layer[one])], far)[0]

    keep_0, send = mix(0, down_0, other_activ, *far_grads.values())
    come_0, down_2 = send_all([(send, side), (downs[2], twin)], far_grads[last])
    grad_blocks = [grads[k] for k in range(layers)] + [far_grads[k] for k in range(layers)]
    own_grads = hidden_grads(grad_blocks, [down], [(0, width)], by=by)

    keep_1, send = mix(1, down_1, send)
    own_0, *pieces = add_sides(keep_0, come_0, types)
    (come_1,) = send_all([(send, side)], own_0, own_grads)
    far_0, next_0 = send_on(pieces)
    near_0 = send_last(pieces, next_0, far_0)
    other_grad = hidden_grads(grad_blocks, [down_0, down_1], chunks[:2])

    keep_2, send = mix(2, down_2, send, other_grad, near_0)
    own_1, *pieces = add_sides(keep_1, come_1, types)
    (come_2,) = send_all([(send, side)], own_1)
    far_1, next_1 = send_on(pieces)

    other_by = after(other_by, next_1, far_1)
    other_grads = hidden_grads(grad_blocks, [down_2], chunks[2:], by=other_by, before=other_grad)
    weights = [gate_weight, up_weight, other_gate, other_up]

    def back(c, *waits):
        lo, hi = back_chunks[c]
        return back_columns(own_grads, after(other_grads, *waits), weights, lo // (hi - lo), hi - lo)

    near_1 = send_last(pieces, next_1, far_1)
    keep_3, send = back(0)
    (come_3,) = send_all([(send, side)])

    keep_4, send = back(1, near_1)
    own_2, *pieces = add_sides(keep_2, come_2, types)
    (come_4,) = send_all([(send, side)], own_2)
    far_2, next_2 = send_on(pieces, far_1)
    near_2 = send_last(pieces, next_2, far_2)

    keep_5, send = back(2, near_2)
    own_3, *pieces = add_sides(keep_3, come_3, types)
    (come_5,) = send_all([(send, side)], own_3)
    far_3, next_3 = send_on(pieces, near_1)
    near_3 = send_last(pieces, next_3, far_3)

    mixed = finish(chunks, [(own_0, far_0, near_0), (own_1, far_1, near_1), (own_2, far_2, near_2)], width)
    own_4, *pieces = add_sides(keep_4, after(come_4, mixed), types)
    far_4, next_4 = send_on(pieces, near_2)
    near_4 = send_last(pieces, next_4, far_4)

    types = [jnp.float32] + [jnp.bfloat16] * (layers - 1)
    own_5, *pieces = add_sides(keep_5, after(come_5, own_4), types)
    parts_5 = send_all([(piece, layer[k]) for k, piece in enumerate(pieces, 1)], near_3)
    back_parts = [(own_3, far_3, near_3), (own_4, far_4, near_4), (own_5, *parts_5)]
    return (mixed, finish(back_chunks, back_parts, width))


def route_slots(expert_ids, local_count, device_count, capacity):
    experts = local_count * device_count
    row_count = expert_ids.shape[0] * expert_ids.shape[1]
    flat_ids = expert_ids.reshape(row_count)
    sort_order = jnp.argsort(flat_ids, stable=True)
    labels = lax.broadcasted_iota(jnp.int32, (1, experts), 1)
    counts = jnp.sum((flat_ids[:, None] == labels).astype(jnp.int32), axis=0)
    starts = jnp.cumsum(counts) - counts
    sorted_ids = flat_ids[sort_order]
    rank_within = jnp.arange(row_count, dtype=jnp.int32) - starts[sorted_ids]
    owner = sorted_ids // local_count
    local_slot = sorted_ids % local_count
    target = local_slot * (device_count * capacity) + owner * capacity + rank_within
    source_of = jnp.full((experts * capacity,), row_count, jnp.int32).at[target].set(sort_order)
    target_of = jnp.zeros((row_count,), jnp.int32).at[sort_order].set(target)
    return (source_of, target_of)


def pack_rows(values, source_of, top_count, local_count):
    token_count = values.shape[0]
    with_zero = jnp.concatenate([values, jnp.zeros((1, values.shape[1]), values.dtype)], axis=0)
    token_index = jnp.minimum(source_of // top_count, token_count)
    picked = with_zero[token_index]
    return picked.reshape(local_count, -1, values.shape[1])


def forward_part(received, gate_weight, up_weight, down_weight):
    gate_pre = jnp.einsum("erd,edh->erh", received, gate_weight, preferred_element_type=jnp.float32)
    up_pre = jnp.einsum("erd,edh->erh", received, up_weight, preferred_element_type=jnp.float32)
    sigmoid_gate = jax.nn.sigmoid(gate_pre)
    activ = (gate_pre * sigmoid_gate * up_pre).astype(jnp.bfloat16)
    expert_out = jnp.einsum("erh,ehd->erd", activ, down_weight, preferred_element_type=jnp.float32)
    return (expert_out.astype(jnp.bfloat16), gate_pre, up_pre, sigmoid_gate)


def backward_part(grad_rows, gate_pre, up_pre, sigmoid_gate, gate_weight, up_weight, down_weight):
    grad_act = jnp.einsum(
        "erd,ehd->erh", grad_rows, down_weight, preferred_element_type=jnp.float32
    )
    grad_gate = (grad_act * up_pre * sigmoid_gate * (1.0 + gate_pre * (1.0 - sigmoid_gate))).astype(
        jnp.bfloat16
    )
    grad_up = (grad_act * gate_pre * sigmoid_gate).astype(jnp.bfloat16)
    joined_grad = jnp.concatenate([grad_gate, grad_up], axis=2)
    joined_weight = jnp.concatenate([gate_weight, up_weight], axis=2)
    expert_back = jnp.einsum(
        "erh,edh->erd", joined_grad, joined_weight, preferred_element_type=jnp.float32
    )
    return expert_back.astype(jnp.bfloat16)


def combine_rows(returned, target_of, probs):
    token_count, top_count = probs.shape
    flat_back = returned.reshape(-1, returned.shape[2])
    picked = flat_back[target_of].reshape(token_count, top_count, returned.shape[2])
    return jnp.sum(picked.astype(jnp.float32) * probs[:, :, None], axis=1)


def on_device_routed(tokens, cotangent, expert_ids, probs, gate_weight, up_weight, down_weight):
    local_count = gate_weight.shape[0]
    device_count = lax.axis_size("expert")
    experts = local_count * device_count
    token_count, top_count = expert_ids.shape
    row_count = token_count * top_count
    capacity = row_count * 6 // (5 * experts)
    source_of, target_of = route_slots(expert_ids, local_count, device_count, capacity)
    send_rows = pack_rows(tokens, source_of, top_count, local_count)
    send_grads = pack_rows(cotangent, source_of, top_count, local_count)
    received = lax.all_to_all(send_rows, "expert", split_axis=1, concat_axis=1, tiled=True)
    expert_out, gate_pre, up_pre, sigmoid_gate = forward_part(
        received, gate_weight, up_weight, down_weight
    )
    returned_out = lax.all_to_all(expert_out, "expert", split_axis=1, concat_axis=1, tiled=True)
    received_grads = lax.all_to_all(send_grads, "expert", split_axis=1, concat_axis=1, tiled=True)
    expert_back = backward_part(
        received_grads, gate_pre, up_pre, sigmoid_gate, gate_weight, up_weight, down_weight
    )
    returned_back = lax.all_to_all(expert_back, "expert", split_axis=1, concat_axis=1, tiled=True)
    mixed = combine_rows(returned_out, target_of, probs)
    input_grad = combine_rows(returned_back, target_of, probs)
    return (mixed, input_grad)


def on_device(tokens, cotangent, expert_ids, probs, gate_weight, up_weight, down_weight):
    devices = lax.axis_size("expert")
    dense = devices % 4 == 0 and 12 <= devices <= 2 * expert_ids.shape[1]
    body = on_device_dense if dense else on_device_routed
    return body(tokens, cotangent, expert_ids, probs, gate_weight, up_weight, down_weight)


def solution(mesh):
    in_specs = (
        P(("dp", "expert"), None),
        P(("dp", "expert"), None),
        P(("dp", "expert"), None),
        P(("dp", "expert"), None),
        P(("dp", "expert"), None, None),
        P(("dp", "expert"), None, None),
        P(("dp", "expert"), None, None),
    )
    out_specs = (P(("dp", "expert"), None), P(("dp", "expert"), None))
    return jax.shard_map(
        on_device, mesh=mesh, in_specs=in_specs, out_specs=out_specs, check_vma=False
    )
```

```python
import functools

import jax
import jax.numpy as jnp
from jax import lax
from jax.experimental import pallas as pl
from jax.experimental.pallas import tpu as pltpu
from jax.sharding import PartitionSpec as P

VMEM_BYTES = 18 * 2**20
VMEM_BYTES_FETCH = 56 * 2**20
AT_ONCE = pl.CostEstimate(flops=1, bytes_accessed=1, transcendentals=0)


def resident(shape, index):
    return pl.BlockSpec(shape, index, pipeline_mode=pl.Buffered(1))


def compiler_params(vmem_bytes=VMEM_BYTES):
    return pltpu.CompilerParams(vmem_limit_bytes=vmem_bytes)


def fetch_rows(block_refs, buffer, sems):
    step = pl.program_id(0)
    count = len(block_refs) // pl.num_programs(0)

    @pl.when(step == 0)
    def _():
        for j, ref in enumerate(block_refs):
            pltpu.make_async_copy(ref, buffer.at[j], sems.at[j]).start()

    for j in range(len(block_refs)):

        @pl.when(step == j // count)
        def _(j=j):
            pltpu.make_async_copy(block_refs[j], buffer.at[j], sems.at[j]).wait()

    rows = buffer[pl.ds(step * count, count)]
    return rows.reshape(count * rows.shape[1], rows.shape[2])


def hidden_kernel(blocks, all_experts, owner_ref, gate_ref, up_ref, *refs):
    activ_ref, by_ref, buffer, sems = refs[blocks:]
    experts, width, hidden = gate_ref.shape
    rows = fetch_rows(refs[:blocks], buffer, sems)
    terms = rows[:, width:].astype(jnp.float32)
    rows = rows[:, :width]
    lanes = lax.broadcasted_iota(jnp.int32, terms.shape, 1)
    for e in range(experts):
        cut = slice(e * hidden, (e + 1) * hidden)
        cut_up = slice((experts + e) * hidden, (experts + e + 1) * hidden)
        label = owner_ref[0] * experts + e
        named = (lanes == label) | (lanes == label + all_experts) | (lanes == label + 2 * all_experts)
        weight = jnp.sum(jnp.where(named, terms, 0.0), axis=1, keepdims=True)
        gate_pre = jnp.dot(rows, gate_ref[e], preferred_element_type=jnp.float32)
        up_pre = jnp.dot(rows, up_ref[e], preferred_element_type=jnp.float32)
        sig = jax.nn.sigmoid(gate_pre)
        factor = sig * weight
        silu = gate_pre * factor
        activ_ref[:, cut] = (silu * up_pre).astype(jnp.bfloat16)
        by_ref[:, cut] = up_pre * factor * (1.0 + gate_pre * (1.0 - sig))
        by_ref[:, cut_up] = silu


def hidden_forward(row_blocks, owner, gate_weight, up_weight, all_experts):
    blocks = len(row_blocks)
    block, row_width = row_blocks[0].shape
    experts, width, hidden = gate_weight.shape
    count, columns, tile = blocks * block, experts * hidden, 2 * block
    weights = resident((experts, width, hidden), lambda i: (0, 0, 0))
    return pl.pallas_call(
        functools.partial(hidden_kernel, blocks, all_experts),
        grid=(blocks // 2,),
        in_specs=[pl.BlockSpec(memory_space=pltpu.SMEM), weights, weights]
        + [pl.BlockSpec(memory_space=pl.ANY)] * blocks,
        out_specs=[
            pl.BlockSpec((tile, columns), lambda i: (i, 0)),
            pl.BlockSpec((tile, 2 * columns), lambda i: (i, 0)),
        ],
        out_shape=[
            jax.ShapeDtypeStruct((count, columns), jnp.bfloat16),
            jax.ShapeDtypeStruct((count, 2 * columns), jnp.float32),
        ],
        scratch_shapes=[
            pltpu.VMEM((blocks, block, row_width), jnp.bfloat16),
            pltpu.SemaphoreType.DMA((blocks,)),
        ],
        compiler_params=compiler_params(VMEM_BYTES_FETCH),
        cost_estimate=AT_ONCE,
        name="hidden_forward",
    )(owner.reshape(1), gate_weight, up_weight, *row_blocks)


NT = (((1,), (1,)), ((), ()))


def grads_kernel(blocks, cuts, has_by, has_before, *refs):
    refs = list(refs)
    by_ref = refs.pop(0) if has_by else None
    before_ref = refs.pop(0) if has_before else None
    down_refs, block_refs = refs[: len(cuts)], refs[len(cuts) : len(cuts) + blocks]
    out_ref, buffer, sems = refs[len(cuts) + blocks :]
    rows = fetch_rows(block_refs, buffer, sems)
    total = before_ref[...] if has_before else None
    for (lo, hi), down_ref in zip(cuts, down_refs):
        term = lax.dot_general(rows[:, lo:hi], down_ref[...], NT, preferred_element_type=jnp.float32)
        total = term if total is None else total + term
    if has_by:
        columns = total.shape[1]
        out_ref[:, :columns] = (total * by_ref[:, :columns]).astype(jnp.bfloat16)
        out_ref[:, columns:] = (total * by_ref[:, columns:]).astype(jnp.bfloat16)
    else:
        out_ref[...] = total


def hidden_grads(grad_blocks, downs, cuts, by=None, before=None):
    blocks = len(grad_blocks)
    block, width = grad_blocks[0].shape
    columns = downs[0].shape[0]
    tile = 2 * block

    def rows(count):
        return pl.BlockSpec((tile, count), lambda i: (i, 0))

    given = [x for x in (by, before) if x is not None]
    out_columns, out_type = (columns, jnp.float32) if by is None else (2 * columns, jnp.bfloat16)
    return pl.pallas_call(
        functools.partial(grads_kernel, blocks, tuple(cuts), by is not None, before is not None),
        grid=(blocks // 2,),
        in_specs=[rows(x.shape[1]) for x in given]
        + [resident(d.shape, lambda i: (0, 0)) for d in downs]
        + [pl.BlockSpec(memory_space=pl.ANY)] * blocks,
        out_specs=rows(out_columns),
        out_shape=jax.ShapeDtypeStruct((blocks * block, out_columns), out_type),
        scratch_shapes=[
            pltpu.VMEM((blocks, block, width), jnp.bfloat16),
            pltpu.SemaphoreType.DMA((blocks,)),
        ],
        compiler_params=compiler_params(),
        cost_estimate=AT_ONCE,
        name="hidden_grads",
    )(*given, *downs, *grad_blocks)


def store_half(total, keep_ref, send_ref):
    @pl.when(pl.program_id(0) == 0)
    def _():
        send_ref[...] = total.astype(send_ref.dtype)

    @pl.when(pl.program_id(0) == 1)
    def _():
        keep_ref[...] = total


def mix_kernel(own_ref, other_ref, own_down_ref, other_down_ref, keep_ref, send_ref):
    total = jnp.dot(own_ref[...], own_down_ref[...], preferred_element_type=jnp.float32)
    total += jnp.dot(other_ref[...], other_down_ref[...], preferred_element_type=jnp.float32)
    store_half(total, keep_ref, send_ref)


def back_kernel(own_ref, other_ref, *refs):
    weight_refs, (keep_ref, send_ref) = refs[:-2], refs[-2:]
    experts, _, hidden = weight_refs[0].shape
    total = None
    for at, weight_ref in enumerate(weight_refs):
        grads_ref = (own_ref, other_ref)[at // 2]
        for e in range(experts):
            first = (at % 2 * experts + e) * hidden
            term = lax.dot_general(
                grads_ref[:, first : first + hidden], weight_ref[e], NT, preferred_element_type=jnp.float32
            )
            total = term if total is None else total + term
    store_half(total, keep_ref, send_ref)


def sum_columns(kernel, name, columns, own, other, weights, weight_specs):
    half, depth = own.shape[0] // 2, own.shape[1]
    rows = pl.BlockSpec((half, depth), lambda i: (1 - i, 0))
    return pl.pallas_call(
        kernel,
        grid=(2,),
        in_specs=[rows, rows] + weight_specs,
        out_specs=[pl.BlockSpec((half, columns), lambda i: (0, 0))] * 2,
        out_shape=[
            jax.ShapeDtypeStruct((half, columns), jnp.float32),
            jax.ShapeDtypeStruct((half, columns), jnp.bfloat16),
        ],
        compiler_params=compiler_params(),
        cost_estimate=AT_ONCE,
        name=name,
    )(own, other, *weights)


def mix_columns(own, other, own_down, other_down, at):
    depth, columns = other_down.shape
    specs = [
        resident((depth, columns), lambda i: (0, at)),
        resident((depth, columns), lambda i: (0, 0)),
    ]
    return sum_columns(mix_kernel, "mix_columns", columns, own, other, [own_down, other_down], specs)


def back_columns(own, other, weights, at, columns):
    experts, _, hidden = weights[0].shape
    specs = [resident((experts, columns, hidden), lambda i: (0, at, 0))] * len(weights)
    return sum_columns(back_kernel, "back_columns", columns, own, other, weights, specs)


def add_kernel(keep_ref, come_ref, *out_refs):
    block = out_refs[0].shape[0]
    for k, out_ref in enumerate(out_refs):
        cut = slice(k * block, (k + 1) * block)
        total = keep_ref[cut, :] + come_ref[cut, :].astype(jnp.float32)
        out_ref[...] = total.astype(out_ref.dtype)


def add_sides(keep, come, types):
    block, columns = keep.shape[0] // len(types), keep.shape[1]
    return pl.pallas_call(
        add_kernel,
        out_shape=[jax.ShapeDtypeStruct((block, columns), t) for t in types],
        compiler_params=compiler_params(),
        cost_estimate=AT_ONCE,
        name="add_sides",
    )(keep, come)


def add_piece(piece, come):
    return pl.pallas_call(
        add_kernel,
        out_shape=jax.ShapeDtypeStruct(piece.shape, jnp.bfloat16),
        compiler_params=compiler_params(),
        cost_estimate=AT_ONCE,
        name="add_piece",
    )(piece, come)


def pair_kernel(keep_ref, send_ref, own_ref, side_ref, *piece_refs):
    block = own_ref.shape[0]
    own_ref[...] = keep_ref[:block, :]
    side_ref[...] = send_ref[:block, :].astype(side_ref.dtype)
    for k, piece_ref in enumerate(piece_refs, 1):
        cut = slice(k * block, (k + 1) * block)
        piece_ref[:block, :] = keep_ref[cut, :].astype(piece_ref.dtype)
        piece_ref[block:, :] = send_ref[cut, :].astype(piece_ref.dtype)


def pair_sides(keep, send, types):
    block, columns = keep.shape[0] // len(types), keep.shape[1]
    pieces = [jax.ShapeDtypeStruct((2 * block, columns), t) for t in types[1:]]
    return pl.pallas_call(
        pair_kernel,
        out_shape=[jax.ShapeDtypeStruct((block, columns), jnp.float32)] * 2 + pieces,
        compiler_params=compiler_params(),
        cost_estimate=AT_ONCE,
        name="pair_sides",
    )(keep, send)


def parts_kernel(side_ref, *refs):
    block = side_ref.shape[0]
    total = side_ref[...]
    for part_ref in refs[:-1]:
        total += part_ref[block:, :].astype(jnp.float32)
    refs[-1][...] = total.astype(refs[-1].dtype)


def add_parts(side, *parts):
    return pl.pallas_call(
        parts_kernel,
        out_shape=jax.ShapeDtypeStruct(side.shape, jnp.bfloat16),
        compiler_params=compiler_params(),
        cost_estimate=AT_ONCE,
        name="add_parts",
    )(side, *parts)


def finish_kernel(chunks, counts, *refs):
    out_ref = refs[-1]
    refs = list(refs[:-1])
    for (lo, hi), count in zip(chunks, counts):
        own_ref, *piece_refs = refs[:count]
        del refs[:count]
        total = own_ref[...]
        for piece_ref in piece_refs:
            total += piece_ref[: total.shape[0], :].astype(jnp.float32)
        out_ref[:, lo:hi] = total


def finish(chunks, parts, width):
    return pl.pallas_call(
        functools.partial(finish_kernel, tuple(chunks), tuple(map(len, parts))),
        out_shape=jax.ShapeDtypeStruct((parts[0][0].shape[0], width), jnp.float32),
        compiler_params=compiler_params(),
        cost_estimate=AT_ONCE,
        name="finish",
    )(*[p for part in parts for p in part])


def cut_columns(width, eighths):
    eighth = width // 8
    return [(lo * eighth, hi * eighth) for lo, hi in eighths]


def after(values, *others):
    return lax.optimization_barrier((values, *others))[0]


def send_all(sends, *waits):
    values, _ = lax.optimization_barrier(([v for v, _ in sends], waits))
    return [lax.ppermute(v, "expert", pairs) for v, (_, pairs) in zip(values, sends)]


def on_device_dense(tokens, cotangent, expert_ids, probs, gate_weight, up_weight, down_weight):
    local_count, hidden, width = down_weight.shape
    devices = lax.axis_size("expert")
    layers = devices // 4
    experts = local_count * devices
    block = tokens.shape[0]
    chunks = cut_columns(width, ((0, 4), (4, 8)))
    back_chunks = cut_columns(width, ((6, 8), (0, 4), (4, 6)))
    me = lax.axis_index("expert")
    twin = [(d, d ^ 1) for d in range(devices)]
    side = [(d, d ^ 2) for d in range(devices)]
    layer = [[(d, (d + 4 * k) % devices) for d in range(devices)] for k in range(layers)]

    labels = lax.broadcasted_iota(jnp.int32, (1, 1, experts), 2)
    weight = jnp.sum(jnp.where(expert_ids[:, :, None] == labels, probs[:, :, None], 0.0), axis=1)
    first = lax.reduce_precision(weight, 8, 7)
    second = lax.reduce_precision(weight - first, 8, 7)
    third = weight - first - second
    spare = jnp.zeros((block, -3 * experts % 128), jnp.bfloat16)
    terms = [t.astype(jnp.bfloat16) for t in (first, second, third)]
    row = jnp.concatenate([tokens] + terms + [spare], axis=1)
    grad = cotangent
    down = down_weight.reshape(local_count * hidden, width)
    downs = [down[:, lo:hi] for lo, hi in chunks]

    one, last, *middle = [1, layers - 1, *range(2, layers - 1)]
    rows, far_rows, grads, far_grads = {0: row}, {}, {0: grad}, {}
    other_gate, rows[one], far_rows[0] = send_all([(gate_weight, twin), (row, layer[-one]), (row, side)])
    rows[last], far_grads[0] = send_all([(row, layer[-last]), (grad, side)])
    (far_rows[one],) = send_all([(rows[one], side)], far_rows[0])
    for k in middle:
        (rows[k],) = send_all([(rows[k - 1], layer[-one])], far_rows[0])
    other_up, far_rows[last] = send_all([(up_weight, twin), (rows[last], side)], far_grads[0])
    got = send_all([(grad, layer[-one])] + [(rows[k], side) for k in middle], far_rows[one])
    grads[one] = got[0]
    far_rows.update(zip(middle, got[1:]))
    down_0, grads[last] = send_all([(downs[0], twin), (grad, layer[-last])], far_rows[last], other_gate)
    (far_grads[one],) = send_all([(grads[one], side)], *far_rows.values())
    for k in middle:
        (grads[k],) = send_all([(grads[k - 1], layer[-one])], *far_rows.values())
    (far_grads[last],) = send_all([(grads[last], side)], *far_rows.values())
    row_blocks = [rows[k] for k in range(layers)] + [far_rows[k] for k in range(layers)]
    activ, by = hidden_forward(row_blocks, me, gate_weight, up_weight, experts)
    for k in middle:
        (far_grads[k],) = send_all([(grads[k], side)], far_grads[one], activ)
    other_up = after(other_up, activ)
    other_activ, other_by = hidden_forward(row_blocks, me ^ 1, other_gate, other_up, experts)

    (down_1,) = send_all([(downs[1], twin)], down_0, activ, other_activ)

    def mix(c, other_down, *waits):
        lo, hi = chunks[c]
        return mix_columns(activ, other_activ, down, after(other_down, *waits), lo // (hi - lo))

    types = [jnp.float32, jnp.float32] + [jnp.bfloat16] * (layers - 2)

    def send_on(pieces, *waits):
        (far,) = send_all([(pieces[-1], layer[last])], *waits)
        come = None
        for k in reversed(middle):
            piece = pieces[k - 1] if come is None else add_piece(pieces[k - 1], come)
            (come,) = send_all([(piece, layer[one])], *waits)
        return far, come

    def send_last(pieces, come, *waits):
        piece = pieces[0].astype(jnp.bfloat16) if come is None else add_piece(pieces[0], come)
        return send_all([(piece, layer[one])], *waits)[0]

    keep_0, send = mix(0, down_0, other_activ, *far_grads.values())
    (come_0,) = send_all([(send, side)])
    grad_blocks = [grads[k] for k in range(layers)] + [far_grads[k] for k in range(layers)]
    own_grads = hidden_grads(grad_blocks, [down], [(0, width)], by=by)

    keep_1, send = mix(1, down_1, send)
    (come_1,) = send_all([(send, side)], own_grads)
    own_0, *pieces_0 = add_sides(after(keep_0, send), come_0, types)
    far_0, next_0 = send_on(pieces_0)

    other_by = after(other_by, next_0, far_0)
    other_grads = hidden_grads(grad_blocks, [down_0, down_1], chunks, by=other_by)
    weights = [gate_weight, up_weight, other_gate, other_up]

    def back(c, *waits):
        lo, hi = back_chunks[c]
        return back_columns(own_grads, after(other_grads, *waits), weights, lo // (hi - lo), hi - lo)

    own_2, side_2, *pieces_2 = pair_sides(*back(0), types)
    far_2, next_2 = send_on(pieces_2)
    near_0 = send_last(pieces_0, next_0)

    keep_3, send = back(1, own_2)
    (come_3,) = send_all([(send, side)], own_0)

    own_1, *pieces_1 = add_sides(after(keep_1, send), come_1, types)
    near_2 = send_last(pieces_2, next_2, far_2)
    far_1, next_1 = send_on(pieces_1, near_0)
    keep_4, send = back(2, next_1)
    (come_4,) = send_all([(send, side)], own_1)
    near_1 = send_last(pieces_1, next_1, far_1, near_2)
    (come_2,) = send_all([(add_parts(side_2, far_2, near_2), side)], own_1)

    own_3, *pieces_3 = add_sides(after(keep_3, send), come_3, types)
    far_3, next_3 = send_on(pieces_3, near_1)
    near_3 = send_last(pieces_3, next_3, far_3)

    mixed = finish(chunks, [(own_0, far_0, near_0), (own_1, far_1, near_1)], width)
    types = [jnp.float32] + [jnp.bfloat16] * (layers - 1)
    own_4, *pieces_4 = add_sides(keep_4, after(come_4, own_3), types)
    parts_4 = send_all([(piece, layer[k]) for k, piece in enumerate(pieces_4, 1)], mixed)
    back_parts = [(own_2, far_2, near_2, come_2), (own_3, far_3, near_3), (own_4, *parts_4)]
    return (mixed, finish(back_chunks, back_parts, width))


def route_slots(expert_ids, local_count, device_count, capacity):
    experts = local_count * device_count
    row_count = expert_ids.shape[0] * expert_ids.shape[1]
    flat_ids = expert_ids.reshape(row_count)
    sort_order = jnp.argsort(flat_ids, stable=True)
    labels = lax.broadcasted_iota(jnp.int32, (1, experts), 1)
    counts = jnp.sum((flat_ids[:, None] == labels).astype(jnp.int32), axis=0)
    starts = jnp.cumsum(counts) - counts
    sorted_ids = flat_ids[sort_order]
    rank_within = jnp.arange(row_count, dtype=jnp.int32) - starts[sorted_ids]
    owner = sorted_ids // local_count
    local_slot = sorted_ids % local_count
    target = local_slot * (device_count * capacity) + owner * capacity + rank_within
    source_of = jnp.full((experts * capacity,), row_count, jnp.int32).at[target].set(sort_order)
    target_of = jnp.zeros((row_count,), jnp.int32).at[sort_order].set(target)
    return (source_of, target_of)


def pack_rows(values, source_of, top_count, local_count):
    token_count = values.shape[0]
    with_zero = jnp.concatenate([values, jnp.zeros((1, values.shape[1]), values.dtype)], axis=0)
    token_index = jnp.minimum(source_of // top_count, token_count)
    picked = with_zero[token_index]
    return picked.reshape(local_count, -1, values.shape[1])


def forward_part(received, gate_weight, up_weight, down_weight):
    gate_pre = jnp.einsum("erd,edh->erh", received, gate_weight, preferred_element_type=jnp.float32)
    up_pre = jnp.einsum("erd,edh->erh", received, up_weight, preferred_element_type=jnp.float32)
    sigmoid_gate = jax.nn.sigmoid(gate_pre)
    activ = (gate_pre * sigmoid_gate * up_pre).astype(jnp.bfloat16)
    expert_out = jnp.einsum("erh,ehd->erd", activ, down_weight, preferred_element_type=jnp.float32)
    return (expert_out.astype(jnp.bfloat16), gate_pre, up_pre, sigmoid_gate)


def backward_part(grad_rows, gate_pre, up_pre, sigmoid_gate, gate_weight, up_weight, down_weight):
    grad_act = jnp.einsum(
        "erd,ehd->erh", grad_rows, down_weight, preferred_element_type=jnp.float32
    )
    grad_gate = (grad_act * up_pre * sigmoid_gate * (1.0 + gate_pre * (1.0 - sigmoid_gate))).astype(
        jnp.bfloat16
    )
    grad_up = (grad_act * gate_pre * sigmoid_gate).astype(jnp.bfloat16)
    joined_grad = jnp.concatenate([grad_gate, grad_up], axis=2)
    joined_weight = jnp.concatenate([gate_weight, up_weight], axis=2)
    expert_back = jnp.einsum(
        "erh,edh->erd", joined_grad, joined_weight, preferred_element_type=jnp.float32
    )
    return expert_back.astype(jnp.bfloat16)


def combine_rows(returned, target_of, probs):
    token_count, top_count = probs.shape
    flat_back = returned.reshape(-1, returned.shape[2])
    picked = flat_back[target_of].reshape(token_count, top_count, returned.shape[2])
    return jnp.sum(picked.astype(jnp.float32) * probs[:, :, None], axis=1)


def on_device_routed(tokens, cotangent, expert_ids, probs, gate_weight, up_weight, down_weight):
    local_count = gate_weight.shape[0]
    device_count = lax.axis_size("expert")
    experts = local_count * device_count
    token_count, top_count = expert_ids.shape
    row_count = token_count * top_count
    capacity = row_count * 6 // (5 * experts)
    source_of, target_of = route_slots(expert_ids, local_count, device_count, capacity)
    send_rows = pack_rows(tokens, source_of, top_count, local_count)
    send_grads = pack_rows(cotangent, source_of, top_count, local_count)
    received = lax.all_to_all(send_rows, "expert", split_axis=1, concat_axis=1, tiled=True)
    expert_out, gate_pre, up_pre, sigmoid_gate = forward_part(
        received, gate_weight, up_weight, down_weight
    )
    returned_out = lax.all_to_all(expert_out, "expert", split_axis=1, concat_axis=1, tiled=True)
    received_grads = lax.all_to_all(send_grads, "expert", split_axis=1, concat_axis=1, tiled=True)
    expert_back = backward_part(
        received_grads, gate_pre, up_pre, sigmoid_gate, gate_weight, up_weight, down_weight
    )
    returned_back = lax.all_to_all(expert_back, "expert", split_axis=1, concat_axis=1, tiled=True)
    mixed = combine_rows(returned_out, target_of, probs)
    input_grad = combine_rows(returned_back, target_of, probs)
    return (mixed, input_grad)


def on_device(tokens, cotangent, expert_ids, probs, gate_weight, up_weight, down_weight):
    devices = lax.axis_size("expert")
    dense = devices % 4 == 0 and 12 <= devices <= 2 * expert_ids.shape[1]
    body = on_device_dense if dense else on_device_routed
    return body(tokens, cotangent, expert_ids, probs, gate_weight, up_weight, down_weight)


def solution(mesh):
    in_specs = (
        P(("dp", "expert"), None),
        P(("dp", "expert"), None),
        P(("dp", "expert"), None),
        P(("dp", "expert"), None),
        P(("dp", "expert"), None, None),
        P(("dp", "expert"), None, None),
        P(("dp", "expert"), None, None),
    )
    out_specs = (P(("dp", "expert"), None), P(("dp", "expert"), None))
    return jax.shard_map(
        on_device, mesh=mesh, in_specs=in_specs, out_specs=out_specs, check_vma=False
    )
```

```python
import functools

import jax
import jax.numpy as jnp
from jax import lax
from jax.experimental import pallas as pl
from jax.experimental.pallas import tpu as pltpu
from jax.sharding import PartitionSpec as P

VMEM_BYTES = 18 * 2**20
VMEM_BYTES_FETCH = 56 * 2**20
AT_ONCE = pl.CostEstimate(flops=1, bytes_accessed=1, transcendentals=0)


def resident(shape, index):
    return pl.BlockSpec(shape, index, pipeline_mode=pl.Buffered(1))


def compiler_params(vmem_bytes=VMEM_BYTES):
    return pltpu.CompilerParams(vmem_limit_bytes=vmem_bytes)


def fetch_rows(block_refs, buffer, sems):
    step = pl.program_id(0)
    count = len(block_refs) // pl.num_programs(0)

    @pl.when(step == 0)
    def _():
        for j, ref in enumerate(block_refs):
            pltpu.make_async_copy(ref, buffer.at[j], sems.at[j]).start()

    for j in range(len(block_refs)):

        @pl.when(step == j // count)
        def _(j=j):
            pltpu.make_async_copy(block_refs[j], buffer.at[j], sems.at[j]).wait()

    rows = buffer[pl.ds(step * count, count)]
    return rows.reshape(count * rows.shape[1], rows.shape[2])


def hidden_kernel(blocks, all_experts, owner_ref, gate_ref, up_ref, *refs):
    activ_ref, by_ref, buffer, sems = refs[blocks:]
    experts, width, hidden = gate_ref.shape
    rows = fetch_rows(refs[:blocks], buffer, sems)
    terms = rows[:, width:].astype(jnp.float32)
    rows = rows[:, :width]
    lanes = lax.broadcasted_iota(jnp.int32, terms.shape, 1)
    for e in range(experts):
        cut = slice(e * hidden, (e + 1) * hidden)
        cut_up = slice((experts + e) * hidden, (experts + e + 1) * hidden)
        label = owner_ref[0] * experts + e
        named = (lanes == label) | (lanes == label + all_experts) | (lanes == label + 2 * all_experts)
        weight = jnp.sum(jnp.where(named, terms, 0.0), axis=1, keepdims=True)
        gate_pre = jnp.dot(rows, gate_ref[e], preferred_element_type=jnp.float32)
        up_pre = jnp.dot(rows, up_ref[e], preferred_element_type=jnp.float32)
        sig = jax.nn.sigmoid(gate_pre)
        factor = sig * weight
        silu = gate_pre * factor
        activ_ref[:, cut] = (silu * up_pre).astype(jnp.bfloat16)
        by_ref[:, cut] = up_pre * factor * (1.0 + gate_pre * (1.0 - sig))
        by_ref[:, cut_up] = silu


def hidden_forward(row_blocks, owner, gate_weight, up_weight, all_experts):
    blocks = len(row_blocks)
    block, row_width = row_blocks[0].shape
    experts, width, hidden = gate_weight.shape
    count, columns, tile = blocks * block, experts * hidden, 2 * block
    weights = resident((experts, width, hidden), lambda i: (0, 0, 0))
    return pl.pallas_call(
        functools.partial(hidden_kernel, blocks, all_experts),
        grid=(blocks // 2,),
        in_specs=[pl.BlockSpec(memory_space=pltpu.SMEM), weights, weights]
        + [pl.BlockSpec(memory_space=pl.ANY)] * blocks,
        out_specs=[
            pl.BlockSpec((tile, columns), lambda i: (i, 0)),
            pl.BlockSpec((tile, 2 * columns), lambda i: (i, 0)),
        ],
        out_shape=[
            jax.ShapeDtypeStruct((count, columns), jnp.bfloat16),
            jax.ShapeDtypeStruct((count, 2 * columns), jnp.float32),
        ],
        scratch_shapes=[
            pltpu.VMEM((blocks, block, row_width), jnp.bfloat16),
            pltpu.SemaphoreType.DMA((blocks,)),
        ],
        compiler_params=compiler_params(VMEM_BYTES_FETCH),
        cost_estimate=AT_ONCE,
        name="hidden_forward",
    )(owner.reshape(1), gate_weight, up_weight, *row_blocks)


NT = (((1,), (1,)), ((), ()))


def grads_kernel(blocks, cuts, has_by, has_before, *refs):
    refs = list(refs)
    by_ref = refs.pop(0) if has_by else None
    before_ref = refs.pop(0) if has_before else None
    down_refs, block_refs = refs[: len(cuts)], refs[len(cuts) : len(cuts) + blocks]
    out_ref, buffer, sems = refs[len(cuts) + blocks :]
    rows = fetch_rows(block_refs, buffer, sems)
    total = before_ref[...] if has_before else None
    for (lo, hi), down_ref in zip(cuts, down_refs):
        term = lax.dot_general(rows[:, lo:hi], down_ref[...], NT, preferred_element_type=jnp.float32)
        total = term if total is None else total + term
    if has_by:
        columns = total.shape[1]
        out_ref[:, :columns] = (total * by_ref[:, :columns]).astype(jnp.bfloat16)
        out_ref[:, columns:] = (total * by_ref[:, columns:]).astype(jnp.bfloat16)
    else:
        out_ref[...] = total


def hidden_grads(grad_blocks, downs, cuts, by=None, before=None):
    blocks = len(grad_blocks)
    block, width = grad_blocks[0].shape
    columns = downs[0].shape[0]
    tile = 2 * block

    def rows(count):
        return pl.BlockSpec((tile, count), lambda i: (i, 0))

    given = [x for x in (by, before) if x is not None]
    out_columns, out_type = (columns, jnp.float32) if by is None else (2 * columns, jnp.bfloat16)
    return pl.pallas_call(
        functools.partial(grads_kernel, blocks, tuple(cuts), by is not None, before is not None),
        grid=(blocks // 2,),
        in_specs=[rows(x.shape[1]) for x in given]
        + [resident(d.shape, lambda i: (0, 0)) for d in downs]
        + [pl.BlockSpec(memory_space=pl.ANY)] * blocks,
        out_specs=rows(out_columns),
        out_shape=jax.ShapeDtypeStruct((blocks * block, out_columns), out_type),
        scratch_shapes=[
            pltpu.VMEM((blocks, block, width), jnp.bfloat16),
            pltpu.SemaphoreType.DMA((blocks,)),
        ],
        compiler_params=compiler_params(),
        cost_estimate=AT_ONCE,
        name="hidden_grads",
    )(*given, *downs, *grad_blocks)


def store_half(total, keep_ref, send_ref):
    @pl.when(pl.program_id(0) == 0)
    def _():
        send_ref[...] = total.astype(send_ref.dtype)

    @pl.when(pl.program_id(0) == 1)
    def _():
        keep_ref[...] = total


def mix_kernel(own_ref, other_ref, own_down_ref, other_down_ref, keep_ref, send_ref):
    total = jnp.dot(own_ref[...], own_down_ref[...], preferred_element_type=jnp.float32)
    total += jnp.dot(other_ref[...], other_down_ref[...], preferred_element_type=jnp.float32)
    store_half(total, keep_ref, send_ref)


def back_kernel(own_ref, other_ref, *refs):
    weight_refs, (keep_ref, send_ref) = refs[:-2], refs[-2:]
    experts, _, hidden = weight_refs[0].shape
    total = None
    for at, weight_ref in enumerate(weight_refs):
        grads_ref = (own_ref, other_ref)[at // 2]
        for e in range(experts):
            first = (at % 2 * experts + e) * hidden
            term = lax.dot_general(
                grads_ref[:, first : first + hidden], weight_ref[e], NT, preferred_element_type=jnp.float32
            )
            total = term if total is None else total + term
    store_half(total, keep_ref, send_ref)


def sum_columns(kernel, name, columns, own, other, weights, weight_specs):
    half, depth = own.shape[0] // 2, own.shape[1]
    rows = pl.BlockSpec((half, depth), lambda i: (1 - i, 0))
    return pl.pallas_call(
        kernel,
        grid=(2,),
        in_specs=[rows, rows] + weight_specs,
        out_specs=[pl.BlockSpec((half, columns), lambda i: (0, 0))] * 2,
        out_shape=[
            jax.ShapeDtypeStruct((half, columns), jnp.float32),
            jax.ShapeDtypeStruct((half, columns), jnp.bfloat16),
        ],
        compiler_params=compiler_params(),
        cost_estimate=AT_ONCE,
        name=name,
    )(own, other, *weights)


def mix_columns(own, other, own_down, other_down, at):
    depth, columns = other_down.shape
    specs = [
        resident((depth, columns), lambda i: (0, at)),
        resident((depth, columns), lambda i: (0, 0)),
    ]
    return sum_columns(mix_kernel, "mix_columns", columns, own, other, [own_down, other_down], specs)


def back_columns(own, other, weights, at, columns):
    experts, _, hidden = weights[0].shape
    specs = [resident((experts, columns, hidden), lambda i: (0, at, 0))] * len(weights)
    return sum_columns(back_kernel, "back_columns", columns, own, other, weights, specs)


def add_kernel(keep_ref, come_ref, *out_refs):
    block = out_refs[0].shape[0]
    for k, out_ref in enumerate(out_refs):
        cut = slice(k * block, (k + 1) * block)
        total = keep_ref[cut, :] + come_ref[cut, :].astype(jnp.float32)
        out_ref[...] = total.astype(out_ref.dtype)


def add_sides(keep, come, types):
    block, columns = keep.shape[0] // len(types), keep.shape[1]
    return pl.pallas_call(
        add_kernel,
        out_shape=[jax.ShapeDtypeStruct((block, columns), t) for t in types],
        compiler_params=compiler_params(),
        cost_estimate=AT_ONCE,
        name="add_sides",
    )(keep, come)


def add_piece(piece, come):
    return pl.pallas_call(
        add_kernel,
        out_shape=jax.ShapeDtypeStruct(piece.shape, jnp.bfloat16),
        compiler_params=compiler_params(),
        cost_estimate=AT_ONCE,
        name="add_piece",
    )(piece, come)


def finish_kernel(chunks, counts, *refs):
    out_ref = refs[-1]
    refs = list(refs[:-1])
    for (lo, hi), count in zip(chunks, counts):
        own_ref, *piece_refs = refs[:count]
        del refs[:count]
        total = own_ref[...]
        for piece_ref in piece_refs:
            total += piece_ref[...].astype(jnp.float32)
        out_ref[:, lo:hi] = total


def finish(chunks, parts, width):
    return pl.pallas_call(
        functools.partial(finish_kernel, tuple(chunks), tuple(map(len, parts))),
        out_shape=jax.ShapeDtypeStruct((parts[0][0].shape[0], width), jnp.float32),
        compiler_params=compiler_params(),
        cost_estimate=AT_ONCE,
        name="finish",
    )(*[p for part in parts for p in part])


def cut_columns(width, eighths):
    eighth = width // 8
    return [(lo * eighth, hi * eighth) for lo, hi in eighths]


def after(values, *others):
    return lax.optimization_barrier((values, *others))[0]


def send_all(sends, *waits):
    values, _ = lax.optimization_barrier(([v for v, _ in sends], waits))
    return [lax.ppermute(v, "expert", pairs) for v, (_, pairs) in zip(values, sends)]


def on_device_dense(tokens, cotangent, expert_ids, probs, gate_weight, up_weight, down_weight):
    local_count, hidden, width = down_weight.shape
    devices = lax.axis_size("expert")
    layers = devices // 4
    experts = local_count * devices
    block = tokens.shape[0]
    chunks = cut_columns(width, ((0, 4), (4, 8)))
    back_chunks = cut_columns(width, ((0, 5), (6, 8), (5, 6)))
    me = lax.axis_index("expert")
    twin = [(d, d ^ 1) for d in range(devices)]
    side = [(d, d ^ 2) for d in range(devices)]
    layer = [[(d, (d + 4 * k) % devices) for d in range(devices)] for k in range(layers)]

    labels = lax.broadcasted_iota(jnp.int32, (1, 1, experts), 2)
    weight = jnp.sum(jnp.where(expert_ids[:, :, None] == labels, probs[:, :, None], 0.0), axis=1)
    first = lax.reduce_precision(weight, 8, 7)
    second = lax.reduce_precision(weight - first, 8, 7)
    third = weight - first - second
    spare = jnp.zeros((block, -3 * experts % 128), jnp.bfloat16)
    terms = [t.astype(jnp.bfloat16) for t in (first, second, third)]
    row = jnp.concatenate([tokens] + terms + [spare], axis=1)
    grad = cotangent
    down = down_weight.reshape(local_count * hidden, width)
    downs = [down[:, lo:hi] for lo, hi in chunks]

    one, last, *middle = [1, layers - 1, *range(2, layers - 1)]
    rows, far_rows, grads, far_grads = {0: row}, {}, {0: grad}, {}
    other_gate, rows[one], far_rows[0] = send_all([(gate_weight, twin), (row, layer[-one]), (row, side)])
    rows[last], far_grads[0] = send_all([(row, layer[-last]), (grad, side)])
    (far_rows[one],) = send_all([(rows[one], side)], far_rows[0])
    for k in middle:
        (rows[k],) = send_all([(rows[k - 1], layer[-one])], far_rows[0])
    other_up, far_rows[last] = send_all([(up_weight, twin), (rows[last], side)], far_grads[0])
    got = send_all([(grad, layer[-one])] + [(rows[k], side) for k in middle], far_rows[one])
    grads[one] = got[0]
    far_rows.update(zip(middle, got[1:]))
    down_0, grads[last] = send_all([(downs[0], twin), (grad, layer[-last])], far_rows[last], other_gate)
    (far_grads[one],) = send_all([(grads[one], side)], *far_rows.values())
    for k in middle:
        (grads[k],) = send_all([(grads[k - 1], layer[-one])], *far_rows.values())
    (far_grads[last],) = send_all([(grads[last], side)], *far_rows.values())
    row_blocks = [rows[k] for k in range(layers)] + [far_rows[k] for k in range(layers)]
    activ, by = hidden_forward(row_blocks, me, gate_weight, up_weight, experts)
    for k in middle:
        (far_grads[k],) = send_all([(grads[k], side)], far_grads[one], activ)
    other_up = after(other_up, activ)
    other_activ, other_by = hidden_forward(row_blocks, me ^ 1, other_gate, other_up, experts)

    (down_1,) = send_all([(downs[1], twin)], down_0, activ, other_activ)

    def mix(c, other_down, *waits):
        lo, hi = chunks[c]
        return mix_columns(activ, other_activ, down, after(other_down, *waits), lo // (hi - lo))

    types = [jnp.float32, jnp.float32] + [jnp.bfloat16] * (layers - 2)

    def send_on(pieces, *waits):
        (far,) = send_all([(pieces[-1], layer[last])], *waits)
        come = None
        for k in reversed(middle):
            piece = pieces[k - 1] if come is None else add_piece(pieces[k - 1], come)
            (come,) = send_all([(piece, layer[one])], *waits)
        return far, come

    def send_last(pieces, come, *waits):
        piece = pieces[0].astype(jnp.bfloat16) if come is None else add_piece(pieces[0], come)
        return send_all([(piece, layer[one])], *waits)[0]

    keep_0, send = mix(0, down_0, other_activ, *far_grads.values())
    (come_0,) = send_all([(send, side)])
    grad_blocks = [grads[k] for k in range(layers)] + [far_grads[k] for k in range(layers)]
    own_grads = hidden_grads(grad_blocks, [down], [(0, width)], by=by)

    keep_1, send = mix(1, down_1, send)
    (come_1,) = send_all([(send, side)], own_grads)

    other_by = after(other_by, send)
    other_grads = hidden_grads(grad_blocks, [down_0, down_1], chunks, by=other_by)
    weights = [gate_weight, up_weight, other_gate, other_up]

    def back(c, *waits):
        lo, hi = back_chunks[c]
        return back_columns(own_grads, after(other_grads, *waits), weights, lo // (hi - lo), hi - lo)

    own_0, *pieces = add_sides(after(keep_0, other_grads), come_0, types)
    far_0, next_0 = send_on(pieces)
    keep_2, send = back(0, next_0, far_0)
    near_0 = send_last(pieces, next_0)
    (come_2,) = send_all([(send, side)], own_0)

    own_1, *pieces = add_sides(after(keep_1, send), come_1, types)
    far_1, next_1 = send_on(pieces, near_0)
    keep_3, send = back(1, next_1)
    (come_3,) = send_all([(send, side)], own_1)
    near_1 = send_last(pieces, next_1, far_1)

    keep_4, send = back(2, near_1)
    own_2, *pieces = add_sides(after(keep_2, send), come_2, types)
    (come_4,) = send_all([(send, side)], own_2)
    far_2, next_2 = send_on(pieces)
    near_2 = send_last(pieces, next_2, far_2)

    own_3, *pieces = add_sides(keep_3, after(come_3, next_2), types)
    far_3, next_3 = send_on(pieces)
    near_3 = send_last(pieces, next_3, far_3)

    mixed = finish(chunks, [(own_0, far_0, near_0), (own_1, far_1, near_1)], width)
    types = [jnp.float32] + [jnp.bfloat16] * (layers - 1)
    own_4, *pieces = add_sides(keep_4, after(come_4, own_3), types)
    parts_4 = send_all([(piece, layer[k]) for k, piece in enumerate(pieces, 1)], mixed)
    back_parts = [(own_2, far_2, near_2), (own_3, far_3, near_3), (own_4, *parts_4)]
    return (mixed, finish(back_chunks, back_parts, width))


def route_slots(expert_ids, local_count, device_count, capacity):
    experts = local_count * device_count
    row_count = expert_ids.shape[0] * expert_ids.shape[1]
    flat_ids = expert_ids.reshape(row_count)
    sort_order = jnp.argsort(flat_ids, stable=True)
    labels = lax.broadcasted_iota(jnp.int32, (1, experts), 1)
    counts = jnp.sum((flat_ids[:, None] == labels).astype(jnp.int32), axis=0)
    starts = jnp.cumsum(counts) - counts
    sorted_ids = flat_ids[sort_order]
    rank_within = jnp.arange(row_count, dtype=jnp.int32) - starts[sorted_ids]
    owner = sorted_ids // local_count
    local_slot = sorted_ids % local_count
    target = local_slot * (device_count * capacity) + owner * capacity + rank_within
    source_of = jnp.full((experts * capacity,), row_count, jnp.int32).at[target].set(sort_order)
    target_of = jnp.zeros((row_count,), jnp.int32).at[sort_order].set(target)
    return (source_of, target_of)


def pack_rows(values, source_of, top_count, local_count):
    token_count = values.shape[0]
    with_zero = jnp.concatenate([values, jnp.zeros((1, values.shape[1]), values.dtype)], axis=0)
    token_index = jnp.minimum(source_of // top_count, token_count)
    picked = with_zero[token_index]
    return picked.reshape(local_count, -1, values.shape[1])


def forward_part(received, gate_weight, up_weight, down_weight):
    gate_pre = jnp.einsum("erd,edh->erh", received, gate_weight, preferred_element_type=jnp.float32)
    up_pre = jnp.einsum("erd,edh->erh", received, up_weight, preferred_element_type=jnp.float32)
    sigmoid_gate = jax.nn.sigmoid(gate_pre)
    activ = (gate_pre * sigmoid_gate * up_pre).astype(jnp.bfloat16)
    expert_out = jnp.einsum("erh,ehd->erd", activ, down_weight, preferred_element_type=jnp.float32)
    return (expert_out.astype(jnp.bfloat16), gate_pre, up_pre, sigmoid_gate)


def backward_part(grad_rows, gate_pre, up_pre, sigmoid_gate, gate_weight, up_weight, down_weight):
    grad_act = jnp.einsum(
        "erd,ehd->erh", grad_rows, down_weight, preferred_element_type=jnp.float32
    )
    grad_gate = (grad_act * up_pre * sigmoid_gate * (1.0 + gate_pre * (1.0 - sigmoid_gate))).astype(
        jnp.bfloat16
    )
    grad_up = (grad_act * gate_pre * sigmoid_gate).astype(jnp.bfloat16)
    joined_grad = jnp.concatenate([grad_gate, grad_up], axis=2)
    joined_weight = jnp.concatenate([gate_weight, up_weight], axis=2)
    expert_back = jnp.einsum(
        "erh,edh->erd", joined_grad, joined_weight, preferred_element_type=jnp.float32
    )
    return expert_back.astype(jnp.bfloat16)


def combine_rows(returned, target_of, probs):
    token_count, top_count = probs.shape
    flat_back = returned.reshape(-1, returned.shape[2])
    picked = flat_back[target_of].reshape(token_count, top_count, returned.shape[2])
    return jnp.sum(picked.astype(jnp.float32) * probs[:, :, None], axis=1)


def on_device_routed(tokens, cotangent, expert_ids, probs, gate_weight, up_weight, down_weight):
    local_count = gate_weight.shape[0]
    device_count = lax.axis_size("expert")
    experts = local_count * device_count
    token_count, top_count = expert_ids.shape
    row_count = token_count * top_count
    capacity = row_count * 6 // (5 * experts)
    source_of, target_of = route_slots(expert_ids, local_count, device_count, capacity)
    send_rows = pack_rows(tokens, source_of, top_count, local_count)
    send_grads = pack_rows(cotangent, source_of, top_count, local_count)
    received = lax.all_to_all(send_rows, "expert", split_axis=1, concat_axis=1, tiled=True)
    expert_out, gate_pre, up_pre, sigmoid_gate = forward_part(
        received, gate_weight, up_weight, down_weight
    )
    returned_out = lax.all_to_all(expert_out, "expert", split_axis=1, concat_axis=1, tiled=True)
    received_grads = lax.all_to_all(send_grads, "expert", split_axis=1, concat_axis=1, tiled=True)
    expert_back = backward_part(
        received_grads, gate_pre, up_pre, sigmoid_gate, gate_weight, up_weight, down_weight
    )
    returned_back = lax.all_to_all(expert_back, "expert", split_axis=1, concat_axis=1, tiled=True)
    mixed = combine_rows(returned_out, target_of, probs)
    input_grad = combine_rows(returned_back, target_of, probs)
    return (mixed, input_grad)


def on_device(tokens, cotangent, expert_ids, probs, gate_weight, up_weight, down_weight):
    devices = lax.axis_size("expert")
    dense = devices % 4 == 0 and 12 <= devices <= 2 * expert_ids.shape[1]
    body = on_device_dense if dense else on_device_routed
    return body(tokens, cotangent, expert_ids, probs, gate_weight, up_weight, down_weight)


def solution(mesh):
    in_specs = (
        P(("dp", "expert"), None),
        P(("dp", "expert"), None),
        P(("dp", "expert"), None),
        P(("dp", "expert"), None),
        P(("dp", "expert"), None, None),
        P(("dp", "expert"), None, None),
        P(("dp", "expert"), None, None),
    )
    out_specs = (P(("dp", "expert"), None), P(("dp", "expert"), None))
    return jax.shard_map(
        on_device, mesh=mesh, in_specs=in_specs, out_specs=out_specs, check_vma=False
    )
```

```python
import functools

import jax
import jax.numpy as jnp
from jax import lax
from jax.experimental import pallas as pl
from jax.experimental.pallas import tpu as pltpu
from jax.sharding import PartitionSpec as P

VMEM_BYTES = 18 * 2**20
VMEM_BYTES_FETCH = 56 * 2**20
AT_ONCE = pl.CostEstimate(flops=1, bytes_accessed=1, transcendentals=0)


def resident(shape, index):
    return pl.BlockSpec(shape, index, pipeline_mode=pl.Buffered(1))


def compiler_params(vmem_bytes=VMEM_BYTES):
    return pltpu.CompilerParams(vmem_limit_bytes=vmem_bytes)


def fetch_rows(block_refs, buffer, sems):
    step = pl.program_id(0)
    count = len(block_refs) // pl.num_programs(0)

    @pl.when(step == 0)
    def _():
        for j, ref in enumerate(block_refs):
            pltpu.make_async_copy(ref, buffer.at[j], sems.at[j]).start()

    for j in range(len(block_refs)):

        @pl.when(step == j // count)
        def _(j=j):
            pltpu.make_async_copy(block_refs[j], buffer.at[j], sems.at[j]).wait()

    rows = buffer[pl.ds(step * count, count)]
    return rows.reshape(count * rows.shape[1], rows.shape[2])


def hidden_kernel(blocks, all_experts, owner_ref, gate_ref, up_ref, *refs):
    activ_ref, by_ref, buffer, sems = refs[blocks:]
    experts, width, hidden = gate_ref.shape
    rows = fetch_rows(refs[:blocks], buffer, sems)
    terms = rows[:, width:].astype(jnp.float32)
    rows = rows[:, :width]
    lanes = lax.broadcasted_iota(jnp.int32, terms.shape, 1)
    for e in range(experts):
        cut = slice(e * hidden, (e + 1) * hidden)
        cut_up = slice((experts + e) * hidden, (experts + e + 1) * hidden)
        label = owner_ref[0] * experts + e
        named = (lanes == label) | (lanes == label + all_experts) | (lanes == label + 2 * all_experts)
        weight = jnp.sum(jnp.where(named, terms, 0.0), axis=1, keepdims=True)
        gate_pre = jnp.dot(rows, gate_ref[e], preferred_element_type=jnp.float32)
        up_pre = jnp.dot(rows, up_ref[e], preferred_element_type=jnp.float32)
        sig = jax.nn.sigmoid(gate_pre)
        factor = sig * weight
        silu = gate_pre * factor
        activ_ref[:, cut] = (silu * up_pre).astype(jnp.bfloat16)
        by_ref[:, cut] = up_pre * factor * (1.0 + gate_pre * (1.0 - sig))
        by_ref[:, cut_up] = silu


def hidden_forward(row_blocks, owner, gate_weight, up_weight, all_experts):
    blocks = len(row_blocks)
    block, row_width = row_blocks[0].shape
    experts, width, hidden = gate_weight.shape
    count, columns, tile = blocks * block, experts * hidden, 2 * block
    weights = resident((experts, width, hidden), lambda i: (0, 0, 0))
    return pl.pallas_call(
        functools.partial(hidden_kernel, blocks, all_experts),
        grid=(blocks // 2,),
        in_specs=[pl.BlockSpec(memory_space=pltpu.SMEM), weights, weights]
        + [pl.BlockSpec(memory_space=pl.ANY)] * blocks,
        out_specs=[
            pl.BlockSpec((tile, columns), lambda i: (i, 0)),
            pl.BlockSpec((tile, 2 * columns), lambda i: (i, 0)),
        ],
        out_shape=[
            jax.ShapeDtypeStruct((count, columns), jnp.bfloat16),
            jax.ShapeDtypeStruct((count, 2 * columns), jnp.float32),
        ],
        scratch_shapes=[
            pltpu.VMEM((blocks, block, row_width), jnp.bfloat16),
            pltpu.SemaphoreType.DMA((blocks,)),
        ],
        compiler_params=compiler_params(VMEM_BYTES_FETCH),
        cost_estimate=AT_ONCE,
        name="hidden_forward",
    )(owner.reshape(1), gate_weight, up_weight, *row_blocks)


NT = (((1,), (1,)), ((), ()))


def grads_kernel(blocks, cuts, has_by, has_before, *refs):
    refs = list(refs)
    by_ref = refs.pop(0) if has_by else None
    before_ref = refs.pop(0) if has_before else None
    down_refs, block_refs = refs[: len(cuts)], refs[len(cuts) : len(cuts) + blocks]
    out_ref, buffer, sems = refs[len(cuts) + blocks :]
    rows = fetch_rows(block_refs, buffer, sems)
    total = before_ref[...] if has_before else None
    for (lo, hi), down_ref in zip(cuts, down_refs):
        term = lax.dot_general(rows[:, lo:hi], down_ref[...], NT, preferred_element_type=jnp.float32)
        total = term if total is None else total + term
    if has_by:
        columns = total.shape[1]
        out_ref[:, :columns] = (total * by_ref[:, :columns]).astype(jnp.bfloat16)
        out_ref[:, columns:] = (total * by_ref[:, columns:]).astype(jnp.bfloat16)
    else:
        out_ref[...] = total


def hidden_grads(grad_blocks, downs, cuts, by=None, before=None):
    blocks = len(grad_blocks)
    block, width = grad_blocks[0].shape
    columns = downs[0].shape[0]
    tile = 2 * block

    def rows(count):
        return pl.BlockSpec((tile, count), lambda i: (i, 0))

    given = [x for x in (by, before) if x is not None]
    out_columns, out_type = (columns, jnp.float32) if by is None else (2 * columns, jnp.bfloat16)
    return pl.pallas_call(
        functools.partial(grads_kernel, blocks, tuple(cuts), by is not None, before is not None),
        grid=(blocks // 2,),
        in_specs=[rows(x.shape[1]) for x in given]
        + [resident(d.shape, lambda i: (0, 0)) for d in downs]
        + [pl.BlockSpec(memory_space=pl.ANY)] * blocks,
        out_specs=rows(out_columns),
        out_shape=jax.ShapeDtypeStruct((blocks * block, out_columns), out_type),
        scratch_shapes=[
            pltpu.VMEM((blocks, block, width), jnp.bfloat16),
            pltpu.SemaphoreType.DMA((blocks,)),
        ],
        compiler_params=compiler_params(),
        cost_estimate=AT_ONCE,
        name="hidden_grads",
    )(*given, *downs, *grad_blocks)


def store_half(total, keep_ref, send_ref):
    @pl.when(pl.program_id(0) == 0)
    def _():
        send_ref[...] = total.astype(send_ref.dtype)

    @pl.when(pl.program_id(0) == 1)
    def _():
        keep_ref[...] = total


def mix_kernel(own_ref, other_ref, own_down_ref, other_down_ref, keep_ref, send_ref):
    total = jnp.dot(own_ref[...], own_down_ref[...], preferred_element_type=jnp.float32)
    total += jnp.dot(other_ref[...], other_down_ref[...], preferred_element_type=jnp.float32)
    store_half(total, keep_ref, send_ref)


def back_kernel(own_ref, other_ref, *refs):
    weight_refs, (keep_ref, send_ref) = refs[:-2], refs[-2:]
    experts, _, hidden = weight_refs[0].shape
    total = None
    for at, weight_ref in enumerate(weight_refs):
        grads_ref = (own_ref, other_ref)[at // 2]
        for e in range(experts):
            first = (at % 2 * experts + e) * hidden
            term = lax.dot_general(
                grads_ref[:, first : first + hidden], weight_ref[e], NT, preferred_element_type=jnp.float32
            )
            total = term if total is None else total + term
    store_half(total, keep_ref, send_ref)


def sum_columns(kernel, name, columns, own, other, weights, weight_specs):
    half, depth = own.shape[0] // 2, own.shape[1]
    rows = pl.BlockSpec((half, depth), lambda i: (1 - i, 0))
    return pl.pallas_call(
        kernel,
        grid=(2,),
        in_specs=[rows, rows] + weight_specs,
        out_specs=[pl.BlockSpec((half, columns), lambda i: (0, 0))] * 2,
        out_shape=[
            jax.ShapeDtypeStruct((half, columns), jnp.float32),
            jax.ShapeDtypeStruct((half, columns), jnp.bfloat16),
        ],
        compiler_params=compiler_params(),
        cost_estimate=AT_ONCE,
        name=name,
    )(own, other, *weights)


def mix_columns(own, other, own_down, other_down, at):
    depth, columns = other_down.shape
    specs = [
        resident((depth, columns), lambda i: (0, at)),
        resident((depth, columns), lambda i: (0, 0)),
    ]
    return sum_columns(mix_kernel, "mix_columns", columns, own, other, [own_down, other_down], specs)


def back_columns(own, other, weights, at, columns):
    experts, _, hidden = weights[0].shape
    specs = [resident((experts, columns, hidden), lambda i: (0, at, 0))] * len(weights)
    return sum_columns(back_kernel, "back_columns", columns, own, other, weights, specs)


def add_kernel(keep_ref, come_ref, *out_refs):
    block = out_refs[0].shape[0]
    for k, out_ref in enumerate(out_refs):
        cut = slice(k * block, (k + 1) * block)
        total = keep_ref[cut, :] + come_ref[cut, :].astype(jnp.float32)
        out_ref[...] = total.astype(out_ref.dtype)


def add_sides(keep, come, types):
    block, columns = keep.shape[0] // len(types), keep.shape[1]
    return pl.pallas_call(
        add_kernel,
        out_shape=[jax.ShapeDtypeStruct((block, columns), t) for t in types],
        compiler_params=compiler_params(),
        cost_estimate=AT_ONCE,
        name="add_sides",
    )(keep, come)


def add_piece(piece, come):
    return pl.pallas_call(
        add_kernel,
        out_shape=jax.ShapeDtypeStruct(piece.shape, jnp.bfloat16),
        compiler_params=compiler_params(),
        cost_estimate=AT_ONCE,
        name="add_piece",
    )(piece, come)


def finish_kernel(chunks, counts, *refs):
    out_ref = refs[-1]
    refs = list(refs[:-1])
    for (lo, hi), count in zip(chunks, counts):
        own_ref, *piece_refs = refs[:count]
        del refs[:count]
        total = own_ref[...]
        for piece_ref in piece_refs:
            total += piece_ref[...].astype(jnp.float32)
        out_ref[:, lo:hi] = total


def finish(chunks, parts, width):
    return pl.pallas_call(
        functools.partial(finish_kernel, tuple(chunks), tuple(map(len, parts))),
        out_shape=jax.ShapeDtypeStruct((parts[0][0].shape[0], width), jnp.float32),
        compiler_params=compiler_params(),
        cost_estimate=AT_ONCE,
        name="finish",
    )(*[p for part in parts for p in part])


def cut_columns(width, eighths):
    eighth = width // 8
    return [(lo * eighth, hi * eighth) for lo, hi in eighths]


def after(values, *others):
    return lax.optimization_barrier((values, *others))[0]


def send_all(sends, *waits):
    values, _ = lax.optimization_barrier(([v for v, _ in sends], waits))
    return [lax.ppermute(v, "expert", pairs) for v, (_, pairs) in zip(values, sends)]


def on_device_dense(tokens, cotangent, expert_ids, probs, gate_weight, up_weight, down_weight):
    local_count, hidden, width = down_weight.shape
    devices = lax.axis_size("expert")
    layers = devices // 4
    experts = local_count * devices
    block = tokens.shape[0]
    chunks = cut_columns(width, ((0, 4), (4, 8)))
    back_chunks = cut_columns(width, ((0, 4), (4, 6), (6, 8)))
    me = lax.axis_index("expert")
    twin = [(d, d ^ 1) for d in range(devices)]
    side = [(d, d ^ 2) for d in range(devices)]
    layer = [[(d, (d + 4 * k) % devices) for d in range(devices)] for k in range(layers)]

    labels = lax.broadcasted_iota(jnp.int32, (1, 1, experts), 2)
    weight = jnp.sum(jnp.where(expert_ids[:, :, None] == labels, probs[:, :, None], 0.0), axis=1)
    first = lax.reduce_precision(weight, 8, 7)
    second = lax.reduce_precision(weight - first, 8, 7)
    third = weight - first - second
    spare = jnp.zeros((block, -3 * experts % 128), jnp.bfloat16)
    terms = [t.astype(jnp.bfloat16) for t in (first, second, third)]
    row = jnp.concatenate([tokens] + terms + [spare], axis=1)
    grad = cotangent
    down = down_weight.reshape(local_count * hidden, width)
    downs = [down[:, lo:hi] for lo, hi in chunks]

    one, last, *middle = [1, layers - 1, *range(2, layers - 1)]
    rows, far_rows, grads, far_grads = {0: row}, {}, {0: grad}, {}
    other_gate, rows[one], far_rows[0] = send_all([(gate_weight, twin), (row, layer[-one]), (row, side)])
    rows[last], far_grads[0] = send_all([(row, layer[-last]), (grad, side)])
    (far_rows[one],) = send_all([(rows[one], side)], far_rows[0])
    for k in middle:
        (rows[k],) = send_all([(rows[k - 1], layer[-one])], far_rows[0])
    other_up, far_rows[last] = send_all([(up_weight, twin), (rows[last], side)], far_grads[0])
    got = send_all([(grad, layer[-one])] + [(rows[k], side) for k in middle], far_rows[one])
    grads[one] = got[0]
    far_rows.update(zip(middle, got[1:]))
    down_0, grads[last] = send_all([(downs[0], twin), (grad, layer[-last])], far_rows[last], other_gate)
    (far_grads[one],) = send_all([(grads[one], side)], *far_rows.values())
    for k in middle:
        (grads[k],) = send_all([(grads[k - 1], layer[-one])], *far_rows.values())
    (far_grads[last],) = send_all([(grads[last], side)], *far_rows.values())
    row_blocks = [rows[k] for k in range(layers)] + [far_rows[k] for k in range(layers)]
    activ, by = hidden_forward(row_blocks, me, gate_weight, up_weight, experts)
    for k in middle:
        (far_grads[k],) = send_all([(grads[k], side)], far_grads[one], activ)
    other_up = after(other_up, activ)
    other_activ, other_by = hidden_forward(row_blocks, me ^ 1, other_gate, other_up, experts)

    (down_1,) = send_all([(downs[1], twin)], down_0, activ, other_activ)

    def mix(c, other_down, *waits):
        lo, hi = chunks[c]
        return mix_columns(activ, other_activ, down, after(other_down, *waits), lo // (hi - lo))

    types = [jnp.float32, jnp.float32] + [jnp.bfloat16] * (layers - 2)

    def send_on(pieces, *waits):
        (far,) = send_all([(pieces[-1], layer[last])], *waits)
        come = None
        for k in reversed(middle):
            piece = pieces[k - 1] if come is None else add_piece(pieces[k - 1], come)
            (come,) = send_all([(piece, layer[one])], *waits)
        return far, come

    def send_last(pieces, come, *waits):
        piece = pieces[0].astype(jnp.bfloat16) if come is None else add_piece(pieces[0], come)
        return send_all([(piece, layer[one])], *waits)[0]

    keep_0, send = mix(0, down_0, other_activ, *far_grads.values())
    (come_0,) = send_all([(send, side)])
    grad_blocks = [grads[k] for k in range(layers)] + [far_grads[k] for k in range(layers)]
    own_grads = hidden_grads(grad_blocks, [down], [(0, width)], by=by)

    keep_1, send = mix(1, down_1, send)
    (come_1,) = send_all([(send, side)], own_grads)

    other_by = after(other_by, send)
    other_grads = hidden_grads(grad_blocks, [down_0, down_1], chunks, by=other_by)
    weights = [gate_weight, up_weight, other_gate, other_up]

    def back(c, *waits):
        lo, hi = back_chunks[c]
        return back_columns(own_grads, after(other_grads, *waits), weights, lo // (hi - lo), hi - lo)

    keep_2, send = back(0)
    own_0, *pieces = add_sides(after(keep_0, send), come_0, types)
    (come_2,) = send_all([(send, side)], own_0)
    far_0, next_0 = send_on(pieces)
    near_0 = send_last(pieces, next_0)

    keep_3, send = back(1, next_0, far_0)
    own_1, *pieces = add_sides(after(keep_1, send), come_1, types)
    (come_3,) = send_all([(send, side)], own_1)
    far_1, next_1 = send_on(pieces)
    near_1 = send_last(pieces, next_1, far_1, near_0)

    keep_4, send = back(2, next_1)
    own_2, *pieces = add_sides(after(keep_2, send), come_2, types)
    (come_4,) = send_all([(send, side)], own_2)
    far_2, next_2 = send_on(pieces)
    near_2 = send_last(pieces, next_2, far_2, near_1)
    mixed = finish(chunks, [(own_0, far_0, near_0), (own_1, far_1, near_1)], width)

    own_3, *pieces = add_sides(after(keep_3, mixed), come_3, types)
    far_3, next_3 = send_on(pieces)
    near_3 = send_last(pieces, next_3, far_3)

    types = [jnp.float32] + [jnp.bfloat16] * (layers - 1)
    own_4, *pieces = add_sides(keep_4, after(come_4, own_3), types)
    parts_4 = send_all([(piece, layer[k]) for k, piece in enumerate(pieces, 1)], near_2)
    back_parts = [(own_2, far_2, near_2), (own_3, far_3, near_3), (own_4, *parts_4)]
    return (mixed, finish(back_chunks, back_parts, width))


def route_slots(expert_ids, local_count, device_count, capacity):
    experts = local_count * device_count
    row_count = expert_ids.shape[0] * expert_ids.shape[1]
    flat_ids = expert_ids.reshape(row_count)
    sort_order = jnp.argsort(flat_ids, stable=True)
    labels = lax.broadcasted_iota(jnp.int32, (1, experts), 1)
    counts = jnp.sum((flat_ids[:, None] == labels).astype(jnp.int32), axis=0)
    starts = jnp.cumsum(counts) - counts
    sorted_ids = flat_ids[sort_order]
    rank_within = jnp.arange(row_count, dtype=jnp.int32) - starts[sorted_ids]
    owner = sorted_ids // local_count
    local_slot = sorted_ids % local_count
    target = local_slot * (device_count * capacity) + owner * capacity + rank_within
    source_of = jnp.full((experts * capacity,), row_count, jnp.int32).at[target].set(sort_order)
    target_of = jnp.zeros((row_count,), jnp.int32).at[sort_order].set(target)
    return (source_of, target_of)


def pack_rows(values, source_of, top_count, local_count):
    token_count = values.shape[0]
    with_zero = jnp.concatenate([values, jnp.zeros((1, values.shape[1]), values.dtype)], axis=0)
    token_index = jnp.minimum(source_of // top_count, token_count)
    picked = with_zero[token_index]
    return picked.reshape(local_count, -1, values.shape[1])


def forward_part(received, gate_weight, up_weight, down_weight):
    gate_pre = jnp.einsum("erd,edh->erh", received, gate_weight, preferred_element_type=jnp.float32)
    up_pre = jnp.einsum("erd,edh->erh", received, up_weight, preferred_element_type=jnp.float32)
    sigmoid_gate = jax.nn.sigmoid(gate_pre)
    activ = (gate_pre * sigmoid_gate * up_pre).astype(jnp.bfloat16)
    expert_out = jnp.einsum("erh,ehd->erd", activ, down_weight, preferred_element_type=jnp.float32)
    return (expert_out.astype(jnp.bfloat16), gate_pre, up_pre, sigmoid_gate)


def backward_part(grad_rows, gate_pre, up_pre, sigmoid_gate, gate_weight, up_weight, down_weight):
    grad_act = jnp.einsum(
        "erd,ehd->erh", grad_rows, down_weight, preferred_element_type=jnp.float32
    )
    grad_gate = (grad_act * up_pre * sigmoid_gate * (1.0 + gate_pre * (1.0 - sigmoid_gate))).astype(
        jnp.bfloat16
    )
    grad_up = (grad_act * gate_pre * sigmoid_gate).astype(jnp.bfloat16)
    joined_grad = jnp.concatenate([grad_gate, grad_up], axis=2)
    joined_weight = jnp.concatenate([gate_weight, up_weight], axis=2)
    expert_back = jnp.einsum(
        "erh,edh->erd", joined_grad, joined_weight, preferred_element_type=jnp.float32
    )
    return expert_back.astype(jnp.bfloat16)


def combine_rows(returned, target_of, probs):
    token_count, top_count = probs.shape
    flat_back = returned.reshape(-1, returned.shape[2])
    picked = flat_back[target_of].reshape(token_count, top_count, returned.shape[2])
    return jnp.sum(picked.astype(jnp.float32) * probs[:, :, None], axis=1)


def on_device_routed(tokens, cotangent, expert_ids, probs, gate_weight, up_weight, down_weight):
    local_count = gate_weight.shape[0]
    device_count = lax.axis_size("expert")
    experts = local_count * device_count
    token_count, top_count = expert_ids.shape
    row_count = token_count * top_count
    capacity = row_count * 6 // (5 * experts)
    source_of, target_of = route_slots(expert_ids, local_count, device_count, capacity)
    send_rows = pack_rows(tokens, source_of, top_count, local_count)
    send_grads = pack_rows(cotangent, source_of, top_count, local_count)
    received = lax.all_to_all(send_rows, "expert", split_axis=1, concat_axis=1, tiled=True)
    expert_out, gate_pre, up_pre, sigmoid_gate = forward_part(
        received, gate_weight, up_weight, down_weight
    )
    returned_out = lax.all_to_all(expert_out, "expert", split_axis=1, concat_axis=1, tiled=True)
    received_grads = lax.all_to_all(send_grads, "expert", split_axis=1, concat_axis=1, tiled=True)
    expert_back = backward_part(
        received_grads, gate_pre, up_pre, sigmoid_gate, gate_weight, up_weight, down_weight
    )
    returned_back = lax.all_to_all(expert_back, "expert", split_axis=1, concat_axis=1, tiled=True)
    mixed = combine_rows(returned_out, target_of, probs)
    input_grad = combine_rows(returned_back, target_of, probs)
    return (mixed, input_grad)


def on_device(tokens, cotangent, expert_ids, probs, gate_weight, up_weight, down_weight):
    devices = lax.axis_size("expert")
    dense = devices % 4 == 0 and 12 <= devices <= 2 * expert_ids.shape[1]
    body = on_device_dense if dense else on_device_routed
    return body(tokens, cotangent, expert_ids, probs, gate_weight, up_weight, down_weight)


def solution(mesh):
    in_specs = (
        P(("dp", "expert"), None),
        P(("dp", "expert"), None),
        P(("dp", "expert"), None),
        P(("dp", "expert"), None),
        P(("dp", "expert"), None, None),
        P(("dp", "expert"), None, None),
        P(("dp", "expert"), None, None),
    )
    out_specs = (P(("dp", "expert"), None), P(("dp", "expert"), None))
    return jax.shard_map(
        on_device, mesh=mesh, in_specs=in_specs, out_specs=out_specs, check_vma=False
    )
```

```python
import functools

import jax
import jax.numpy as jnp
from jax import lax
from jax.experimental import pallas as pl
from jax.experimental.pallas import tpu as pltpu
from jax.sharding import PartitionSpec as P

VMEM_BYTES = 18 * 2**20
VMEM_BYTES_FETCH = 56 * 2**20
AT_ONCE = pl.CostEstimate(flops=1, bytes_accessed=1, transcendentals=0)


def resident(shape, index):
    return pl.BlockSpec(shape, index, pipeline_mode=pl.Buffered(1))


def compiler_params(vmem_bytes=VMEM_BYTES):
    return pltpu.CompilerParams(vmem_limit_bytes=vmem_bytes)


def fetch_rows(block_refs, buffer, sems):
    step = pl.program_id(0)
    count = len(block_refs) // pl.num_programs(0)

    @pl.when(step == 0)
    def _():
        for j, ref in enumerate(block_refs):
            pltpu.make_async_copy(ref, buffer.at[j], sems.at[j]).start()

    for j in range(len(block_refs)):

        @pl.when(step == j // count)
        def _(j=j):
            pltpu.make_async_copy(block_refs[j], buffer.at[j], sems.at[j]).wait()

    rows = buffer[pl.ds(step * count, count)]
    return rows.reshape(count * rows.shape[1], rows.shape[2])


def hidden_kernel(blocks, all_experts, owner_ref, gate_ref, up_ref, *refs):
    activ_ref, by_ref, buffer, sems = refs[blocks:]
    experts, width, hidden = gate_ref.shape
    rows = fetch_rows(refs[:blocks], buffer, sems)
    terms = rows[:, width:].astype(jnp.float32)
    rows = rows[:, :width]
    lanes = lax.broadcasted_iota(jnp.int32, terms.shape, 1)
    for e in range(experts):
        cut = slice(e * hidden, (e + 1) * hidden)
        cut_up = slice((experts + e) * hidden, (experts + e + 1) * hidden)
        label = owner_ref[0] * experts + e
        named = (lanes == label) | (lanes == label + all_experts) | (lanes == label + 2 * all_experts)
        weight = jnp.sum(jnp.where(named, terms, 0.0), axis=1, keepdims=True)
        gate_pre = jnp.dot(rows, gate_ref[e], preferred_element_type=jnp.float32)
        up_pre = jnp.dot(rows, up_ref[e], preferred_element_type=jnp.float32)
        sig = jax.nn.sigmoid(gate_pre)
        factor = sig * weight
        silu = gate_pre * factor
        activ_ref[:, cut] = (silu * up_pre).astype(jnp.bfloat16)
        by_ref[:, cut] = up_pre * factor * (1.0 + gate_pre * (1.0 - sig))
        by_ref[:, cut_up] = silu


def hidden_forward(row_blocks, owner, gate_weight, up_weight, all_experts):
    blocks = len(row_blocks)
    block, row_width = row_blocks[0].shape
    experts, width, hidden = gate_weight.shape
    count, columns, tile = blocks * block, experts * hidden, 2 * block
    weights = resident((experts, width, hidden), lambda i: (0, 0, 0))
    return pl.pallas_call(
        functools.partial(hidden_kernel, blocks, all_experts),
        grid=(blocks // 2,),
        in_specs=[pl.BlockSpec(memory_space=pltpu.SMEM), weights, weights]
        + [pl.BlockSpec(memory_space=pl.ANY)] * blocks,
        out_specs=[
            pl.BlockSpec((tile, columns), lambda i: (i, 0)),
            pl.BlockSpec((tile, 2 * columns), lambda i: (i, 0)),
        ],
        out_shape=[
            jax.ShapeDtypeStruct((count, columns), jnp.bfloat16),
            jax.ShapeDtypeStruct((count, 2 * columns), jnp.float32),
        ],
        scratch_shapes=[
            pltpu.VMEM((blocks, block, row_width), jnp.bfloat16),
            pltpu.SemaphoreType.DMA((blocks,)),
        ],
        compiler_params=compiler_params(VMEM_BYTES_FETCH),
        cost_estimate=AT_ONCE,
        name="hidden_forward",
    )(owner.reshape(1), gate_weight, up_weight, *row_blocks)


NT = (((1,), (1,)), ((), ()))


def grads_kernel(blocks, cuts, has_by, has_before, *refs):
    refs = list(refs)
    by_ref = refs.pop(0) if has_by else None
    before_ref = refs.pop(0) if has_before else None
    down_refs, block_refs = refs[: len(cuts)], refs[len(cuts) : len(cuts) + blocks]
    out_ref, buffer, sems = refs[len(cuts) + blocks :]
    rows = fetch_rows(block_refs, buffer, sems)
    total = before_ref[...] if has_before else None
    for (lo, hi), down_ref in zip(cuts, down_refs):
        term = lax.dot_general(rows[:, lo:hi], down_ref[...], NT, preferred_element_type=jnp.float32)
        total = term if total is None else total + term
    if has_by:
        columns = total.shape[1]
        out_ref[:, :columns] = (total * by_ref[:, :columns]).astype(jnp.bfloat16)
        out_ref[:, columns:] = (total * by_ref[:, columns:]).astype(jnp.bfloat16)
    else:
        out_ref[...] = total


def hidden_grads(grad_blocks, downs, cuts, by=None, before=None):
    blocks = len(grad_blocks)
    block, width = grad_blocks[0].shape
    columns = downs[0].shape[0]
    tile = 2 * block

    def rows(count):
        return pl.BlockSpec((tile, count), lambda i: (i, 0))

    given = [x for x in (by, before) if x is not None]
    out_columns, out_type = (columns, jnp.float32) if by is None else (2 * columns, jnp.bfloat16)
    return pl.pallas_call(
        functools.partial(grads_kernel, blocks, tuple(cuts), by is not None, before is not None),
        grid=(blocks // 2,),
        in_specs=[rows(x.shape[1]) for x in given]
        + [resident(d.shape, lambda i: (0, 0)) for d in downs]
        + [pl.BlockSpec(memory_space=pl.ANY)] * blocks,
        out_specs=rows(out_columns),
        out_shape=jax.ShapeDtypeStruct((blocks * block, out_columns), out_type),
        scratch_shapes=[
            pltpu.VMEM((blocks, block, width), jnp.bfloat16),
            pltpu.SemaphoreType.DMA((blocks,)),
        ],
        compiler_params=compiler_params(),
        cost_estimate=AT_ONCE,
        name="hidden_grads",
    )(*given, *downs, *grad_blocks)


def store_half(total, keep_ref, send_ref):
    @pl.when(pl.program_id(0) == 0)
    def _():
        send_ref[...] = total.astype(send_ref.dtype)

    @pl.when(pl.program_id(0) == 1)
    def _():
        keep_ref[...] = total


def mix_kernel(own_ref, other_ref, own_down_ref, other_down_ref, keep_ref, send_ref):
    total = jnp.dot(own_ref[...], own_down_ref[...], preferred_element_type=jnp.float32)
    total += jnp.dot(other_ref[...], other_down_ref[...], preferred_element_type=jnp.float32)
    store_half(total, keep_ref, send_ref)


def back_kernel(own_ref, other_ref, *refs):
    weight_refs, (keep_ref, send_ref) = refs[:-2], refs[-2:]
    experts, _, hidden = weight_refs[0].shape
    total = None
    for at, weight_ref in enumerate(weight_refs):
        grads_ref = (own_ref, other_ref)[at // 2]
        for e in range(experts):
            first = (at % 2 * experts + e) * hidden
            term = lax.dot_general(
                grads_ref[:, first : first + hidden], weight_ref[e], NT, preferred_element_type=jnp.float32
            )
            total = term if total is None else total + term
    store_half(total, keep_ref, send_ref)


def sum_columns(kernel, name, columns, own, other, weights, weight_specs):
    half, depth = own.shape[0] // 2, own.shape[1]
    rows = pl.BlockSpec((half, depth), lambda i: (1 - i, 0))
    return pl.pallas_call(
        kernel,
        grid=(2,),
        in_specs=[rows, rows] + weight_specs,
        out_specs=[pl.BlockSpec((half, columns), lambda i: (0, 0))] * 2,
        out_shape=[
            jax.ShapeDtypeStruct((half, columns), jnp.float32),
            jax.ShapeDtypeStruct((half, columns), jnp.bfloat16),
        ],
        compiler_params=compiler_params(),
        cost_estimate=AT_ONCE,
        name=name,
    )(own, other, *weights)


def mix_columns(own, other, own_down, other_down, at):
    depth, columns = other_down.shape
    specs = [
        resident((depth, columns), lambda i: (0, at)),
        resident((depth, columns), lambda i: (0, 0)),
    ]
    return sum_columns(mix_kernel, "mix_columns", columns, own, other, [own_down, other_down], specs)


def back_columns(own, other, weights, at, columns):
    experts, _, hidden = weights[0].shape
    specs = [resident((experts, columns, hidden), lambda i: (0, at, 0))] * len(weights)
    return sum_columns(back_kernel, "back_columns", columns, own, other, weights, specs)


def add_kernel(keep_ref, come_ref, *out_refs):
    block = out_refs[0].shape[0]
    for k, out_ref in enumerate(out_refs):
        cut = slice(k * block, (k + 1) * block)
        total = keep_ref[cut, :] + come_ref[cut, :].astype(jnp.float32)
        out_ref[...] = total.astype(out_ref.dtype)


def add_sides(keep, come, types):
    block, columns = keep.shape[0] // len(types), keep.shape[1]
    return pl.pallas_call(
        add_kernel,
        out_shape=[jax.ShapeDtypeStruct((block, columns), t) for t in types],
        compiler_params=compiler_params(),
        cost_estimate=AT_ONCE,
        name="add_sides",
    )(keep, come)


def add_piece(piece, come):
    return pl.pallas_call(
        add_kernel,
        out_shape=jax.ShapeDtypeStruct(piece.shape, jnp.bfloat16),
        compiler_params=compiler_params(),
        cost_estimate=AT_ONCE,
        name="add_piece",
    )(piece, come)


def finish_kernel(chunks, counts, *refs):
    out_ref = refs[-1]
    refs = list(refs[:-1])
    for (lo, hi), count in zip(chunks, counts):
        own_ref, *piece_refs = refs[:count]
        del refs[:count]
        total = own_ref[...]
        for piece_ref in piece_refs:
            total += piece_ref[...].astype(jnp.float32)
        out_ref[:, lo:hi] = total


def finish(chunks, parts, width):
    return pl.pallas_call(
        functools.partial(finish_kernel, tuple(chunks), tuple(map(len, parts))),
        out_shape=jax.ShapeDtypeStruct((parts[0][0].shape[0], width), jnp.float32),
        compiler_params=compiler_params(),
        cost_estimate=AT_ONCE,
        name="finish",
    )(*[p for part in parts for p in part])


def cut_columns(width, eighths):
    eighth = width // 8
    return [(lo * eighth, hi * eighth) for lo, hi in eighths]


def after(values, *others):
    return lax.optimization_barrier((values, *others))[0]


def send_all(sends, *waits):
    values, _ = lax.optimization_barrier(([v for v, _ in sends], waits))
    return [lax.ppermute(v, "expert", pairs) for v, (_, pairs) in zip(values, sends)]


def on_device_dense(tokens, cotangent, expert_ids, probs, gate_weight, up_weight, down_weight):
    local_count, hidden, width = down_weight.shape
    devices = lax.axis_size("expert")
    layers = devices // 4
    experts = local_count * devices
    block = tokens.shape[0]
    chunks = cut_columns(width, ((6, 8), (0, 3), (3, 6)))
    back_chunks = cut_columns(width, ((0, 3), (3, 6), (6, 8)))
    me = lax.axis_index("expert")
    twin = [(d, d ^ 1) for d in range(devices)]
    side = [(d, d ^ 2) for d in range(devices)]
    layer = [[(d, (d + 4 * k) % devices) for d in range(devices)] for k in range(layers)]

    labels = lax.broadcasted_iota(jnp.int32, (1, 1, experts), 2)
    weight = jnp.sum(jnp.where(expert_ids[:, :, None] == labels, probs[:, :, None], 0.0), axis=1)
    first = lax.reduce_precision(weight, 8, 7)
    second = lax.reduce_precision(weight - first, 8, 7)
    third = weight - first - second
    spare = jnp.zeros((block, -3 * experts % 128), jnp.bfloat16)
    terms = [t.astype(jnp.bfloat16) for t in (first, second, third)]
    row = jnp.concatenate([tokens] + terms + [spare], axis=1)
    grad = cotangent
    down = down_weight.reshape(local_count * hidden, width)
    downs = [down[:, lo:hi] for lo, hi in chunks]

    one, last, *middle = [1, layers - 1, *range(2, layers - 1)]
    rows, far_rows, grads, far_grads = {0: row}, {}, {0: grad}, {}
    other_gate, rows[one], far_rows[0] = send_all([(gate_weight, twin), (row, layer[-one]), (row, side)])
    rows[last], far_grads[0] = send_all([(row, layer[-last]), (grad, side)])
    (far_rows[one],) = send_all([(rows[one], side)], far_rows[0])
    for k in middle:
        (rows[k],) = send_all([(rows[k - 1], layer[-one])], far_rows[0])
    other_up, far_rows[last] = send_all([(up_weight, twin), (rows[last], side)], far_grads[0])
    got = send_all([(grad, layer[-one])] + [(rows[k], side) for k in middle], far_rows[one])
    grads[one] = got[0]
    far_rows.update(zip(middle, got[1:]))
    down_0, grads[last] = send_all([(downs[0], twin), (grad, layer[-last])], far_rows[last], other_gate)
    (far_grads[one],) = send_all([(grads[one], side)], *far_rows.values())
    for k in middle:
        (grads[k],) = send_all([(grads[k - 1], layer[-one])], *far_rows.values())
    (far_grads[last],) = send_all([(grads[last], side)], *far_rows.values())
    row_blocks = [rows[k] for k in range(layers)] + [far_rows[k] for k in range(layers)]
    activ, by = hidden_forward(row_blocks, me, gate_weight, up_weight, experts)
    for k in middle:
        (far_grads[k],) = send_all([(grads[k], side)], far_grads[one], activ)
    other_up = after(other_up, activ)
    other_activ, other_by = hidden_forward(row_blocks, me ^ 1, other_gate, other_up, experts)

    (down_1,) = send_all([(downs[1], twin)], down_0, activ, other_activ)

    def mix(c, other_down, *waits):
        lo, hi = chunks[c]
        return mix_columns(activ, other_activ, down, after(other_down, *waits), lo // (hi - lo))

    types = [jnp.float32, jnp.float32] + [jnp.bfloat16] * (layers - 2)

    def send_on(pieces, *waits):
        (far,) = send_all([(pieces[-1], layer[last])], *waits)
        come = None
        for k in reversed(middle):
            piece = pieces[k - 1] if come is None else add_piece(pieces[k - 1], come)
            (come,) = send_all([(piece, layer[one])], *waits)
        return far, come

    def send_last(pieces, come, *waits):
        piece = pieces[0].astype(jnp.bfloat16) if come is None else add_piece(pieces[0], come)
        return send_all([(piece, layer[one])], *waits)[0]

    keep_0, send = mix(0, down_0, other_activ, *far_grads.values())
    come_0, down_2 = send_all([(send, side), (downs[2], twin)])
    grad_blocks = [grads[k] for k in range(layers)] + [far_grads[k] for k in range(layers)]
    own_grads = hidden_grads(grad_blocks, [down], [(0, width)], by=by)

    keep_1, send = mix(1, down_1, send, own_grads)
    own_0, *pieces = add_sides(keep_0, come_0, types)
    (come_1,) = send_all([(send, side)])
    far_0, next_0 = send_on(pieces)
    near_0 = send_last(pieces, next_0, far_0)
    grad_blocks = [after(grad_blocks[0], next_0), *grad_blocks[1:]]
    other_grad = hidden_grads(grad_blocks, [down_0, down_1], chunks[:2])

    keep_2, send = mix(2, down_2, other_grad, near_0)
    (come_2,) = send_all([(send, side)], own_0)

    other_by = after(other_by, send)
    other_grads = hidden_grads(grad_blocks, [down_2], chunks[2:], by=other_by, before=other_grad)
    weights = [gate_weight, up_weight, other_gate, other_up]

    def back(c, *waits):
        lo, hi = back_chunks[c]
        return back_columns(own_grads, after(other_grads, *waits), weights, lo // (hi - lo), hi - lo)

    keep_3, send = back(0)
    own_1, *pieces = add_sides(after(keep_1, send), come_1, types)
    (come_3,) = send_all([(send, side)], own_1)
    far_1, next_1 = send_on(pieces)
    near_1 = send_last(pieces, next_1, far_1)

    keep_4, send = back(1, next_1, far_1)
    own_2, *pieces = add_sides(after(keep_2, send), come_2, types)
    (come_4,) = send_all([(send, side)], own_2)
    far_2, next_2 = send_on(pieces)
    near_2 = send_last(pieces, next_2, far_2, near_1)

    keep_5, send = back(2, next_2)
    own_3, *pieces = add_sides(after(keep_3, send), come_3, types)
    (come_5,) = send_all([(send, side)], own_3)
    far_3, next_3 = send_on(pieces)
    near_3 = send_last(pieces, next_3, far_3, near_2)
    mixed = finish(chunks, [(own_0, far_0, near_0), (own_1, far_1, near_1), (own_2, far_2, near_2)], width)

    own_4, *pieces = add_sides(after(keep_4, mixed), after(come_4, next_3), types)
    far_4, next_4 = send_on(pieces)
    near_4 = send_last(pieces, next_4, far_4)

    types = [jnp.float32] + [jnp.bfloat16] * (layers - 1)
    own_5, *pieces = add_sides(keep_5, after(come_5, own_4), types)
    parts_5 = send_all([(piece, layer[k]) for k, piece in enumerate(pieces, 1)], near_3)
    back_parts = [(own_3, far_3, near_3), (own_4, far_4, near_4), (own_5, *parts_5)]
    return (mixed, finish(back_chunks, back_parts, width))


def route_slots(expert_ids, local_count, device_count, capacity):
    experts = local_count * device_count
    row_count = expert_ids.shape[0] * expert_ids.shape[1]
    flat_ids = expert_ids.reshape(row_count)
    sort_order = jnp.argsort(flat_ids, stable=True)
    labels = lax.broadcasted_iota(jnp.int32, (1, experts), 1)
    counts = jnp.sum((flat_ids[:, None] == labels).astype(jnp.int32), axis=0)
    starts = jnp.cumsum(counts) - counts
    sorted_ids = flat_ids[sort_order]
    rank_within = jnp.arange(row_count, dtype=jnp.int32) - starts[sorted_ids]
    owner = sorted_ids // local_count
    local_slot = sorted_ids % local_count
    target = local_slot * (device_count * capacity) + owner * capacity + rank_within
    source_of = jnp.full((experts * capacity,), row_count, jnp.int32).at[target].set(sort_order)
    target_of = jnp.zeros((row_count,), jnp.int32).at[sort_order].set(target)
    return (source_of, target_of)


def pack_rows(values, source_of, top_count, local_count):
    token_count = values.shape[0]
    with_zero = jnp.concatenate([values, jnp.zeros((1, values.shape[1]), values.dtype)], axis=0)
    token_index = jnp.minimum(source_of // top_count, token_count)
    picked = with_zero[token_index]
    return picked.reshape(local_count, -1, values.shape[1])


def forward_part(received, gate_weight, up_weight, down_weight):
    gate_pre = jnp.einsum("erd,edh->erh", received, gate_weight, preferred_element_type=jnp.float32)
    up_pre = jnp.einsum("erd,edh->erh", received, up_weight, preferred_element_type=jnp.float32)
    sigmoid_gate = jax.nn.sigmoid(gate_pre)
    activ = (gate_pre * sigmoid_gate * up_pre).astype(jnp.bfloat16)
    expert_out = jnp.einsum("erh,ehd->erd", activ, down_weight, preferred_element_type=jnp.float32)
    return (expert_out.astype(jnp.bfloat16), gate_pre, up_pre, sigmoid_gate)


def backward_part(grad_rows, gate_pre, up_pre, sigmoid_gate, gate_weight, up_weight, down_weight):
    grad_act = jnp.einsum(
        "erd,ehd->erh", grad_rows, down_weight, preferred_element_type=jnp.float32
    )
    grad_gate = (grad_act * up_pre * sigmoid_gate * (1.0 + gate_pre * (1.0 - sigmoid_gate))).astype(
        jnp.bfloat16
    )
    grad_up = (grad_act * gate_pre * sigmoid_gate).astype(jnp.bfloat16)
    joined_grad = jnp.concatenate([grad_gate, grad_up], axis=2)
    joined_weight = jnp.concatenate([gate_weight, up_weight], axis=2)
    expert_back = jnp.einsum(
        "erh,edh->erd", joined_grad, joined_weight, preferred_element_type=jnp.float32
    )
    return expert_back.astype(jnp.bfloat16)


def combine_rows(returned, target_of, probs):
    token_count, top_count = probs.shape
    flat_back = returned.reshape(-1, returned.shape[2])
    picked = flat_back[target_of].reshape(token_count, top_count, returned.shape[2])
    return jnp.sum(picked.astype(jnp.float32) * probs[:, :, None], axis=1)


def on_device_routed(tokens, cotangent, expert_ids, probs, gate_weight, up_weight, down_weight):
    local_count = gate_weight.shape[0]
    device_count = lax.axis_size("expert")
    experts = local_count * device_count
    token_count, top_count = expert_ids.shape
    row_count = token_count * top_count
    capacity = row_count * 6 // (5 * experts)
    source_of, target_of = route_slots(expert_ids, local_count, device_count, capacity)
    send_rows = pack_rows(tokens, source_of, top_count, local_count)
    send_grads = pack_rows(cotangent, source_of, top_count, local_count)
    received = lax.all_to_all(send_rows, "expert", split_axis=1, concat_axis=1, tiled=True)
    expert_out, gate_pre, up_pre, sigmoid_gate = forward_part(
        received, gate_weight, up_weight, down_weight
    )
    returned_out = lax.all_to_all(expert_out, "expert", split_axis=1, concat_axis=1, tiled=True)
    received_grads = lax.all_to_all(send_grads, "expert", split_axis=1, concat_axis=1, tiled=True)
    expert_back = backward_part(
        received_grads, gate_pre, up_pre, sigmoid_gate, gate_weight, up_weight, down_weight
    )
    returned_back = lax.all_to_all(expert_back, "expert", split_axis=1, concat_axis=1, tiled=True)
    mixed = combine_rows(returned_out, target_of, probs)
    input_grad = combine_rows(returned_back, target_of, probs)
    return (mixed, input_grad)


def on_device(tokens, cotangent, expert_ids, probs, gate_weight, up_weight, down_weight):
    devices = lax.axis_size("expert")
    dense = devices % 4 == 0 and 12 <= devices <= 2 * expert_ids.shape[1]
    body = on_device_dense if dense else on_device_routed
    return body(tokens, cotangent, expert_ids, probs, gate_weight, up_weight, down_weight)


def solution(mesh):
    in_specs = (
        P(("dp", "expert"), None),
        P(("dp", "expert"), None),
        P(("dp", "expert"), None),
        P(("dp", "expert"), None),
        P(("dp", "expert"), None, None),
        P(("dp", "expert"), None, None),
        P(("dp", "expert"), None, None),
    )
    out_specs = (P(("dp", "expert"), None), P(("dp", "expert"), None))
    return jax.shard_map(
        on_device, mesh=mesh, in_specs=in_specs, out_specs=out_specs, check_vma=False
    )
```

```python
import functools

import jax
import jax.numpy as jnp
from jax import lax
from jax.experimental import pallas as pl
from jax.experimental.pallas import tpu as pltpu
from jax.sharding import PartitionSpec as P

VMEM_BYTES = 18 * 2**20
VMEM_BYTES_FETCH = 56 * 2**20
AT_ONCE = pl.CostEstimate(flops=1, bytes_accessed=1, transcendentals=0)


def resident(shape, index):
    return pl.BlockSpec(shape, index, pipeline_mode=pl.Buffered(1))


def compiler_params(vmem_bytes=VMEM_BYTES):
    return pltpu.CompilerParams(vmem_limit_bytes=vmem_bytes)


def fetch_rows(block_refs, buffer, sems):
    step = pl.program_id(0)
    count = len(block_refs) // pl.num_programs(0)

    @pl.when(step == 0)
    def _():
        for j, ref in enumerate(block_refs):
            pltpu.make_async_copy(ref, buffer.at[j], sems.at[j]).start()

    for j in range(len(block_refs)):

        @pl.when(step == j // count)
        def _(j=j):
            pltpu.make_async_copy(block_refs[j], buffer.at[j], sems.at[j]).wait()

    rows = buffer[pl.ds(step * count, count)]
    return rows.reshape(count * rows.shape[1], rows.shape[2])


def hidden_kernel(blocks, all_experts, owner_ref, gate_ref, up_ref, *refs):
    activ_ref, by_ref, buffer, sems = refs[blocks:]
    experts, width, hidden = gate_ref.shape
    rows = fetch_rows(refs[:blocks], buffer, sems)
    terms = rows[:, width:].astype(jnp.float32)
    rows = rows[:, :width]
    lanes = lax.broadcasted_iota(jnp.int32, terms.shape, 1)
    for e in range(experts):
        cut = slice(e * hidden, (e + 1) * hidden)
        cut_up = slice((experts + e) * hidden, (experts + e + 1) * hidden)
        label = owner_ref[0] * experts + e
        named = (lanes == label) | (lanes == label + all_experts) | (lanes == label + 2 * all_experts)
        weight = jnp.sum(jnp.where(named, terms, 0.0), axis=1, keepdims=True)
        gate_pre = jnp.dot(rows, gate_ref[e], preferred_element_type=jnp.float32)
        up_pre = jnp.dot(rows, up_ref[e], preferred_element_type=jnp.float32)
        sig = jax.nn.sigmoid(gate_pre)
        factor = sig * weight
        silu = gate_pre * factor
        activ_ref[:, cut] = (silu * up_pre).astype(jnp.bfloat16)
        by_ref[:, cut] = up_pre * factor * (1.0 + gate_pre * (1.0 - sig))
        by_ref[:, cut_up] = silu


def hidden_forward(row_blocks, owner, gate_weight, up_weight, all_experts):
    blocks = len(row_blocks)
    block, row_width = row_blocks[0].shape
    experts, width, hidden = gate_weight.shape
    count, columns, tile = blocks * block, experts * hidden, blocks // 2 * block
    weights = resident((experts, width, hidden), lambda i: (0, 0, 0))
    return pl.pallas_call(
        functools.partial(hidden_kernel, blocks, all_experts),
        grid=(2,),
        in_specs=[pl.BlockSpec(memory_space=pltpu.SMEM), weights, weights]
        + [pl.BlockSpec(memory_space=pl.ANY)] * blocks,
        out_specs=[
            pl.BlockSpec((tile, columns), lambda i: (i, 0)),
            pl.BlockSpec((tile, 2 * columns), lambda i: (i, 0)),
        ],
        out_shape=[
            jax.ShapeDtypeStruct((count, columns), jnp.bfloat16),
            jax.ShapeDtypeStruct((count, 2 * columns), jnp.float32),
        ],
        scratch_shapes=[
            pltpu.VMEM((blocks, block, row_width), jnp.bfloat16),
            pltpu.SemaphoreType.DMA((blocks,)),
        ],
        compiler_params=compiler_params(VMEM_BYTES_FETCH),
        cost_estimate=AT_ONCE,
        name="hidden_forward",
    )(owner.reshape(1), gate_weight, up_weight, *row_blocks)


NT = (((1,), (1,)), ((), ()))


def grads_kernel(blocks, cuts, has_by, has_before, *refs):
    refs = list(refs)
    by_ref = refs.pop(0) if has_by else None
    before_ref = refs.pop(0) if has_before else None
    down_refs, block_refs = refs[: len(cuts)], refs[len(cuts) : len(cuts) + blocks]
    out_ref, buffer, sems = refs[len(cuts) + blocks :]
    rows = fetch_rows(block_refs, buffer, sems)
    total = before_ref[...] if has_before else None
    for (lo, hi), down_ref in zip(cuts, down_refs):
        term = lax.dot_general(rows[:, lo:hi], down_ref[...], NT, preferred_element_type=jnp.float32)
        total = term if total is None else total + term
    if has_by:
        columns = total.shape[1]
        out_ref[:, :columns] = (total * by_ref[:, :columns]).astype(jnp.bfloat16)
        out_ref[:, columns:] = (total * by_ref[:, columns:]).astype(jnp.bfloat16)
    else:
        out_ref[...] = total


def hidden_grads(grad_blocks, downs, cuts, by=None, before=None):
    blocks = len(grad_blocks)
    block, width = grad_blocks[0].shape
    columns = downs[0].shape[0]
    tile = blocks // 2 * block

    def rows(count):
        return pl.BlockSpec((tile, count), lambda i: (i, 0))

    given = [x for x in (by, before) if x is not None]
    out_columns, out_type = (columns, jnp.float32) if by is None else (2 * columns, jnp.bfloat16)
    return pl.pallas_call(
        functools.partial(grads_kernel, blocks, tuple(cuts), by is not None, before is not None),
        grid=(2,),
        in_specs=[rows(x.shape[1]) for x in given]
        + [resident(d.shape, lambda i: (0, 0)) for d in downs]
        + [pl.BlockSpec(memory_space=pl.ANY)] * blocks,
        out_specs=rows(out_columns),
        out_shape=jax.ShapeDtypeStruct((blocks * block, out_columns), out_type),
        scratch_shapes=[
            pltpu.VMEM((blocks, block, width), jnp.bfloat16),
            pltpu.SemaphoreType.DMA((blocks,)),
        ],
        compiler_params=compiler_params(),
        cost_estimate=AT_ONCE,
        name="hidden_grads",
    )(*given, *downs, *grad_blocks)


def store_half(total, keep_ref, send_ref):
    @pl.when(pl.program_id(0) == 0)
    def _():
        send_ref[...] = total.astype(send_ref.dtype)

    @pl.when(pl.program_id(0) == 1)
    def _():
        keep_ref[...] = total


def mix_kernel(own_ref, other_ref, own_down_ref, other_down_ref, keep_ref, send_ref):
    total = jnp.dot(own_ref[...], own_down_ref[...], preferred_element_type=jnp.float32)
    total += jnp.dot(other_ref[...], other_down_ref[...], preferred_element_type=jnp.float32)
    store_half(total, keep_ref, send_ref)


def back_kernel(own_ref, other_ref, *refs):
    weight_refs, (keep_ref, send_ref) = refs[:-2], refs[-2:]
    experts, _, hidden = weight_refs[0].shape
    total = None
    for at, weight_ref in enumerate(weight_refs):
        grads_ref = (own_ref, other_ref)[at // 2]
        for e in range(experts):
            first = (at % 2 * experts + e) * hidden
            term = lax.dot_general(
                grads_ref[:, first : first + hidden], weight_ref[e], NT, preferred_element_type=jnp.float32
            )
            total = term if total is None else total + term
    store_half(total, keep_ref, send_ref)


def sum_columns(kernel, name, columns, own, other, weights, weight_specs):
    half, depth = own.shape[0] // 2, own.shape[1]
    rows = pl.BlockSpec((half, depth), lambda i: (1 - i, 0))
    return pl.pallas_call(
        kernel,
        grid=(2,),
        in_specs=[rows, rows] + weight_specs,
        out_specs=[pl.BlockSpec((half, columns), lambda i: (0, 0))] * 2,
        out_shape=[
            jax.ShapeDtypeStruct((half, columns), jnp.float32),
            jax.ShapeDtypeStruct((half, columns), jnp.bfloat16),
        ],
        compiler_params=compiler_params(),
        cost_estimate=AT_ONCE,
        name=name,
    )(own, other, *weights)


def mix_columns(own, other, own_down, other_down, at):
    depth, columns = other_down.shape
    specs = [
        resident((depth, columns), lambda i: (0, at)),
        resident((depth, columns), lambda i: (0, 0)),
    ]
    return sum_columns(mix_kernel, "mix_columns", columns, own, other, [own_down, other_down], specs)


def back_columns(own, other, weights, at, columns):
    experts, _, hidden = weights[0].shape
    specs = [resident((experts, columns, hidden), lambda i: (0, at, 0))] * len(weights)
    return sum_columns(back_kernel, "back_columns", columns, own, other, weights, specs)


def add_kernel(keep_ref, come_ref, *out_refs):
    block = out_refs[0].shape[0]
    for k, out_ref in enumerate(out_refs):
        cut = slice(k * block, (k + 1) * block)
        total = keep_ref[cut, :] + come_ref[cut, :].astype(jnp.float32)
        out_ref[...] = total.astype(out_ref.dtype)


def add_sides(keep, come, types):
    block, columns = keep.shape[0] // len(types), keep.shape[1]
    return pl.pallas_call(
        add_kernel,
        out_shape=[jax.ShapeDtypeStruct((block, columns), t) for t in types],
        compiler_params=compiler_params(),
        cost_estimate=AT_ONCE,
        name="add_sides",
    )(keep, come)


def add_piece(piece, come):
    return pl.pallas_call(
        add_kernel,
        out_shape=jax.ShapeDtypeStruct(piece.shape, jnp.bfloat16),
        compiler_params=compiler_params(),
        cost_estimate=AT_ONCE,
        name="add_piece",
    )(piece, come)


def finish_kernel(chunks, counts, *refs):
    out_ref = refs[-1]
    refs = list(refs[:-1])
    for (lo, hi), count in zip(chunks, counts):
        own_ref, *piece_refs = refs[:count]
        del refs[:count]
        total = own_ref[...]
        for piece_ref in piece_refs:
            total += piece_ref[...].astype(jnp.float32)
        out_ref[:, lo:hi] = total


def finish(chunks, parts, width):
    return pl.pallas_call(
        functools.partial(finish_kernel, tuple(chunks), tuple(map(len, parts))),
        out_shape=jax.ShapeDtypeStruct((parts[0][0].shape[0], width), jnp.float32),
        compiler_params=compiler_params(),
        cost_estimate=AT_ONCE,
        name="finish",
    )(*[p for part in parts for p in part])


def cut_columns(width, eighths):
    eighth = width // 8
    return [(lo * eighth, hi * eighth) for lo, hi in eighths]


def after(values, *others):
    return lax.optimization_barrier((values, *others))[0]


def send_all(sends, *waits):
    values, _ = lax.optimization_barrier(([v for v, _ in sends], waits))
    return [lax.ppermute(v, "expert", pairs) for v, (_, pairs) in zip(values, sends)]


def on_device_dense(tokens, cotangent, expert_ids, probs, gate_weight, up_weight, down_weight):
    local_count, hidden, width = down_weight.shape
    devices = lax.axis_size("expert")
    layers = devices // 4
    experts = local_count * devices
    block = tokens.shape[0]
    chunks = cut_columns(width, ((6, 8), (0, 3), (3, 6)))
    back_chunks = cut_columns(width, ((0, 3), (3, 6), (6, 8)))
    me = lax.axis_index("expert")
    twin = [(d, d ^ 1) for d in range(devices)]
    side = [(d, d ^ 2) for d in range(devices)]
    layer = [[(d, (d + 4 * k) % devices) for d in range(devices)] for k in range(layers)]

    labels = lax.broadcasted_iota(jnp.int32, (1, 1, experts), 2)
    weight = jnp.sum(jnp.where(expert_ids[:, :, None] == labels, probs[:, :, None], 0.0), axis=1)
    first = lax.reduce_precision(weight, 8, 7)
    second = lax.reduce_precision(weight - first, 8, 7)
    third = weight - first - second
    spare = jnp.zeros((block, -3 * experts % 128), jnp.bfloat16)
    terms = [t.astype(jnp.bfloat16) for t in (first, second, third)]
    row = jnp.concatenate([tokens] + terms + [spare], axis=1)
    grad = cotangent
    down = down_weight.reshape(local_count * hidden, width)
    downs = [down[:, lo:hi] for lo, hi in chunks]

    one, last, *middle = [1, layers - 1, *range(2, layers - 1)]
    rows, far_rows, grads, far_grads = {0: row}, {}, {0: grad}, {}
    other_gate, rows[one], far_rows[0] = send_all([(gate_weight, twin), (row, layer[-one]), (row, side)])
    rows[last], far_grads[0] = send_all([(row, layer[-last]), (grad, side)])
    (far_rows[one],) = send_all([(rows[one], side)], far_rows[0])
    for k in middle:
        (rows[k],) = send_all([(rows[k - 1], layer[-one])], far_rows[0])
    other_up, far_rows[last] = send_all([(up_weight, twin), (rows[last], side)], far_grads[0])
    got = send_all([(grad, layer[-one])] + [(rows[k], side) for k in middle], far_rows[one])
    grads[one] = got[0]
    far_rows.update(zip(middle, got[1:]))
    down_0, grads[last] = send_all([(downs[0], twin), (grad, layer[-last])], far_rows[last], other_gate)
    (far_grads[one],) = send_all([(grads[one], side)], *far_rows.values())
    for k in middle:
        (grads[k],) = send_all([(grads[k - 1], layer[-one])], *far_rows.values())
    (far_grads[last],) = send_all([(grads[last], side)], *far_rows.values())
    row_blocks = [rows[k] for k in range(layers)] + [far_rows[k] for k in range(layers)]
    activ, by = hidden_forward(row_blocks, me, gate_weight, up_weight, experts)
    for k in middle:
        (far_grads[k],) = send_all([(grads[k], side)], far_grads[one], activ)
    other_up = after(other_up, activ)
    other_activ, other_by = hidden_forward(row_blocks, me ^ 1, other_gate, other_up, experts)

    (down_1,) = send_all([(downs[1], twin)], down_0, activ, other_activ)

    def mix(c, other_down, *waits):
        return mix_columns(activ, other_activ, downs[c], after(other_down, *waits), 0)

    types = [jnp.float32, jnp.float32] + [jnp.bfloat16] * (layers - 2)

    def send_on(pieces, *waits):
        (far,) = send_all([(pieces[-1], layer[last])], *waits)
        come = None
        for k in reversed(middle):
            piece = pieces[k - 1] if come is None else add_piece(pieces[k - 1], come)
            (come,) = send_all([(piece, layer[one])], *waits)
        return far, come

    def send_last(pieces, come, *waits):
        piece = pieces[0].astype(jnp.bfloat16) if come is None else add_piece(pieces[0], come)
        return send_all([(piece, layer[one])], *waits)[0]

    keep_0, send = mix(0, down_0, other_activ, *far_grads.values())
    come_0, down_2 = send_all([(send, side), (downs[2], twin)])
    grad_blocks = [grads[k] for k in range(layers)] + [far_grads[k] for k in range(layers)]
    own_grads = hidden_grads(grad_blocks, [down], [(0, width)], by=by)

    keep_1, send = mix(1, down_1, send, own_grads)
    own_0, *pieces = add_sides(after(keep_0, send), come_0, types)
    (come_1,) = send_all([(send, side)])
    far_0, next_0 = send_on(pieces)
    near_0 = send_last(pieces, next_0, far_0)
    grad_blocks = [after(grad_blocks[0], next_0), *grad_blocks[1:]]
    other_grad = hidden_grads(grad_blocks, [down_0, down_1], chunks[:2])

    keep_2, send = mix(2, down_2, other_grad, near_0)
    (come_2,) = send_all([(send, side)], own_0)

    other_by = after(other_by, send)
    other_grads = hidden_grads(grad_blocks, [down_2], chunks[2:], by=other_by, before=other_grad)
    weights = [gate_weight, up_weight, other_gate, other_up]

    def back(c, *waits):
        lo, hi = back_chunks[c]
        return back_columns(own_grads, after(other_grads, *waits), weights, lo // (hi - lo), hi - lo)

    keep_3, send = back(0)
    own_1, *pieces = add_sides(after(keep_1, send), come_1, types)
    (come_3,) = send_all([(send, side)], own_1)
    far_1, next_1 = send_on(pieces)
    near_1 = send_last(pieces, next_1, far_1)

    keep_4, send = back(1, next_1, far_1)
    own_2, *pieces = add_sides(after(keep_2, send), come_2, types)
    (come_4,) = send_all([(send, side)], own_2)
    far_2, next_2 = send_on(pieces)
    near_2 = send_last(pieces, next_2, far_2, near_1)

    keep_5, send = back(2, next_2)
    own_3, *pieces = add_sides(after(keep_3, send), come_3, types)
    (come_5,) = send_all([(send, side)], own_3)
    far_3, next_3 = send_on(pieces)
    near_3 = send_last(pieces, next_3, far_3, near_2)
    mixed = finish(chunks, [(own_0, far_0, near_0), (own_1, far_1, near_1), (own_2, far_2, near_2)], width)

    own_4, *pieces = add_sides(after(keep_4, mixed), after(come_4, near_3), types)
    far_4, next_4 = send_on(pieces)
    near_4 = send_last(pieces, next_4, far_4)

    types = [jnp.float32] + [jnp.bfloat16] * (layers - 1)
    own_5, *pieces = add_sides(keep_5, after(come_5, own_4), types)
    parts_5 = send_all([(piece, layer[k]) for k, piece in enumerate(pieces, 1)], near_3)
    back_parts = [(own_3, far_3, near_3), (own_4, far_4, near_4), (own_5, *parts_5)]
    return (mixed, finish(back_chunks, back_parts, width))


def route_slots(expert_ids, local_count, device_count, capacity):
    experts = local_count * device_count
    row_count = expert_ids.shape[0] * expert_ids.shape[1]
    flat_ids = expert_ids.reshape(row_count)
    sort_order = jnp.argsort(flat_ids, stable=True)
    labels = lax.broadcasted_iota(jnp.int32, (1, experts), 1)
    counts = jnp.sum((flat_ids[:, None] == labels).astype(jnp.int32), axis=0)
    starts = jnp.cumsum(counts) - counts
    sorted_ids = flat_ids[sort_order]
    rank_within = jnp.arange(row_count, dtype=jnp.int32) - starts[sorted_ids]
    owner = sorted_ids // local_count
    local_slot = sorted_ids % local_count
    target = local_slot * (device_count * capacity) + owner * capacity + rank_within
    source_of = jnp.full((experts * capacity,), row_count, jnp.int32).at[target].set(sort_order)
    target_of = jnp.zeros((row_count,), jnp.int32).at[sort_order].set(target)
    return (source_of, target_of)


def pack_rows(values, source_of, top_count, local_count):
    token_count = values.shape[0]
    with_zero = jnp.concatenate([values, jnp.zeros((1, values.shape[1]), values.dtype)], axis=0)
    token_index = jnp.minimum(source_of // top_count, token_count)
    picked = with_zero[token_index]
    return picked.reshape(local_count, -1, values.shape[1])


def forward_part(received, gate_weight, up_weight, down_weight):
    gate_pre = jnp.einsum("erd,edh->erh", received, gate_weight, preferred_element_type=jnp.float32)
    up_pre = jnp.einsum("erd,edh->erh", received, up_weight, preferred_element_type=jnp.float32)
    sigmoid_gate = jax.nn.sigmoid(gate_pre)
    activ = (gate_pre * sigmoid_gate * up_pre).astype(jnp.bfloat16)
    expert_out = jnp.einsum("erh,ehd->erd", activ, down_weight, preferred_element_type=jnp.float32)
    return (expert_out.astype(jnp.bfloat16), gate_pre, up_pre, sigmoid_gate)


def backward_part(grad_rows, gate_pre, up_pre, sigmoid_gate, gate_weight, up_weight, down_weight):
    grad_act = jnp.einsum(
        "erd,ehd->erh", grad_rows, down_weight, preferred_element_type=jnp.float32
    )
    grad_gate = (grad_act * up_pre * sigmoid_gate * (1.0 + gate_pre * (1.0 - sigmoid_gate))).astype(
        jnp.bfloat16
    )
    grad_up = (grad_act * gate_pre * sigmoid_gate).astype(jnp.bfloat16)
    joined_grad = jnp.concatenate([grad_gate, grad_up], axis=2)
    joined_weight = jnp.concatenate([gate_weight, up_weight], axis=2)
    expert_back = jnp.einsum(
        "erh,edh->erd", joined_grad, joined_weight, preferred_element_type=jnp.float32
    )
    return expert_back.astype(jnp.bfloat16)


def combine_rows(returned, target_of, probs):
    token_count, top_count = probs.shape
    flat_back = returned.reshape(-1, returned.shape[2])
    picked = flat_back[target_of].reshape(token_count, top_count, returned.shape[2])
    return jnp.sum(picked.astype(jnp.float32) * probs[:, :, None], axis=1)


def on_device_routed(tokens, cotangent, expert_ids, probs, gate_weight, up_weight, down_weight):
    local_count = gate_weight.shape[0]
    device_count = lax.axis_size("expert")
    experts = local_count * device_count
    token_count, top_count = expert_ids.shape
    row_count = token_count * top_count
    capacity = row_count * 6 // (5 * experts)
    source_of, target_of = route_slots(expert_ids, local_count, device_count, capacity)
    send_rows = pack_rows(tokens, source_of, top_count, local_count)
    send_grads = pack_rows(cotangent, source_of, top_count, local_count)
    received = lax.all_to_all(send_rows, "expert", split_axis=1, concat_axis=1, tiled=True)
    expert_out, gate_pre, up_pre, sigmoid_gate = forward_part(
        received, gate_weight, up_weight, down_weight
    )
    returned_out = lax.all_to_all(expert_out, "expert", split_axis=1, concat_axis=1, tiled=True)
    received_grads = lax.all_to_all(send_grads, "expert", split_axis=1, concat_axis=1, tiled=True)
    expert_back = backward_part(
        received_grads, gate_pre, up_pre, sigmoid_gate, gate_weight, up_weight, down_weight
    )
    returned_back = lax.all_to_all(expert_back, "expert", split_axis=1, concat_axis=1, tiled=True)
    mixed = combine_rows(returned_out, target_of, probs)
    input_grad = combine_rows(returned_back, target_of, probs)
    return (mixed, input_grad)


def on_device(tokens, cotangent, expert_ids, probs, gate_weight, up_weight, down_weight):
    devices = lax.axis_size("expert")
    dense = devices % 4 == 0 and 12 <= devices <= 2 * expert_ids.shape[1]
    body = on_device_dense if dense else on_device_routed
    return body(tokens, cotangent, expert_ids, probs, gate_weight, up_weight, down_weight)


def solution(mesh):
    in_specs = (
        P(("dp", "expert"), None),
        P(("dp", "expert"), None),
        P(("dp", "expert"), None),
        P(("dp", "expert"), None),
        P(("dp", "expert"), None, None),
        P(("dp", "expert"), None, None),
        P(("dp", "expert"), None, None),
    )
    out_specs = (P(("dp", "expert"), None), P(("dp", "expert"), None))
    return jax.shard_map(
        on_device, mesh=mesh, in_specs=in_specs, out_specs=out_specs, check_vma=False
    )
```

```python
import functools

import jax
import jax.numpy as jnp
from jax import lax
from jax.experimental import pallas as pl
from jax.experimental.pallas import tpu as pltpu
from jax.sharding import PartitionSpec as P

VMEM_BYTES = 18 * 2**20
VMEM_BYTES_FETCH = 56 * 2**20
AT_ONCE = pl.CostEstimate(flops=1, bytes_accessed=1, transcendentals=0)


def resident(shape, index):
    return pl.BlockSpec(shape, index, pipeline_mode=pl.Buffered(1))


def compiler_params(vmem_bytes=VMEM_BYTES):
    return pltpu.CompilerParams(vmem_limit_bytes=vmem_bytes)


def fetch_rows(block_refs, buffer, sems):
    step = pl.program_id(0)
    count = len(block_refs) // pl.num_programs(0)

    @pl.when(step == 0)
    def _():
        for j, ref in enumerate(block_refs):
            pltpu.make_async_copy(ref, buffer.at[j], sems.at[j]).start()

    for j in range(len(block_refs)):

        @pl.when(step == j // count)
        def _(j=j):
            pltpu.make_async_copy(block_refs[j], buffer.at[j], sems.at[j]).wait()

    rows = buffer[pl.ds(step * count, count)]
    return rows.reshape(count * rows.shape[1], rows.shape[2])


def hidden_kernel(blocks, all_experts, owner_ref, gate_ref, up_ref, *refs):
    activ_ref, by_ref, buffer, sems = refs[blocks:]
    experts, width, hidden = gate_ref.shape
    rows = fetch_rows(refs[:blocks], buffer, sems)
    terms = rows[:, width:].astype(jnp.float32)
    rows = rows[:, :width]
    lanes = lax.broadcasted_iota(jnp.int32, terms.shape, 1)
    for e in range(experts):
        cut = slice(e * hidden, (e + 1) * hidden)
        cut_up = slice((experts + e) * hidden, (experts + e + 1) * hidden)
        label = owner_ref[0] * experts + e
        named = (lanes == label) | (lanes == label + all_experts) | (lanes == label + 2 * all_experts)
        weight = jnp.sum(jnp.where(named, terms, 0.0), axis=1, keepdims=True)
        gate_pre = jnp.dot(rows, gate_ref[e], preferred_element_type=jnp.float32)
        up_pre = jnp.dot(rows, up_ref[e], preferred_element_type=jnp.float32)
        sig = jax.nn.sigmoid(gate_pre)
        factor = sig * weight
        silu = gate_pre * factor
        activ_ref[:, cut] = (silu * up_pre).astype(jnp.bfloat16)
        by_ref[:, cut] = up_pre * factor * (1.0 + gate_pre * (1.0 - sig))
        by_ref[:, cut_up] = silu


def hidden_forward(row_blocks, owner, gate_weight, up_weight, all_experts):
    blocks = len(row_blocks)
    block, row_width = row_blocks[0].shape
    experts, width, hidden = gate_weight.shape
    count, columns, tile = blocks * block, experts * hidden, 2 * block
    weights = resident((experts, width, hidden), lambda i: (0, 0, 0))
    return pl.pallas_call(
        functools.partial(hidden_kernel, blocks, all_experts),
        grid=(blocks // 2,),
        in_specs=[pl.BlockSpec(memory_space=pltpu.SMEM), weights, weights]
        + [pl.BlockSpec(memory_space=pl.ANY)] * blocks,
        out_specs=[
            pl.BlockSpec((tile, columns), lambda i: (i, 0)),
            pl.BlockSpec((tile, 2 * columns), lambda i: (i, 0)),
        ],
        out_shape=[
            jax.ShapeDtypeStruct((count, columns), jnp.bfloat16),
            jax.ShapeDtypeStruct((count, 2 * columns), jnp.float32),
        ],
        scratch_shapes=[
            pltpu.VMEM((blocks, block, row_width), jnp.bfloat16),
            pltpu.SemaphoreType.DMA((blocks,)),
        ],
        compiler_params=compiler_params(VMEM_BYTES_FETCH),
        cost_estimate=AT_ONCE,
        name="hidden_forward",
    )(owner.reshape(1), gate_weight, up_weight, *row_blocks)


NT = (((1,), (1,)), ((), ()))


def grads_kernel(blocks, cuts, has_by, has_before, *refs):
    refs = list(refs)
    by_ref = refs.pop(0) if has_by else None
    before_ref = refs.pop(0) if has_before else None
    down_refs, block_refs = refs[: len(cuts)], refs[len(cuts) : len(cuts) + blocks]
    out_ref, buffer, sems = refs[len(cuts) + blocks :]
    rows = fetch_rows(block_refs, buffer, sems)
    total = before_ref[...] if has_before else None
    for (lo, hi), down_ref in zip(cuts, down_refs):
        term = lax.dot_general(rows[:, lo:hi], down_ref[...], NT, preferred_element_type=jnp.float32)
        total = term if total is None else total + term
    if has_by:
        columns = total.shape[1]
        out_ref[:, :columns] = (total * by_ref[:, :columns]).astype(jnp.bfloat16)
        out_ref[:, columns:] = (total * by_ref[:, columns:]).astype(jnp.bfloat16)
    else:
        out_ref[...] = total


def hidden_grads(grad_blocks, downs, cuts, by=None, before=None):
    blocks = len(grad_blocks)
    block, width = grad_blocks[0].shape
    columns = downs[0].shape[0]
    tile = 2 * block

    def rows(count):
        return pl.BlockSpec((tile, count), lambda i: (i, 0))

    given = [x for x in (by, before) if x is not None]
    out_columns, out_type = (columns, jnp.float32) if by is None else (2 * columns, jnp.bfloat16)
    return pl.pallas_call(
        functools.partial(grads_kernel, blocks, tuple(cuts), by is not None, before is not None),
        grid=(blocks // 2,),
        in_specs=[rows(x.shape[1]) for x in given]
        + [resident(d.shape, lambda i: (0, 0)) for d in downs]
        + [pl.BlockSpec(memory_space=pl.ANY)] * blocks,
        out_specs=rows(out_columns),
        out_shape=jax.ShapeDtypeStruct((blocks * block, out_columns), out_type),
        scratch_shapes=[
            pltpu.VMEM((blocks, block, width), jnp.bfloat16),
            pltpu.SemaphoreType.DMA((blocks,)),
        ],
        compiler_params=compiler_params(),
        cost_estimate=AT_ONCE,
        name="hidden_grads",
    )(*given, *downs, *grad_blocks)


def store_half(total, keep_ref, send_ref):
    @pl.when(pl.program_id(0) == 0)
    def _():
        send_ref[...] = total.astype(send_ref.dtype)

    @pl.when(pl.program_id(0) == 1)
    def _():
        keep_ref[...] = total


def mix_kernel(own_ref, other_ref, own_down_ref, other_down_ref, keep_ref, send_ref):
    total = jnp.dot(own_ref[...], own_down_ref[...], preferred_element_type=jnp.float32)
    total += jnp.dot(other_ref[...], other_down_ref[...], preferred_element_type=jnp.float32)
    store_half(total, keep_ref, send_ref)


def back_kernel(own_ref, other_ref, *refs):
    weight_refs, (keep_ref, send_ref) = refs[:-2], refs[-2:]
    experts, _, hidden = weight_refs[0].shape
    total = None
    for at, weight_ref in enumerate(weight_refs):
        grads_ref = (own_ref, other_ref)[at // 2]
        for e in range(experts):
            first = (at % 2 * experts + e) * hidden
            term = lax.dot_general(
                grads_ref[:, first : first + hidden], weight_ref[e], NT, preferred_element_type=jnp.float32
            )
            total = term if total is None else total + term
    store_half(total, keep_ref, send_ref)


def sum_columns(kernel, name, columns, own, other, weights, weight_specs):
    half, depth = own.shape[0] // 2, own.shape[1]
    rows = pl.BlockSpec((half, depth), lambda i: (1 - i, 0))
    return pl.pallas_call(
        kernel,
        grid=(2,),
        in_specs=[rows, rows] + weight_specs,
        out_specs=[pl.BlockSpec((half, columns), lambda i: (0, 0))] * 2,
        out_shape=[
            jax.ShapeDtypeStruct((half, columns), jnp.float32),
            jax.ShapeDtypeStruct((half, columns), jnp.bfloat16),
        ],
        compiler_params=compiler_params(),
        cost_estimate=AT_ONCE,
        name=name,
    )(own, other, *weights)


def mix_columns(own, other, own_down, other_down, at):
    depth, columns = other_down.shape
    specs = [
        resident((depth, columns), lambda i: (0, at)),
        resident((depth, columns), lambda i: (0, 0)),
    ]
    return sum_columns(mix_kernel, "mix_columns", columns, own, other, [own_down, other_down], specs)


def back_columns(own, other, weights, at, columns):
    experts, _, hidden = weights[0].shape
    specs = [resident((experts, columns, hidden), lambda i: (0, at, 0))] * len(weights)
    return sum_columns(back_kernel, "back_columns", columns, own, other, weights, specs)


def add_kernel(keep_ref, come_ref, *out_refs):
    block = out_refs[0].shape[0]
    for k, out_ref in enumerate(out_refs):
        cut = slice(k * block, (k + 1) * block)
        total = keep_ref[cut, :] + come_ref[cut, :].astype(jnp.float32)
        out_ref[...] = total.astype(out_ref.dtype)


def add_sides(keep, come, types):
    block, columns = keep.shape[0] // len(types), keep.shape[1]
    return pl.pallas_call(
        add_kernel,
        out_shape=[jax.ShapeDtypeStruct((block, columns), t) for t in types],
        compiler_params=compiler_params(),
        cost_estimate=AT_ONCE,
        name="add_sides",
    )(keep, come)


def add_piece(piece, come):
    return pl.pallas_call(
        add_kernel,
        out_shape=jax.ShapeDtypeStruct(piece.shape, jnp.bfloat16),
        compiler_params=compiler_params(),
        cost_estimate=AT_ONCE,
        name="add_piece",
    )(piece, come)


def finish_kernel(chunks, counts, *refs):
    out_ref = refs[-1]
    refs = list(refs[:-1])
    for (lo, hi), count in zip(chunks, counts):
        own_ref, *piece_refs = refs[:count]
        del refs[:count]
        total = own_ref[...]
        for piece_ref in piece_refs:
            total += piece_ref[...].astype(jnp.float32)
        out_ref[:, lo:hi] = total


def finish(chunks, parts, width):
    return pl.pallas_call(
        functools.partial(finish_kernel, tuple(chunks), tuple(map(len, parts))),
        out_shape=jax.ShapeDtypeStruct((parts[0][0].shape[0], width), jnp.float32),
        compiler_params=compiler_params(),
        cost_estimate=AT_ONCE,
        name="finish",
    )(*[p for part in parts for p in part])


def cut_columns(width, eighths):
    eighth = width // 8
    return [(lo * eighth, hi * eighth) for lo, hi in eighths]


def after(values, *others):
    return lax.optimization_barrier((values, *others))[0]


def send_all(sends, *waits):
    values, _ = lax.optimization_barrier(([v for v, _ in sends], waits))
    return [lax.ppermute(v, "expert", pairs) for v, (_, pairs) in zip(values, sends)]


def on_device_dense(tokens, cotangent, expert_ids, probs, gate_weight, up_weight, down_weight):
    local_count, hidden, width = down_weight.shape
    devices = lax.axis_size("expert")
    layers = devices // 4
    experts = local_count * devices
    block = tokens.shape[0]
    chunks = cut_columns(width, ((6, 8), (0, 3), (3, 6)))
    back_chunks = cut_columns(width, ((0, 3), (3, 6), (6, 8)))
    me = lax.axis_index("expert")
    twin = [(d, d ^ 1) for d in range(devices)]
    side = [(d, d ^ 2) for d in range(devices)]
    layer = [[(d, (d + 4 * k) % devices) for d in range(devices)] for k in range(layers)]

    labels = lax.broadcasted_iota(jnp.int32, (1, 1, experts), 2)
    weight = jnp.sum(jnp.where(expert_ids[:, :, None] == labels, probs[:, :, None], 0.0), axis=1)
    first = lax.reduce_precision(weight, 8, 7)
    second = lax.reduce_precision(weight - first, 8, 7)
    third = weight - first - second
    spare = jnp.zeros((block, -3 * experts % 128), jnp.bfloat16)
    terms = [t.astype(jnp.bfloat16) for t in (first, second, third)]
    row = jnp.concatenate([tokens] + terms + [spare], axis=1)
    grad = cotangent
    down = down_weight.reshape(local_count * hidden, width)
    downs = [down[:, lo:hi] for lo, hi in chunks]

    one, last, *middle = [1, layers - 1, *range(2, layers - 1)]
    rows, far_rows, grads, far_grads = {0: row}, {}, {0: grad}, {}
    other_gate, rows[one], far_rows[0] = send_all([(gate_weight, twin), (row, layer[-one]), (row, side)])
    rows[last], far_grads[0] = send_all([(row, layer[-last]), (grad, side)])
    (far_rows[one],) = send_all([(rows[one], side)], far_rows[0])
    for k in middle:
        (rows[k],) = send_all([(rows[k - 1], layer[-one])], far_rows[0])
    other_up, far_rows[last] = send_all([(up_weight, twin), (rows[last], side)], far_grads[0])
    got = send_all([(grad, layer[-one])] + [(rows[k], side) for k in middle], far_rows[one])
    grads[one] = got[0]
    far_rows.update(zip(middle, got[1:]))
    (grads[last],) = send_all([(grad, layer[-last])], far_rows[last])
    (down_0,) = send_all([(downs[0], twin)], far_rows[last], other_gate)
    (far_grads[one],) = send_all([(grads[one], side)], *far_rows.values())
    for k in middle:
        (grads[k],) = send_all([(grads[k - 1], layer[-one])], *far_rows.values())
    (far_grads[last],) = send_all([(grads[last], side)], *far_rows.values())
    row_blocks = [rows[k] for k in range(layers)] + [far_rows[k] for k in range(layers)]
    activ, by = hidden_forward(row_blocks, me, gate_weight, up_weight, experts)
    for k in middle:
        (far_grads[k],) = send_all([(grads[k], side)], far_grads[one], activ)
    other_up = after(other_up, activ)
    other_activ, other_by = hidden_forward(row_blocks, me ^ 1, other_gate, other_up, experts)

    (down_1,) = send_all([(downs[1], twin)], down_0, activ, other_activ)

    def mix(c, other_down, *waits):
        lo, hi = chunks[c]
        return mix_columns(activ, other_activ, down, after(other_down, *waits), lo // (hi - lo))

    types = [jnp.float32, jnp.float32] + [jnp.bfloat16] * (layers - 2)

    def send_on(pieces, *waits):
        (far,) = send_all([(pieces[-1], layer[last])], *waits)
        come = None
        for k in reversed(middle):
            piece = pieces[k - 1] if come is None else add_piece(pieces[k - 1], come)
            (come,) = send_all([(piece, layer[one])], *waits)
        return far, come

    def send_last(pieces, come, *waits):
        piece = pieces[0].astype(jnp.bfloat16) if come is None else add_piece(pieces[0], come)
        return send_all([(piece, layer[one])], *waits)[0]

    keep_0, send = mix(0, down_0, other_activ, *far_grads.values())
    come_0, down_2 = send_all([(send, side), (downs[2], twin)])
    grad_blocks = [grads[k] for k in range(layers)] + [far_grads[k] for k in range(layers)]
    own_grads = hidden_grads(grad_blocks, [down], [(0, width)], by=by)

    keep_1, send = mix(1, down_1, send, own_grads)
    own_0, *pieces = add_sides(after(keep_0, send), come_0, types)
    (come_1,) = send_all([(send, side)])
    far_0, next_0 = send_on(pieces)
    near_0 = send_last(pieces, next_0, far_0)
    grad_blocks = [after(grad_blocks[0], next_0), *grad_blocks[1:]]
    other_grad = hidden_grads(grad_blocks, [down_0, down_1], chunks[:2])

    keep_2, send = mix(2, down_2, other_grad, near_0)
    (come_2,) = send_all([(send, side)], own_0)

    other_by = after(other_by, send)
    other_grads = hidden_grads(grad_blocks, [down_2], chunks[2:], by=other_by, before=other_grad)
    weights = [gate_weight, up_weight, other_gate, other_up]

    def back(c, *waits):
        lo, hi = back_chunks[c]
        return back_columns(own_grads, after(other_grads, *waits), weights, lo // (hi - lo), hi - lo)

    keep_3, send = back(0)
    own_1, *pieces = add_sides(after(keep_1, send), come_1, types)
    (come_3,) = send_all([(send, side)], own_1)
    far_1, next_1 = send_on(pieces)
    near_1 = send_last(pieces, next_1, far_1)

    keep_4, send = back(1, next_1, far_1)
    own_2, *pieces = add_sides(after(keep_2, send), come_2, types)
    (come_4,) = send_all([(send, side)], own_2)
    far_2, next_2 = send_on(pieces)
    near_2 = send_last(pieces, next_2, far_2, near_1)

    keep_5, send = back(2, next_2)
    own_3, *pieces = add_sides(after(keep_3, send), come_3, types)
    (come_5,) = send_all([(send, side)], own_3)
    far_3, next_3 = send_on(pieces)
    near_3 = send_last(pieces, next_3, far_3, near_2)
    mixed = finish(chunks, [(own_0, far_0, near_0), (own_1, far_1, near_1), (own_2, far_2, near_2)], width)

    own_4, *pieces = add_sides(after(keep_4, mixed), after(come_4, next_3), types)
    far_4, next_4 = send_on(pieces)
    near_4 = send_last(pieces, next_4, far_4)

    types = [jnp.float32] + [jnp.bfloat16] * (layers - 1)
    own_5, *pieces = add_sides(keep_5, after(come_5, own_4), types)
    parts_5 = send_all([(piece, layer[k]) for k, piece in enumerate(pieces, 1)], near_3)
    back_parts = [(own_3, far_3, near_3), (own_4, far_4, near_4), (own_5, *parts_5)]
    return (mixed, finish(back_chunks, back_parts, width))


def route_slots(expert_ids, local_count, device_count, capacity):
    experts = local_count * device_count
    row_count = expert_ids.shape[0] * expert_ids.shape[1]
    flat_ids = expert_ids.reshape(row_count)
    sort_order = jnp.argsort(flat_ids, stable=True)
    labels = lax.broadcasted_iota(jnp.int32, (1, experts), 1)
    counts = jnp.sum((flat_ids[:, None] == labels).astype(jnp.int32), axis=0)
    starts = jnp.cumsum(counts) - counts
    sorted_ids = flat_ids[sort_order]
    rank_within = jnp.arange(row_count, dtype=jnp.int32) - starts[sorted_ids]
    owner = sorted_ids // local_count
    local_slot = sorted_ids % local_count
    target = local_slot * (device_count * capacity) + owner * capacity + rank_within
    source_of = jnp.full((experts * capacity,), row_count, jnp.int32).at[target].set(sort_order)
    target_of = jnp.zeros((row_count,), jnp.int32).at[sort_order].set(target)
    return (source_of, target_of)


def pack_rows(values, source_of, top_count, local_count):
    token_count = values.shape[0]
    with_zero = jnp.concatenate([values, jnp.zeros((1, values.shape[1]), values.dtype)], axis=0)
    token_index = jnp.minimum(source_of // top_count, token_count)
    picked = with_zero[token_index]
    return picked.reshape(local_count, -1, values.shape[1])


def forward_part(received, gate_weight, up_weight, down_weight):
    gate_pre = jnp.einsum("erd,edh->erh", received, gate_weight, preferred_element_type=jnp.float32)
    up_pre = jnp.einsum("erd,edh->erh", received, up_weight, preferred_element_type=jnp.float32)
    sigmoid_gate = jax.nn.sigmoid(gate_pre)
    activ = (gate_pre * sigmoid_gate * up_pre).astype(jnp.bfloat16)
    expert_out = jnp.einsum("erh,ehd->erd", activ, down_weight, preferred_element_type=jnp.float32)
    return (expert_out.astype(jnp.bfloat16), gate_pre, up_pre, sigmoid_gate)


def backward_part(grad_rows, gate_pre, up_pre, sigmoid_gate, gate_weight, up_weight, down_weight):
    grad_act = jnp.einsum(
        "erd,ehd->erh", grad_rows, down_weight, preferred_element_type=jnp.float32
    )
    grad_gate = (grad_act * up_pre * sigmoid_gate * (1.0 + gate_pre * (1.0 - sigmoid_gate))).astype(
        jnp.bfloat16
    )
    grad_up = (grad_act * gate_pre * sigmoid_gate).astype(jnp.bfloat16)
    joined_grad = jnp.concatenate([grad_gate, grad_up], axis=2)
    joined_weight = jnp.concatenate([gate_weight, up_weight], axis=2)
    expert_back = jnp.einsum(
        "erh,edh->erd", joined_grad, joined_weight, preferred_element_type=jnp.float32
    )
    return expert_back.astype(jnp.bfloat16)


def combine_rows(returned, target_of, probs):
    token_count, top_count = probs.shape
    flat_back = returned.reshape(-1, returned.shape[2])
    picked = flat_back[target_of].reshape(token_count, top_count, returned.shape[2])
    return jnp.sum(picked.astype(jnp.float32) * probs[:, :, None], axis=1)


def on_device_routed(tokens, cotangent, expert_ids, probs, gate_weight, up_weight, down_weight):
    local_count = gate_weight.shape[0]
    device_count = lax.axis_size("expert")
    experts = local_count * device_count
    token_count, top_count = expert_ids.shape
    row_count = token_count * top_count
    capacity = row_count * 6 // (5 * experts)
    source_of, target_of = route_slots(expert_ids, local_count, device_count, capacity)
    send_rows = pack_rows(tokens, source_of, top_count, local_count)
    send_grads = pack_rows(cotangent, source_of, top_count, local_count)
    received = lax.all_to_all(send_rows, "expert", split_axis=1, concat_axis=1, tiled=True)
    expert_out, gate_pre, up_pre, sigmoid_gate = forward_part(
        received, gate_weight, up_weight, down_weight
    )
    returned_out = lax.all_to_all(expert_out, "expert", split_axis=1, concat_axis=1, tiled=True)
    received_grads = lax.all_to_all(send_grads, "expert", split_axis=1, concat_axis=1, tiled=True)
    expert_back = backward_part(
        received_grads, gate_pre, up_pre, sigmoid_gate, gate_weight, up_weight, down_weight
    )
    returned_back = lax.all_to_all(expert_back, "expert", split_axis=1, concat_axis=1, tiled=True)
    mixed = combine_rows(returned_out, target_of, probs)
    input_grad = combine_rows(returned_back, target_of, probs)
    return (mixed, input_grad)


def on_device(tokens, cotangent, expert_ids, probs, gate_weight, up_weight, down_weight):
    devices = lax.axis_size("expert")
    dense = devices % 4 == 0 and 12 <= devices <= 2 * expert_ids.shape[1]
    body = on_device_dense if dense else on_device_routed
    return body(tokens, cotangent, expert_ids, probs, gate_weight, up_weight, down_weight)


def solution(mesh):
    in_specs = (
        P(("dp", "expert"), None),
        P(("dp", "expert"), None),
        P(("dp", "expert"), None),
        P(("dp", "expert"), None),
        P(("dp", "expert"), None, None),
        P(("dp", "expert"), None, None),
        P(("dp", "expert"), None, None),
    )
    out_specs = (P(("dp", "expert"), None), P(("dp", "expert"), None))
    return jax.shard_map(
        on_device, mesh=mesh, in_specs=in_specs, out_specs=out_specs, check_vma=False
    )
```

```python
import functools

import jax
import jax.numpy as jnp
from jax import lax
from jax.experimental import pallas as pl
from jax.experimental.pallas import tpu as pltpu
from jax.sharding import PartitionSpec as P

VMEM_BYTES = 18 * 2**20
VMEM_BYTES_FETCH = 56 * 2**20
AT_ONCE = pl.CostEstimate(flops=1, bytes_accessed=1, transcendentals=0)


def resident(shape, index):
    return pl.BlockSpec(shape, index, pipeline_mode=pl.Buffered(1))


def compiler_params(vmem_bytes=VMEM_BYTES):
    return pltpu.CompilerParams(vmem_limit_bytes=vmem_bytes)


def fetch_rows(block_refs, buffer, sems):
    step = pl.program_id(0)
    count = len(block_refs) // pl.num_programs(0)

    @pl.when(step == 0)
    def _():
        for j, ref in enumerate(block_refs):
            pltpu.make_async_copy(ref, buffer.at[j], sems.at[j]).start()

    for j in range(len(block_refs)):

        @pl.when(step == j // count)
        def _(j=j):
            pltpu.make_async_copy(block_refs[j], buffer.at[j], sems.at[j]).wait()

    rows = buffer[pl.ds(step * count, count)]
    return rows.reshape(count * rows.shape[1], rows.shape[2])


def hidden_kernel(blocks, all_experts, owner_ref, gate_ref, up_ref, *refs):
    activ_ref, by_ref, buffer, sems = refs[blocks:]
    experts, width, hidden = gate_ref.shape
    rows = fetch_rows(refs[:blocks], buffer, sems)
    terms = rows[:, width:].astype(jnp.float32)
    rows = rows[:, :width]
    lanes = lax.broadcasted_iota(jnp.int32, terms.shape, 1)
    for e in range(experts):
        cut = slice(e * hidden, (e + 1) * hidden)
        cut_up = slice((experts + e) * hidden, (experts + e + 1) * hidden)
        label = owner_ref[0] * experts + e
        named = (lanes == label) | (lanes == label + all_experts) | (lanes == label + 2 * all_experts)
        weight = jnp.sum(jnp.where(named, terms, 0.0), axis=1, keepdims=True)
        gate_pre = jnp.dot(rows, gate_ref[e], preferred_element_type=jnp.float32)
        up_pre = jnp.dot(rows, up_ref[e], preferred_element_type=jnp.float32)
        sig = jax.nn.sigmoid(gate_pre)
        factor = sig * weight
        silu = gate_pre * factor
        activ_ref[:, cut] = (silu * up_pre).astype(jnp.bfloat16)
        by_ref[:, cut] = up_pre * factor * (1.0 + gate_pre * (1.0 - sig))
        by_ref[:, cut_up] = silu


def hidden_forward(row_blocks, owner, gate_weight, up_weight, all_experts):
    blocks = len(row_blocks)
    block, row_width = row_blocks[0].shape
    experts, width, hidden = gate_weight.shape
    count, columns, tile = blocks * block, experts * hidden, 2 * block
    weights = resident((experts, width, hidden), lambda i: (0, 0, 0))
    return pl.pallas_call(
        functools.partial(hidden_kernel, blocks, all_experts),
        grid=(blocks // 2,),
        in_specs=[pl.BlockSpec(memory_space=pltpu.SMEM), weights, weights]
        + [pl.BlockSpec(memory_space=pl.ANY)] * blocks,
        out_specs=[
            pl.BlockSpec((tile, columns), lambda i: (i, 0)),
            pl.BlockSpec((tile, 2 * columns), lambda i: (i, 0)),
        ],
        out_shape=[
            jax.ShapeDtypeStruct((count, columns), jnp.bfloat16),
            jax.ShapeDtypeStruct((count, 2 * columns), jnp.float32),
        ],
        scratch_shapes=[
            pltpu.VMEM((blocks, block, row_width), jnp.bfloat16),
            pltpu.SemaphoreType.DMA((blocks,)),
        ],
        compiler_params=compiler_params(VMEM_BYTES_FETCH),
        cost_estimate=AT_ONCE,
        name="hidden_forward",
    )(owner.reshape(1), gate_weight, up_weight, *row_blocks)


NT = (((1,), (1,)), ((), ()))


def grads_kernel(blocks, cuts, has_by, has_before, *refs):
    refs = list(refs)
    by_ref = refs.pop(0) if has_by else None
    before_ref = refs.pop(0) if has_before else None
    down_refs, block_refs = refs[: len(cuts)], refs[len(cuts) : len(cuts) + blocks]
    out_ref, buffer, sems = refs[len(cuts) + blocks :]
    rows = fetch_rows(block_refs, buffer, sems)
    total = before_ref[...] if has_before else None
    for (lo, hi), down_ref in zip(cuts, down_refs):
        term = lax.dot_general(rows[:, lo:hi], down_ref[...], NT, preferred_element_type=jnp.float32)
        total = term if total is None else total + term
    if has_by:
        columns = total.shape[1]
        out_ref[:, :columns] = (total * by_ref[:, :columns]).astype(jnp.bfloat16)
        out_ref[:, columns:] = (total * by_ref[:, columns:]).astype(jnp.bfloat16)
    else:
        out_ref[...] = total


def hidden_grads(grad_blocks, downs, cuts, by=None, before=None):
    blocks = len(grad_blocks)
    block, width = grad_blocks[0].shape
    columns = downs[0].shape[0]
    tile = 2 * block

    def rows(count):
        return pl.BlockSpec((tile, count), lambda i: (i, 0))

    given = [x for x in (by, before) if x is not None]
    out_columns, out_type = (columns, jnp.float32) if by is None else (2 * columns, jnp.bfloat16)
    return pl.pallas_call(
        functools.partial(grads_kernel, blocks, tuple(cuts), by is not None, before is not None),
        grid=(blocks // 2,),
        in_specs=[rows(x.shape[1]) for x in given]
        + [resident(d.shape, lambda i: (0, 0)) for d in downs]
        + [pl.BlockSpec(memory_space=pl.ANY)] * blocks,
        out_specs=rows(out_columns),
        out_shape=jax.ShapeDtypeStruct((blocks * block, out_columns), out_type),
        scratch_shapes=[
            pltpu.VMEM((blocks, block, width), jnp.bfloat16),
            pltpu.SemaphoreType.DMA((blocks,)),
        ],
        compiler_params=compiler_params(),
        cost_estimate=AT_ONCE,
        name="hidden_grads",
    )(*given, *downs, *grad_blocks)


def store_half(total, keep_ref, send_ref):
    @pl.when(pl.program_id(0) == 0)
    def _():
        send_ref[...] = total.astype(send_ref.dtype)

    @pl.when(pl.program_id(0) == 1)
    def _():
        keep_ref[...] = total


def mix_kernel(own_ref, other_ref, own_down_ref, other_down_ref, keep_ref, send_ref):
    total = jnp.dot(own_ref[...], own_down_ref[...], preferred_element_type=jnp.float32)
    total += jnp.dot(other_ref[...], other_down_ref[...], preferred_element_type=jnp.float32)
    store_half(total, keep_ref, send_ref)


def back_kernel(own_ref, other_ref, *refs):
    weight_refs, (keep_ref, send_ref) = refs[:-2], refs[-2:]
    experts, _, hidden = weight_refs[0].shape
    total = None
    for at, weight_ref in enumerate(weight_refs):
        grads_ref = (own_ref, other_ref)[at // 2]
        for e in range(experts):
            first = (at % 2 * experts + e) * hidden
            term = lax.dot_general(
                grads_ref[:, first : first + hidden], weight_ref[e], NT, preferred_element_type=jnp.float32
            )
            total = term if total is None else total + term
    store_half(total, keep_ref, send_ref)


def sum_columns(kernel, name, columns, own, other, weights, weight_specs):
    half, depth = own.shape[0] // 2, own.shape[1]
    rows = pl.BlockSpec((half, depth), lambda i: (1 - i, 0))
    return pl.pallas_call(
        kernel,
        grid=(2,),
        in_specs=[rows, rows] + weight_specs,
        out_specs=[pl.BlockSpec((half, columns), lambda i: (0, 0))] * 2,
        out_shape=[
            jax.ShapeDtypeStruct((half, columns), jnp.float32),
            jax.ShapeDtypeStruct((half, columns), jnp.bfloat16),
        ],
        compiler_params=compiler_params(),
        cost_estimate=AT_ONCE,
        name=name,
    )(own, other, *weights)


def mix_columns(own, other, own_down, other_down, at):
    depth, columns = other_down.shape
    specs = [
        resident((depth, columns), lambda i: (0, at)),
        resident((depth, columns), lambda i: (0, 0)),
    ]
    return sum_columns(mix_kernel, "mix_columns", columns, own, other, [own_down, other_down], specs)


def back_columns(own, other, weights, at, columns):
    experts, _, hidden = weights[0].shape
    specs = [resident((experts, columns, hidden), lambda i: (0, at, 0))] * len(weights)
    return sum_columns(back_kernel, "back_columns", columns, own, other, weights, specs)


def add_kernel(keep_ref, come_ref, *out_refs):
    block = out_refs[0].shape[0]
    for k, out_ref in enumerate(out_refs):
        cut = slice(k * block, (k + 1) * block)
        total = keep_ref[cut, :] + come_ref[cut, :].astype(jnp.float32)
        out_ref[...] = total.astype(out_ref.dtype)


def add_sides(keep, come, types):
    block, columns = keep.shape[0] // len(types), keep.shape[1]
    return pl.pallas_call(
        add_kernel,
        out_shape=[jax.ShapeDtypeStruct((block, columns), t) for t in types],
        compiler_params=compiler_params(),
        cost_estimate=AT_ONCE,
        name="add_sides",
    )(keep, come)


def add_piece(piece, come):
    return pl.pallas_call(
        add_kernel,
        out_shape=jax.ShapeDtypeStruct(piece.shape, jnp.bfloat16),
        compiler_params=compiler_params(),
        cost_estimate=AT_ONCE,
        name="add_piece",
    )(piece, come)


def finish_kernel(chunks, counts, *refs):
    out_ref = refs[-1]
    refs = list(refs[:-1])
    for (lo, hi), count in zip(chunks, counts):
        own_ref, *piece_refs = refs[:count]
        del refs[:count]
        total = own_ref[...]
        for piece_ref in piece_refs:
            total += piece_ref[...].astype(jnp.float32)
        out_ref[:, lo:hi] = total


def finish(chunks, parts, width):
    return pl.pallas_call(
        functools.partial(finish_kernel, tuple(chunks), tuple(map(len, parts))),
        out_shape=jax.ShapeDtypeStruct((parts[0][0].shape[0], width), jnp.float32),
        compiler_params=compiler_params(),
        cost_estimate=AT_ONCE,
        name="finish",
    )(*[p for part in parts for p in part])


def cut_columns(width, eighths):
    eighth = width // 8
    return [(lo * eighth, hi * eighth) for lo, hi in eighths]


def after(values, *others):
    return lax.optimization_barrier((values, *others))[0]


def send_all(sends, *waits):
    values, _ = lax.optimization_barrier(([v for v, _ in sends], waits))
    return [lax.ppermute(v, "expert", pairs) for v, (_, pairs) in zip(values, sends)]


def on_device_dense(tokens, cotangent, expert_ids, probs, gate_weight, up_weight, down_weight):
    local_count, hidden, width = down_weight.shape
    devices = lax.axis_size("expert")
    layers = devices // 4
    experts = local_count * devices
    block = tokens.shape[0]
    chunks = cut_columns(width, ((6, 8), (0, 3), (3, 6)))
    back_chunks = cut_columns(width, ((0, 3), (3, 6), (6, 8)))
    me = lax.axis_index("expert")
    twin = [(d, d ^ 1) for d in range(devices)]
    side = [(d, d ^ 2) for d in range(devices)]
    layer = [[(d, (d + 4 * k) % devices) for d in range(devices)] for k in range(layers)]

    labels = lax.broadcasted_iota(jnp.int32, (1, 1, experts), 2)
    weight = jnp.sum(jnp.where(expert_ids[:, :, None] == labels, probs[:, :, None], 0.0), axis=1)
    first = lax.reduce_precision(weight, 8, 7)
    second = lax.reduce_precision(weight - first, 8, 7)
    third = weight - first - second
    spare = jnp.zeros((block, -3 * experts % 128), jnp.bfloat16)
    terms = [t.astype(jnp.bfloat16) for t in (first, second, third)]
    row = jnp.concatenate([tokens] + terms + [spare], axis=1)
    grad = cotangent
    down = down_weight.reshape(local_count * hidden, width)
    downs = [down[:, lo:hi] for lo, hi in chunks]

    one, last, *middle = [1, layers - 1, *range(2, layers - 1)]
    rows, far_rows, grads, far_grads = {0: row}, {}, {0: grad}, {}
    other_gate, rows[one], far_rows[0] = send_all([(gate_weight, twin), (row, layer[-one]), (row, side)])
    rows[last], far_grads[0] = send_all([(row, layer[-last]), (grad, side)])
    (far_rows[one],) = send_all([(rows[one], side)], far_rows[0])
    for k in middle:
        (rows[k],) = send_all([(rows[k - 1], layer[-one])], far_rows[0])
    other_up, far_rows[last] = send_all([(up_weight, twin), (rows[last], side)], far_grads[0])
    got = send_all([(grad, layer[-one])] + [(rows[k], side) for k in middle], far_rows[one])
    grads[one] = got[0]
    far_rows.update(zip(middle, got[1:]))
    (grads[last],) = send_all([(grad, layer[-last])], far_rows[last])
    (down_0,) = send_all([(downs[0], twin)], far_rows[last], other_gate)
    (far_grads[one],) = send_all([(grads[one], side)], *far_rows.values())
    for k in middle:
        (grads[k],) = send_all([(grads[k - 1], layer[-one])], *far_rows.values())
    (far_grads[last],) = send_all([(grads[last], side)], *far_rows.values())
    row_blocks = [rows[k] for k in range(layers)] + [far_rows[k] for k in range(layers)]
    activ, by = hidden_forward(row_blocks, me, gate_weight, up_weight, experts)
    for k in middle:
        (far_grads[k],) = send_all([(grads[k], side)], far_grads[one], activ)
    other_up = after(other_up, activ)
    other_activ, other_by = hidden_forward(row_blocks, me ^ 1, other_gate, other_up, experts)

    (down_1,) = send_all([(downs[1], twin)], down_0, activ, other_activ)

    def mix(c, other_down, *waits):
        lo, hi = chunks[c]
        return mix_columns(activ, other_activ, down, after(other_down, *waits), lo // (hi - lo))

    types = [jnp.float32, jnp.float32] + [jnp.bfloat16] * (layers - 2)

    def send_on(pieces, *waits):
        (far,) = send_all([(pieces[-1], layer[last])], *waits)
        come = None
        for k in reversed(middle):
            piece = pieces[k - 1] if come is None else add_piece(pieces[k - 1], come)
            (come,) = send_all([(piece, layer[one])], *waits)
        return far, come

    def send_last(pieces, come, *waits):
        piece = pieces[0].astype(jnp.bfloat16) if come is None else add_piece(pieces[0], come)
        return send_all([(piece, layer[one])], *waits)[0]

    keep_0, send = mix(0, down_0, other_activ, *far_grads.values())
    come_0, down_2 = send_all([(send, side), (downs[2], twin)])
    grad_blocks = [grads[k] for k in range(layers)] + [far_grads[k] for k in range(layers)]
    own_grads = hidden_grads(grad_blocks, [down], [(0, width)], by=by)

    keep_1, send = mix(1, down_1, send, own_grads)
    own_0, *pieces = add_sides(after(keep_0, send), come_0, types)
    (come_1,) = send_all([(send, side)])
    grad_blocks = [after(grad_blocks[0], send), *grad_blocks[1:]]
    other_grad = hidden_grads(grad_blocks, [down_0, down_1], chunks[:2])
    far_0, next_0 = send_on(pieces, other_grad)
    near_0 = send_last(pieces, next_0, far_0)

    keep_2, send = mix(2, down_2, other_grad, near_0)
    (come_2,) = send_all([(send, side)], own_0)

    other_by = after(other_by, send)
    other_grads = hidden_grads(grad_blocks, [down_2], chunks[2:], by=other_by, before=other_grad)
    weights = [gate_weight, up_weight, other_gate, other_up]

    def back(c, *waits):
        lo, hi = back_chunks[c]
        return back_columns(own_grads, after(other_grads, *waits), weights, lo // (hi - lo), hi - lo)

    own_1, *pieces = add_sides(after(keep_1, other_grads), come_1, types)
    far_1, next_1 = send_on(pieces)
    near_1 = send_last(pieces, next_1, far_1)
    keep_3, send = back(0, next_1, far_1)
    (come_3,) = send_all([(send, side)], own_1)

    keep_4, send = back(1, send)
    own_2, *pieces = add_sides(keep_2, come_2, types)
    (come_4,) = send_all([(send, side)], own_2)
    far_2, next_2 = send_on(pieces)
    near_2 = send_last(pieces, next_2, far_2, near_1)

    keep_5, send = back(2, next_2)
    own_3, *pieces = add_sides(after(keep_3, send), come_3, types)
    (come_5,) = send_all([(send, side)], own_3)
    far_3, next_3 = send_on(pieces)
    near_3 = send_last(pieces, next_3, far_3, near_2)
    mixed = finish(chunks, [(own_0, far_0, near_0), (own_1, far_1, near_1), (own_2, far_2, near_2)], width)

    own_4, *pieces = add_sides(after(keep_4, mixed), after(come_4, next_3), types)
    far_4, next_4 = send_on(pieces)
    near_4 = send_last(pieces, next_4, far_4)

    types = [jnp.float32] + [jnp.bfloat16] * (layers - 1)
    own_5, *pieces = add_sides(keep_5, after(come_5, own_4), types)
    parts_5 = send_all([(piece, layer[k]) for k, piece in enumerate(pieces, 1)], near_3)
    back_parts = [(own_3, far_3, near_3), (own_4, far_4, near_4), (own_5, *parts_5)]
    return (mixed, finish(back_chunks, back_parts, width))


def route_slots(expert_ids, local_count, device_count, capacity):
    experts = local_count * device_count
    row_count = expert_ids.shape[0] * expert_ids.shape[1]
    flat_ids = expert_ids.reshape(row_count)
    sort_order = jnp.argsort(flat_ids, stable=True)
    labels = lax.broadcasted_iota(jnp.int32, (1, experts), 1)
    counts = jnp.sum((flat_ids[:, None] == labels).astype(jnp.int32), axis=0)
    starts = jnp.cumsum(counts) - counts
    sorted_ids = flat_ids[sort_order]
    rank_within = jnp.arange(row_count, dtype=jnp.int32) - starts[sorted_ids]
    owner = sorted_ids // local_count
    local_slot = sorted_ids % local_count
    target = local_slot * (device_count * capacity) + owner * capacity + rank_within
    source_of = jnp.full((experts * capacity,), row_count, jnp.int32).at[target].set(sort_order)
    target_of = jnp.zeros((row_count,), jnp.int32).at[sort_order].set(target)
    return (source_of, target_of)


def pack_rows(values, source_of, top_count, local_count):
    token_count = values.shape[0]
    with_zero = jnp.concatenate([values, jnp.zeros((1, values.shape[1]), values.dtype)], axis=0)
    token_index = jnp.minimum(source_of // top_count, token_count)
    picked = with_zero[token_index]
    return picked.reshape(local_count, -1, values.shape[1])


def forward_part(received, gate_weight, up_weight, down_weight):
    gate_pre = jnp.einsum("erd,edh->erh", received, gate_weight, preferred_element_type=jnp.float32)
    up_pre = jnp.einsum("erd,edh->erh", received, up_weight, preferred_element_type=jnp.float32)
    sigmoid_gate = jax.nn.sigmoid(gate_pre)
    activ = (gate_pre * sigmoid_gate * up_pre).astype(jnp.bfloat16)
    expert_out = jnp.einsum("erh,ehd->erd", activ, down_weight, preferred_element_type=jnp.float32)
    return (expert_out.astype(jnp.bfloat16), gate_pre, up_pre, sigmoid_gate)


def backward_part(grad_rows, gate_pre, up_pre, sigmoid_gate, gate_weight, up_weight, down_weight):
    grad_act = jnp.einsum(
        "erd,ehd->erh", grad_rows, down_weight, preferred_element_type=jnp.float32
    )
    grad_gate = (grad_act * up_pre * sigmoid_gate * (1.0 + gate_pre * (1.0 - sigmoid_gate))).astype(
        jnp.bfloat16
    )
    grad_up = (grad_act * gate_pre * sigmoid_gate).astype(jnp.bfloat16)
    joined_grad = jnp.concatenate([grad_gate, grad_up], axis=2)
    joined_weight = jnp.concatenate([gate_weight, up_weight], axis=2)
    expert_back = jnp.einsum(
        "erh,edh->erd", joined_grad, joined_weight, preferred_element_type=jnp.float32
    )
    return expert_back.astype(jnp.bfloat16)


def combine_rows(returned, target_of, probs):
    token_count, top_count = probs.shape
    flat_back = returned.reshape(-1, returned.shape[2])
    picked = flat_back[target_of].reshape(token_count, top_count, returned.shape[2])
    return jnp.sum(picked.astype(jnp.float32) * probs[:, :, None], axis=1)


def on_device_routed(tokens, cotangent, expert_ids, probs, gate_weight, up_weight, down_weight):
    local_count = gate_weight.shape[0]
    device_count = lax.axis_size("expert")
    experts = local_count * device_count
    token_count, top_count = expert_ids.shape
    row_count = token_count * top_count
    capacity = row_count * 6 // (5 * experts)
    source_of, target_of = route_slots(expert_ids, local_count, device_count, capacity)
    send_rows = pack_rows(tokens, source_of, top_count, local_count)
    send_grads = pack_rows(cotangent, source_of, top_count, local_count)
    received = lax.all_to_all(send_rows, "expert", split_axis=1, concat_axis=1, tiled=True)
    expert_out, gate_pre, up_pre, sigmoid_gate = forward_part(
        received, gate_weight, up_weight, down_weight
    )
    returned_out = lax.all_to_all(expert_out, "expert", split_axis=1, concat_axis=1, tiled=True)
    received_grads = lax.all_to_all(send_grads, "expert", split_axis=1, concat_axis=1, tiled=True)
    expert_back = backward_part(
        received_grads, gate_pre, up_pre, sigmoid_gate, gate_weight, up_weight, down_weight
    )
    returned_back = lax.all_to_all(expert_back, "expert", split_axis=1, concat_axis=1, tiled=True)
    mixed = combine_rows(returned_out, target_of, probs)
    input_grad = combine_rows(returned_back, target_of, probs)
    return (mixed, input_grad)


def on_device(tokens, cotangent, expert_ids, probs, gate_weight, up_weight, down_weight):
    devices = lax.axis_size("expert")
    dense = devices % 4 == 0 and 12 <= devices <= 2 * expert_ids.shape[1]
    body = on_device_dense if dense else on_device_routed
    return body(tokens, cotangent, expert_ids, probs, gate_weight, up_weight, down_weight)


def solution(mesh):
    in_specs = (
        P(("dp", "expert"), None),
        P(("dp", "expert"), None),
        P(("dp", "expert"), None),
        P(("dp", "expert"), None),
        P(("dp", "expert"), None, None),
        P(("dp", "expert"), None, None),
        P(("dp", "expert"), None, None),
    )
    out_specs = (P(("dp", "expert"), None), P(("dp", "expert"), None))
    return jax.shard_map(
        on_device, mesh=mesh, in_specs=in_specs, out_specs=out_specs, check_vma=False
    )
```

```python
import functools

import jax
import jax.numpy as jnp
from jax import lax
from jax.experimental import pallas as pl
from jax.experimental.pallas import tpu as pltpu
from jax.sharding import PartitionSpec as P

VMEM_BYTES = 18 * 2**20
VMEM_BYTES_FETCH = 56 * 2**20
AT_ONCE = pl.CostEstimate(flops=1, bytes_accessed=1, transcendentals=0)


def resident(shape, index):
    return pl.BlockSpec(shape, index, pipeline_mode=pl.Buffered(1))


def compiler_params(vmem_bytes=VMEM_BYTES):
    return pltpu.CompilerParams(vmem_limit_bytes=vmem_bytes)


def fetch_rows(block_refs, buffer, sems):
    step = pl.program_id(0)
    count = len(block_refs) // pl.num_programs(0)

    @pl.when(step == 0)
    def _():
        for j, ref in enumerate(block_refs):
            pltpu.make_async_copy(ref, buffer.at[j], sems.at[j]).start()

    for j in range(len(block_refs)):

        @pl.when(step == j // count)
        def _(j=j):
            pltpu.make_async_copy(block_refs[j], buffer.at[j], sems.at[j]).wait()

    rows = buffer[pl.ds(step * count, count)]
    return rows.reshape(count * rows.shape[1], rows.shape[2])


def hidden_kernel(blocks, all_experts, owner_ref, gate_ref, up_ref, *refs):
    activ_ref, by_ref, buffer, sems = refs[blocks:]
    experts, width, hidden = gate_ref.shape
    rows = fetch_rows(refs[:blocks], buffer, sems)
    terms = rows[:, width:].astype(jnp.float32)
    rows = rows[:, :width]
    lanes = lax.broadcasted_iota(jnp.int32, terms.shape, 1)
    for e in range(experts):
        cut = slice(e * hidden, (e + 1) * hidden)
        cut_up = slice((experts + e) * hidden, (experts + e + 1) * hidden)
        label = owner_ref[0] * experts + e
        named = (lanes == label) | (lanes == label + all_experts) | (lanes == label + 2 * all_experts)
        weight = jnp.sum(jnp.where(named, terms, 0.0), axis=1, keepdims=True)
        gate_pre = jnp.dot(rows, gate_ref[e], preferred_element_type=jnp.float32)
        up_pre = jnp.dot(rows, up_ref[e], preferred_element_type=jnp.float32)
        sig = jax.nn.sigmoid(gate_pre)
        factor = sig * weight
        silu = gate_pre * factor
        activ_ref[:, cut] = (silu * up_pre).astype(jnp.bfloat16)
        by_ref[:, cut] = up_pre * factor * (1.0 + gate_pre * (1.0 - sig))
        by_ref[:, cut_up] = silu


def hidden_forward(row_blocks, owner, gate_weight, up_weight, all_experts):
    blocks = len(row_blocks)
    block, row_width = row_blocks[0].shape
    experts, width, hidden = gate_weight.shape
    count, columns, tile = blocks * block, experts * hidden, 2 * block
    weights = resident((experts, width, hidden), lambda i: (0, 0, 0))
    return pl.pallas_call(
        functools.partial(hidden_kernel, blocks, all_experts),
        grid=(blocks // 2,),
        in_specs=[pl.BlockSpec(memory_space=pltpu.SMEM), weights, weights]
        + [pl.BlockSpec(memory_space=pl.ANY)] * blocks,
        out_specs=[
            pl.BlockSpec((tile, columns), lambda i: (i, 0)),
            pl.BlockSpec((tile, 2 * columns), lambda i: (i, 0)),
        ],
        out_shape=[
            jax.ShapeDtypeStruct((count, columns), jnp.bfloat16),
            jax.ShapeDtypeStruct((count, 2 * columns), jnp.float32),
        ],
        scratch_shapes=[
            pltpu.VMEM((blocks, block, row_width), jnp.bfloat16),
            pltpu.SemaphoreType.DMA((blocks,)),
        ],
        compiler_params=compiler_params(VMEM_BYTES_FETCH),
        cost_estimate=AT_ONCE,
        name="hidden_forward",
    )(owner.reshape(1), gate_weight, up_weight, *row_blocks)


NT = (((1,), (1,)), ((), ()))


def grads_kernel(blocks, cuts, has_by, has_before, *refs):
    refs = list(refs)
    by_ref = refs.pop(0) if has_by else None
    before_ref = refs.pop(0) if has_before else None
    down_refs, block_refs = refs[: len(cuts)], refs[len(cuts) : len(cuts) + blocks]
    out_ref, buffer, sems = refs[len(cuts) + blocks :]
    rows = fetch_rows(block_refs, buffer, sems)
    total = before_ref[...] if has_before else None
    for (lo, hi), down_ref in zip(cuts, down_refs):
        term = lax.dot_general(rows[:, lo:hi], down_ref[...], NT, preferred_element_type=jnp.float32)
        total = term if total is None else total + term
    if has_by:
        columns = total.shape[1]
        out_ref[:, :columns] = (total * by_ref[:, :columns]).astype(jnp.bfloat16)
        out_ref[:, columns:] = (total * by_ref[:, columns:]).astype(jnp.bfloat16)
    else:
        out_ref[...] = total


def hidden_grads(grad_blocks, downs, cuts, by=None, before=None):
    blocks = len(grad_blocks)
    block, width = grad_blocks[0].shape
    columns = downs[0].shape[0]
    tile = 2 * block

    def rows(count):
        return pl.BlockSpec((tile, count), lambda i: (i, 0))

    given = [x for x in (by, before) if x is not None]
    out_columns, out_type = (columns, jnp.float32) if by is None else (2 * columns, jnp.bfloat16)
    return pl.pallas_call(
        functools.partial(grads_kernel, blocks, tuple(cuts), by is not None, before is not None),
        grid=(blocks // 2,),
        in_specs=[rows(x.shape[1]) for x in given]
        + [resident(d.shape, lambda i: (0, 0)) for d in downs]
        + [pl.BlockSpec(memory_space=pl.ANY)] * blocks,
        out_specs=rows(out_columns),
        out_shape=jax.ShapeDtypeStruct((blocks * block, out_columns), out_type),
        scratch_shapes=[
            pltpu.VMEM((blocks, block, width), jnp.bfloat16),
            pltpu.SemaphoreType.DMA((blocks,)),
        ],
        compiler_params=compiler_params(),
        cost_estimate=AT_ONCE,
        name="hidden_grads",
    )(*given, *downs, *grad_blocks)


def store_half(total, keep_ref, send_ref):
    @pl.when(pl.program_id(0) == 0)
    def _():
        send_ref[...] = total.astype(send_ref.dtype)

    @pl.when(pl.program_id(0) == 1)
    def _():
        keep_ref[...] = total


def mix_kernel(own_ref, other_ref, own_down_ref, other_down_ref, keep_ref, send_ref):
    total = jnp.dot(own_ref[...], own_down_ref[...], preferred_element_type=jnp.float32)
    total += jnp.dot(other_ref[...], other_down_ref[...], preferred_element_type=jnp.float32)
    store_half(total, keep_ref, send_ref)


def back_kernel(own_ref, other_ref, *refs):
    weight_refs, (keep_ref, send_ref) = refs[:-2], refs[-2:]
    experts, _, hidden = weight_refs[0].shape
    total = None
    for at, weight_ref in enumerate(weight_refs):
        grads_ref = (own_ref, other_ref)[at // 2]
        for e in range(experts):
            first = (at % 2 * experts + e) * hidden
            term = lax.dot_general(
                grads_ref[:, first : first + hidden], weight_ref[e], NT, preferred_element_type=jnp.float32
            )
            total = term if total is None else total + term
    store_half(total, keep_ref, send_ref)


def sum_columns(kernel, name, columns, own, other, weights, weight_specs):
    half, depth = own.shape[0] // 2, own.shape[1]
    rows = pl.BlockSpec((half, depth), lambda i: (1 - i, 0))
    return pl.pallas_call(
        kernel,
        grid=(2,),
        in_specs=[rows, rows] + weight_specs,
        out_specs=[pl.BlockSpec((half, columns), lambda i: (0, 0))] * 2,
        out_shape=[
            jax.ShapeDtypeStruct((half, columns), jnp.float32),
            jax.ShapeDtypeStruct((half, columns), jnp.bfloat16),
        ],
        compiler_params=compiler_params(),
        cost_estimate=AT_ONCE,
        name=name,
    )(own, other, *weights)


def mix_columns(own, other, own_down, other_down, at):
    depth, columns = other_down.shape
    specs = [
        resident((depth, columns), lambda i: (0, at)),
        resident((depth, columns), lambda i: (0, 0)),
    ]
    return sum_columns(mix_kernel, "mix_columns", columns, own, other, [own_down, other_down], specs)


def back_columns(own, other, weights, at, columns):
    experts, _, hidden = weights[0].shape
    specs = [resident((experts, columns, hidden), lambda i: (0, at, 0))] * len(weights)
    return sum_columns(back_kernel, "back_columns", columns, own, other, weights, specs)


def add_kernel(keep_ref, come_ref, *out_refs):
    block = out_refs[0].shape[0]
    for k, out_ref in enumerate(out_refs):
        cut = slice(k * block, (k + 1) * block)
        total = keep_ref[cut, :] + come_ref[cut, :].astype(jnp.float32)
        out_ref[...] = total.astype(out_ref.dtype)


def add_sides(keep, come, types):
    block, columns = keep.shape[0] // len(types), keep.shape[1]
    return pl.pallas_call(
        add_kernel,
        out_shape=[jax.ShapeDtypeStruct((block, columns), t) for t in types],
        compiler_params=compiler_params(),
        cost_estimate=AT_ONCE,
        name="add_sides",
    )(keep, come)


def add_piece(piece, come):
    return pl.pallas_call(
        add_kernel,
        out_shape=jax.ShapeDtypeStruct(piece.shape, jnp.bfloat16),
        compiler_params=compiler_params(),
        cost_estimate=AT_ONCE,
        name="add_piece",
    )(piece, come)


def finish_kernel(chunks, counts, *refs):
    out_ref = refs[-1]
    refs = list(refs[:-1])
    for (lo, hi), count in zip(chunks, counts):
        own_ref, *piece_refs = refs[:count]
        del refs[:count]
        total = own_ref[...]
        for piece_ref in piece_refs:
            total += piece_ref[...].astype(jnp.float32)
        out_ref[:, lo:hi] = total


def finish(chunks, parts, width):
    return pl.pallas_call(
        functools.partial(finish_kernel, tuple(chunks), tuple(map(len, parts))),
        out_shape=jax.ShapeDtypeStruct((parts[0][0].shape[0], width), jnp.float32),
        compiler_params=compiler_params(),
        cost_estimate=AT_ONCE,
        name="finish",
    )(*[p for part in parts for p in part])


def cut_columns(width, eighths):
    eighth = width // 8
    return [(lo * eighth, hi * eighth) for lo, hi in eighths]


def after(values, *others):
    return lax.optimization_barrier((values, *others))[0]


def send_all(sends, *waits):
    values, _ = lax.optimization_barrier(([v for v, _ in sends], waits))
    return [lax.ppermute(v, "expert", pairs) for v, (_, pairs) in zip(values, sends)]


def on_device_dense(tokens, cotangent, expert_ids, probs, gate_weight, up_weight, down_weight):
    local_count, hidden, width = down_weight.shape
    devices = lax.axis_size("expert")
    layers = devices // 4
    experts = local_count * devices
    block = tokens.shape[0]
    chunks = cut_columns(width, ((6, 8), (0, 3), (3, 6)))
    back_chunks = cut_columns(width, ((0, 3), (3, 6), (6, 8)))
    me = lax.axis_index("expert")
    twin = [(d, d ^ 1) for d in range(devices)]
    side = [(d, d ^ 2) for d in range(devices)]
    layer = [[(d, (d + 4 * k) % devices) for d in range(devices)] for k in range(layers)]

    labels = lax.broadcasted_iota(jnp.int32, (1, 1, experts), 2)
    weight = jnp.sum(jnp.where(expert_ids[:, :, None] == labels, probs[:, :, None], 0.0), axis=1)
    first = lax.reduce_precision(weight, 8, 7)
    second = lax.reduce_precision(weight - first, 8, 7)
    third = weight - first - second
    spare = jnp.zeros((block, -3 * experts % 128), jnp.bfloat16)
    terms = [t.astype(jnp.bfloat16) for t in (first, second, third)]
    row = jnp.concatenate([tokens] + terms + [spare], axis=1)
    grad = cotangent
    down = down_weight.reshape(local_count * hidden, width)
    downs = [down[:, lo:hi] for lo, hi in chunks]

    one, last, *middle = [1, layers - 1, *range(2, layers - 1)]
    rows, far_rows, grads, far_grads = {0: row}, {}, {0: grad}, {}
    other_gate, rows[one], far_rows[0] = send_all([(gate_weight, twin), (row, layer[-one]), (row, side)])
    rows[last], far_grads[0] = send_all([(row, layer[-last]), (grad, side)])
    (far_rows[one],) = send_all([(rows[one], side)], far_rows[0])
    for k in middle:
        (rows[k],) = send_all([(rows[k - 1], layer[-one])], far_rows[0])
    other_up, far_rows[last] = send_all([(up_weight, twin), (rows[last], side)], far_grads[0])
    got = send_all([(grad, layer[-one])] + [(rows[k], side) for k in middle], far_rows[one])
    grads[one] = got[0]
    far_rows.update(zip(middle, got[1:]))
    (grads[last],) = send_all([(grad, layer[-last])], far_rows[last])
    (down_0,) = send_all([(downs[0], twin)], far_rows[last], other_gate)
    (far_grads[one],) = send_all([(grads[one], side)], *far_rows.values())
    for k in middle:
        (grads[k],) = send_all([(grads[k - 1], layer[-one])], *far_rows.values())
    (far_grads[last],) = send_all([(grads[last], side)], *far_rows.values())
    row_blocks = [rows[k] for k in range(layers)] + [far_rows[k] for k in range(layers)]
    activ, by = hidden_forward(row_blocks, me, gate_weight, up_weight, experts)
    for k in middle:
        (far_grads[k],) = send_all([(grads[k], side)], far_grads[one], activ)
    other_up = after(other_up, activ)
    other_activ, other_by = hidden_forward(row_blocks, me ^ 1, other_gate, other_up, experts)

    (down_1,) = send_all([(downs[1], twin)], down_0, activ, other_activ)

    def mix(c, other_down, *waits):
        lo, hi = chunks[c]
        return mix_columns(activ, other_activ, down, after(other_down, *waits), lo // (hi - lo))

    types = [jnp.float32, jnp.float32] + [jnp.bfloat16] * (layers - 2)

    def send_on(pieces, *waits):
        (far,) = send_all([(pieces[-1], layer[last])], *waits)
        come = None
        for k in reversed(middle):
            piece = pieces[k - 1] if come is None else add_piece(pieces[k - 1], come)
            (come,) = send_all([(piece, layer[one])], *waits)
        return far, come

    def send_last(pieces, come, *waits):
        piece = pieces[0].astype(jnp.bfloat16) if come is None else add_piece(pieces[0], come)
        return send_all([(piece, layer[one])], *waits)[0]

    keep_0, send = mix(0, down_0, other_activ, *far_grads.values())
    come_0, down_2 = send_all([(send, side), (downs[2], twin)])
    grad_blocks = [grads[k] for k in range(layers)] + [far_grads[k] for k in range(layers)]
    own_grads = hidden_grads(grad_blocks, [down], [(0, width)], by=by)

    keep_1, send = mix(1, down_1, send, own_grads)
    own_0, *pieces = add_sides(after(keep_0, send), come_0, types)
    (come_1,) = send_all([(send, side)])
    far_0, next_0 = send_on(pieces)
    near_0 = send_last(pieces, next_0, far_0)
    grad_blocks = [after(grad_blocks[0], next_0), *grad_blocks[1:]]
    other_grad = hidden_grads(grad_blocks, [down_0, down_1], chunks[:2])

    keep_2, send = mix(2, down_2, other_grad, near_0)
    (come_2,) = send_all([(send, side)], own_0)

    other_by = after(other_by, send)
    other_grads = hidden_grads(grad_blocks, [down_2], chunks[2:], by=other_by, before=other_grad)
    weights = [gate_weight, up_weight, other_gate, other_up]

    def back(c, *waits):
        lo, hi = back_chunks[c]
        return back_columns(own_grads, after(other_grads, *waits), weights, lo // (hi - lo), hi - lo)

    keep_3, send = back(0)
    own_1, *pieces = add_sides(after(keep_1, send), come_1, types)
    (come_3,) = send_all([(send, side)], own_1)
    far_1, next_1 = send_on(pieces)
    near_1 = send_last(pieces, next_1, far_1)

    own_2, *pieces = add_sides(keep_2, after(come_2, next_1, far_1), types)
    far_2, next_2 = send_on(pieces)
    near_2 = send_last(pieces, next_2, far_2, near_1)
    keep_4, send = back(1, next_2, near_1)
    (come_4,) = send_all([(send, side)], own_2)

    keep_5, send = back(2, next_2)
    own_3, *pieces = add_sides(after(keep_3, send), come_3, types)
    (come_5,) = send_all([(send, side)], own_3)
    far_3, next_3 = send_on(pieces)
    near_3 = send_last(pieces, next_3, far_3, near_2)
    mixed = finish(chunks, [(own_0, far_0, near_0), (own_1, far_1, near_1), (own_2, far_2, near_2)], width)

    own_4, *pieces = add_sides(after(keep_4, mixed), after(come_4, next_3), types)
    far_4, next_4 = send_on(pieces)
    near_4 = send_last(pieces, next_4, far_4)

    types = [jnp.float32] + [jnp.bfloat16] * (layers - 1)
    own_5, *pieces = add_sides(keep_5, after(come_5, own_4), types)
    parts_5 = send_all([(piece, layer[k]) for k, piece in enumerate(pieces, 1)], near_3)
    back_parts = [(own_3, far_3, near_3), (own_4, far_4, near_4), (own_5, *parts_5)]
    return (mixed, finish(back_chunks, back_parts, width))


def route_slots(expert_ids, local_count, device_count, capacity):
    experts = local_count * device_count
    row_count = expert_ids.shape[0] * expert_ids.shape[1]
    flat_ids = expert_ids.reshape(row_count)
    sort_order = jnp.argsort(flat_ids, stable=True)
    labels = lax.broadcasted_iota(jnp.int32, (1, experts), 1)
    counts = jnp.sum((flat_ids[:, None] == labels).astype(jnp.int32), axis=0)
    starts = jnp.cumsum(counts) - counts
    sorted_ids = flat_ids[sort_order]
    rank_within = jnp.arange(row_count, dtype=jnp.int32) - starts[sorted_ids]
    owner = sorted_ids // local_count
    local_slot = sorted_ids % local_count
    target = local_slot * (device_count * capacity) + owner * capacity + rank_within
    source_of = jnp.full((experts * capacity,), row_count, jnp.int32).at[target].set(sort_order)
    target_of = jnp.zeros((row_count,), jnp.int32).at[sort_order].set(target)
    return (source_of, target_of)


def pack_rows(values, source_of, top_count, local_count):
    token_count = values.shape[0]
    with_zero = jnp.concatenate([values, jnp.zeros((1, values.shape[1]), values.dtype)], axis=0)
    token_index = jnp.minimum(source_of // top_count, token_count)
    picked = with_zero[token_index]
    return picked.reshape(local_count, -1, values.shape[1])


def forward_part(received, gate_weight, up_weight, down_weight):
    gate_pre = jnp.einsum("erd,edh->erh", received, gate_weight, preferred_element_type=jnp.float32)
    up_pre = jnp.einsum("erd,edh->erh", received, up_weight, preferred_element_type=jnp.float32)
    sigmoid_gate = jax.nn.sigmoid(gate_pre)
    activ = (gate_pre * sigmoid_gate * up_pre).astype(jnp.bfloat16)
    expert_out = jnp.einsum("erh,ehd->erd", activ, down_weight, preferred_element_type=jnp.float32)
    return (expert_out.astype(jnp.bfloat16), gate_pre, up_pre, sigmoid_gate)


def backward_part(grad_rows, gate_pre, up_pre, sigmoid_gate, gate_weight, up_weight, down_weight):
    grad_act = jnp.einsum(
        "erd,ehd->erh", grad_rows, down_weight, preferred_element_type=jnp.float32
    )
    grad_gate = (grad_act * up_pre * sigmoid_gate * (1.0 + gate_pre * (1.0 - sigmoid_gate))).astype(
        jnp.bfloat16
    )
    grad_up = (grad_act * gate_pre * sigmoid_gate).astype(jnp.bfloat16)
    joined_grad = jnp.concatenate([grad_gate, grad_up], axis=2)
    joined_weight = jnp.concatenate([gate_weight, up_weight], axis=2)
    expert_back = jnp.einsum(
        "erh,edh->erd", joined_grad, joined_weight, preferred_element_type=jnp.float32
    )
    return expert_back.astype(jnp.bfloat16)


def combine_rows(returned, target_of, probs):
    token_count, top_count = probs.shape
    flat_back = returned.reshape(-1, returned.shape[2])
    picked = flat_back[target_of].reshape(token_count, top_count, returned.shape[2])
    return jnp.sum(picked.astype(jnp.float32) * probs[:, :, None], axis=1)


def on_device_routed(tokens, cotangent, expert_ids, probs, gate_weight, up_weight, down_weight):
    local_count = gate_weight.shape[0]
    device_count = lax.axis_size("expert")
    experts = local_count * device_count
    token_count, top_count = expert_ids.shape
    row_count = token_count * top_count
    capacity = row_count * 6 // (5 * experts)
    source_of, target_of = route_slots(expert_ids, local_count, device_count, capacity)
    send_rows = pack_rows(tokens, source_of, top_count, local_count)
    send_grads = pack_rows(cotangent, source_of, top_count, local_count)
    received = lax.all_to_all(send_rows, "expert", split_axis=1, concat_axis=1, tiled=True)
    expert_out, gate_pre, up_pre, sigmoid_gate = forward_part(
        received, gate_weight, up_weight, down_weight
    )
    returned_out = lax.all_to_all(expert_out, "expert", split_axis=1, concat_axis=1, tiled=True)
    received_grads = lax.all_to_all(send_grads, "expert", split_axis=1, concat_axis=1, tiled=True)
    expert_back = backward_part(
        received_grads, gate_pre, up_pre, sigmoid_gate, gate_weight, up_weight, down_weight
    )
    returned_back = lax.all_to_all(expert_back, "expert", split_axis=1, concat_axis=1, tiled=True)
    mixed = combine_rows(returned_out, target_of, probs)
    input_grad = combine_rows(returned_back, target_of, probs)
    return (mixed, input_grad)


def on_device(tokens, cotangent, expert_ids, probs, gate_weight, up_weight, down_weight):
    devices = lax.axis_size("expert")
    dense = devices % 4 == 0 and 12 <= devices <= 2 * expert_ids.shape[1]
    body = on_device_dense if dense else on_device_routed
    return body(tokens, cotangent, expert_ids, probs, gate_weight, up_weight, down_weight)


def solution(mesh):
    in_specs = (
        P(("dp", "expert"), None),
        P(("dp", "expert"), None),
        P(("dp", "expert"), None),
        P(("dp", "expert"), None),
        P(("dp", "expert"), None, None),
        P(("dp", "expert"), None, None),
        P(("dp", "expert"), None, None),
    )
    out_specs = (P(("dp", "expert"), None), P(("dp", "expert"), None))
    return jax.shard_map(
        on_device, mesh=mesh, in_specs=in_specs, out_specs=out_specs, check_vma=False
    )
```

```python
import functools

import jax
import jax.numpy as jnp
from jax import lax
from jax.experimental import pallas as pl
from jax.experimental.pallas import tpu as pltpu
from jax.sharding import PartitionSpec as P

VMEM_BYTES = 18 * 2**20
VMEM_BYTES_FETCH = 56 * 2**20
AT_ONCE = pl.CostEstimate(flops=1, bytes_accessed=1, transcendentals=0)


def resident(shape, index):
    return pl.BlockSpec(shape, index, pipeline_mode=pl.Buffered(1))


def compiler_params(vmem_bytes=VMEM_BYTES):
    return pltpu.CompilerParams(vmem_limit_bytes=vmem_bytes)


def fetch_rows(block_refs, buffer, sems):
    step = pl.program_id(0)
    count = len(block_refs) // pl.num_programs(0)

    @pl.when(step == 0)
    def _():
        for j, ref in enumerate(block_refs):
            pltpu.make_async_copy(ref, buffer.at[j], sems.at[j]).start()

    for j in range(len(block_refs)):

        @pl.when(step == j // count)
        def _(j=j):
            pltpu.make_async_copy(block_refs[j], buffer.at[j], sems.at[j]).wait()

    rows = buffer[pl.ds(step * count, count)]
    return rows.reshape(count * rows.shape[1], rows.shape[2])


def hidden_kernel(blocks, all_experts, owner_ref, gate_ref, up_ref, *refs):
    activ_ref, by_ref, buffer, sems = refs[blocks:]
    experts, width, hidden = gate_ref.shape
    rows = fetch_rows(refs[:blocks], buffer, sems)
    terms = rows[:, width:].astype(jnp.float32)
    rows = rows[:, :width]
    lanes = lax.broadcasted_iota(jnp.int32, terms.shape, 1)
    for e in range(experts):
        cut = slice(e * hidden, (e + 1) * hidden)
        cut_up = slice((experts + e) * hidden, (experts + e + 1) * hidden)
        label = owner_ref[0] * experts + e
        named = (lanes == label) | (lanes == label + all_experts) | (lanes == label + 2 * all_experts)
        weight = jnp.sum(jnp.where(named, terms, 0.0), axis=1, keepdims=True)
        gate_pre = jnp.dot(rows, gate_ref[e], preferred_element_type=jnp.float32)
        up_pre = jnp.dot(rows, up_ref[e], preferred_element_type=jnp.float32)
        sig = jax.nn.sigmoid(gate_pre)
        factor = sig * weight
        silu = gate_pre * factor
        activ_ref[:, cut] = (silu * up_pre).astype(jnp.bfloat16)
        by_ref[:, cut] = up_pre * factor * (1.0 + gate_pre * (1.0 - sig))
        by_ref[:, cut_up] = silu


def hidden_forward(row_blocks, owner, gate_weight, up_weight, all_experts):
    blocks = len(row_blocks)
    block, row_width = row_blocks[0].shape
    experts, width, hidden = gate_weight.shape
    count, columns, tile = blocks * block, experts * hidden, 2 * block
    weights = resident((experts, width, hidden), lambda i: (0, 0, 0))
    return pl.pallas_call(
        functools.partial(hidden_kernel, blocks, all_experts),
        grid=(blocks // 2,),
        in_specs=[pl.BlockSpec(memory_space=pltpu.SMEM), weights, weights]
        + [pl.BlockSpec(memory_space=pl.ANY)] * blocks,
        out_specs=[
            pl.BlockSpec((tile, columns), lambda i: (i, 0)),
            pl.BlockSpec((tile, 2 * columns), lambda i: (i, 0)),
        ],
        out_shape=[
            jax.ShapeDtypeStruct((count, columns), jnp.bfloat16),
            jax.ShapeDtypeStruct((count, 2 * columns), jnp.float32),
        ],
        scratch_shapes=[
            pltpu.VMEM((blocks, block, row_width), jnp.bfloat16),
            pltpu.SemaphoreType.DMA((blocks,)),
        ],
        compiler_params=compiler_params(VMEM_BYTES_FETCH),
        cost_estimate=AT_ONCE,
        name="hidden_forward",
    )(owner.reshape(1), gate_weight, up_weight, *row_blocks)


NT = (((1,), (1,)), ((), ()))


def grads_kernel(blocks, cuts, has_by, has_before, *refs):
    refs = list(refs)
    by_ref = refs.pop(0) if has_by else None
    before_ref = refs.pop(0) if has_before else None
    down_refs, block_refs = refs[: len(cuts)], refs[len(cuts) : len(cuts) + blocks]
    out_ref, buffer, sems = refs[len(cuts) + blocks :]
    rows = fetch_rows(block_refs, buffer, sems)
    total = before_ref[...] if has_before else None
    for (lo, hi), down_ref in zip(cuts, down_refs):
        term = lax.dot_general(rows[:, lo:hi], down_ref[...], NT, preferred_element_type=jnp.float32)
        total = term if total is None else total + term
    if has_by:
        columns = total.shape[1]
        out_ref[:, :columns] = (total * by_ref[:, :columns]).astype(jnp.bfloat16)
        out_ref[:, columns:] = (total * by_ref[:, columns:]).astype(jnp.bfloat16)
    else:
        out_ref[...] = total


def hidden_grads(grad_blocks, downs, cuts, by=None, before=None):
    blocks = len(grad_blocks)
    block, width = grad_blocks[0].shape
    columns = downs[0].shape[0]
    tile = 2 * block

    def rows(count):
        return pl.BlockSpec((tile, count), lambda i: (i, 0))

    given = [x for x in (by, before) if x is not None]
    out_columns, out_type = (columns, jnp.float32) if by is None else (2 * columns, jnp.bfloat16)
    return pl.pallas_call(
        functools.partial(grads_kernel, blocks, tuple(cuts), by is not None, before is not None),
        grid=(blocks // 2,),
        in_specs=[rows(x.shape[1]) for x in given]
        + [resident(d.shape, lambda i: (0, 0)) for d in downs]
        + [pl.BlockSpec(memory_space=pl.ANY)] * blocks,
        out_specs=rows(out_columns),
        out_shape=jax.ShapeDtypeStruct((blocks * block, out_columns), out_type),
        scratch_shapes=[
            pltpu.VMEM((blocks, block, width), jnp.bfloat16),
            pltpu.SemaphoreType.DMA((blocks,)),
        ],
        compiler_params=compiler_params(),
        cost_estimate=AT_ONCE,
        name="hidden_grads",
    )(*given, *downs, *grad_blocks)


def store_half(total, keep_ref, send_ref):
    @pl.when(pl.program_id(0) == 0)
    def _():
        send_ref[...] = total.astype(send_ref.dtype)

    @pl.when(pl.program_id(0) == 1)
    def _():
        keep_ref[...] = total


def mix_kernel(own_ref, other_ref, own_down_ref, other_down_ref, keep_ref, send_ref):
    total = jnp.dot(own_ref[...], own_down_ref[...], preferred_element_type=jnp.float32)
    total += jnp.dot(other_ref[...], other_down_ref[...], preferred_element_type=jnp.float32)
    store_half(total, keep_ref, send_ref)


def back_kernel(own_ref, other_ref, *refs):
    weight_refs, (keep_ref, send_ref) = refs[:-2], refs[-2:]
    experts, _, hidden = weight_refs[0].shape
    total = None
    for at, weight_ref in enumerate(weight_refs):
        grads_ref = (own_ref, other_ref)[at // 2]
        for e in range(experts):
            first = (at % 2 * experts + e) * hidden
            term = lax.dot_general(
                grads_ref[:, first : first + hidden], weight_ref[e], NT, preferred_element_type=jnp.float32
            )
            total = term if total is None else total + term
    store_half(total, keep_ref, send_ref)


def sum_columns(kernel, name, columns, own, other, weights, weight_specs):
    half, depth = own.shape[0] // 2, own.shape[1]
    rows = pl.BlockSpec((half, depth), lambda i: (1 - i, 0))
    return pl.pallas_call(
        kernel,
        grid=(2,),
        in_specs=[rows, rows] + weight_specs,
        out_specs=[pl.BlockSpec((half, columns), lambda i: (0, 0))] * 2,
        out_shape=[
            jax.ShapeDtypeStruct((half, columns), jnp.float32),
            jax.ShapeDtypeStruct((half, columns), jnp.bfloat16),
        ],
        compiler_params=compiler_params(),
        cost_estimate=AT_ONCE,
        name=name,
    )(own, other, *weights)


def mix_columns(own, other, own_down, other_down, at):
    depth, columns = other_down.shape
    specs = [
        resident((depth, columns), lambda i: (0, at)),
        resident((depth, columns), lambda i: (0, 0)),
    ]
    return sum_columns(mix_kernel, "mix_columns", columns, own, other, [own_down, other_down], specs)


def back_columns(own, other, weights, at, columns):
    experts, _, hidden = weights[0].shape
    specs = [resident((experts, columns, hidden), lambda i: (0, at, 0))] * len(weights)
    return sum_columns(back_kernel, "back_columns", columns, own, other, weights, specs)


def add_kernel(keep_ref, come_ref, *out_refs):
    block = out_refs[0].shape[0]
    for k, out_ref in enumerate(out_refs):
        cut = slice(k * block, (k + 1) * block)
        total = keep_ref[cut, :] + come_ref[cut, :].astype(jnp.float32)
        out_ref[...] = total.astype(out_ref.dtype)


def add_sides(keep, come, types):
    block, columns = keep.shape[0] // len(types), keep.shape[1]
    return pl.pallas_call(
        add_kernel,
        out_shape=[jax.ShapeDtypeStruct((block, columns), t) for t in types],
        compiler_params=compiler_params(),
        cost_estimate=AT_ONCE,
        name="add_sides",
    )(keep, come)


def add_piece(piece, come):
    return pl.pallas_call(
        add_kernel,
        out_shape=jax.ShapeDtypeStruct(piece.shape, jnp.bfloat16),
        compiler_params=compiler_params(),
        cost_estimate=AT_ONCE,
        name="add_piece",
    )(piece, come)


def finish_kernel(chunks, counts, *refs):
    out_ref = refs[-1]
    refs = list(refs[:-1])
    for (lo, hi), count in zip(chunks, counts):
        own_ref, *piece_refs = refs[:count]
        del refs[:count]
        total = own_ref[...]
        for piece_ref in piece_refs:
            total += piece_ref[...].astype(jnp.float32)
        out_ref[:, lo:hi] = total


def finish(chunks, parts, width):
    return pl.pallas_call(
        functools.partial(finish_kernel, tuple(chunks), tuple(map(len, parts))),
        out_shape=jax.ShapeDtypeStruct((parts[0][0].shape[0], width), jnp.float32),
        compiler_params=compiler_params(),
        cost_estimate=AT_ONCE,
        name="finish",
    )(*[p for part in parts for p in part])


def cut_columns(width, eighths):
    eighth = width // 8
    return [(lo * eighth, hi * eighth) for lo, hi in eighths]


def after(values, *others):
    return lax.optimization_barrier((values, *others))[0]


def send_all(sends, *waits):
    values, _ = lax.optimization_barrier(([v for v, _ in sends], waits))
    return [lax.ppermute(v, "expert", pairs) for v, (_, pairs) in zip(values, sends)]


def on_device_dense(tokens, cotangent, expert_ids, probs, gate_weight, up_weight, down_weight):
    local_count, hidden, width = down_weight.shape
    devices = lax.axis_size("expert")
    layers = devices // 4
    experts = local_count * devices
    block = tokens.shape[0]
    chunks = cut_columns(width, ((6, 8), (0, 3), (3, 6)))
    back_chunks = cut_columns(width, ((0, 4), (4, 6), (6, 8)))
    me = lax.axis_index("expert")
    twin = [(d, d ^ 1) for d in range(devices)]
    side = [(d, d ^ 2) for d in range(devices)]
    layer = [[(d, (d + 4 * k) % devices) for d in range(devices)] for k in range(layers)]

    labels = lax.broadcasted_iota(jnp.int32, (1, 1, experts), 2)
    weight = jnp.sum(jnp.where(expert_ids[:, :, None] == labels, probs[:, :, None], 0.0), axis=1)
    first = lax.reduce_precision(weight, 8, 7)
    second = lax.reduce_precision(weight - first, 8, 7)
    third = weight - first - second
    spare = jnp.zeros((block, -3 * experts % 128), jnp.bfloat16)
    terms = [t.astype(jnp.bfloat16) for t in (first, second, third)]
    row = jnp.concatenate([tokens] + terms + [spare], axis=1)
    grad = cotangent
    down = down_weight.reshape(local_count * hidden, width)
    downs = [down[:, lo:hi] for lo, hi in chunks]

    one, last, *middle = [1, layers - 1, *range(2, layers - 1)]
    rows, far_rows, grads, far_grads = {0: row}, {}, {0: grad}, {}
    other_gate, rows[one], far_rows[0] = send_all([(gate_weight, twin), (row, layer[-one]), (row, side)])
    rows[last], far_grads[0] = send_all([(row, layer[-last]), (grad, side)])
    (far_rows[one],) = send_all([(rows[one], side)], far_rows[0])
    for k in middle:
        (rows[k],) = send_all([(rows[k - 1], layer[-one])], far_rows[0])
    other_up, far_rows[last] = send_all([(up_weight, twin), (rows[last], side)], far_grads[0])
    got = send_all([(grad, layer[-one])] + [(rows[k], side) for k in middle], far_rows[one])
    grads[one] = got[0]
    far_rows.update(zip(middle, got[1:]))
    (grads[last],) = send_all([(grad, layer[-last])], far_rows[last])
    (down_0,) = send_all([(downs[0], twin)], far_rows[last], other_gate)
    (far_grads[one],) = send_all([(grads[one], side)], *far_rows.values())
    for k in middle:
        (grads[k],) = send_all([(grads[k - 1], layer[-one])], *far_rows.values())
    (far_grads[last],) = send_all([(grads[last], side)], *far_rows.values())
    row_blocks = [rows[k] for k in range(layers)] + [far_rows[k] for k in range(layers)]
    activ, by = hidden_forward(row_blocks, me, gate_weight, up_weight, experts)
    for k in middle:
        (far_grads[k],) = send_all([(grads[k], side)], far_grads[one], activ)
    other_up = after(other_up, activ)
    other_activ, other_by = hidden_forward(row_blocks, me ^ 1, other_gate, other_up, experts)

    (down_1,) = send_all([(downs[1], twin)], down_0, activ, other_activ)

    def mix(c, other_down, *waits):
        lo, hi = chunks[c]
        return mix_columns(activ, other_activ, down, after(other_down, *waits), lo // (hi - lo))

    types = [jnp.float32, jnp.float32] + [jnp.bfloat16] * (layers - 2)

    def send_on(pieces, *waits):
        (far,) = send_all([(pieces[-1], layer[last])], *waits)
        come = None
        for k in reversed(middle):
            piece = pieces[k - 1] if come is None else add_piece(pieces[k - 1], come)
            (come,) = send_all([(piece, layer[one])], *waits)
        return far, come

    def send_last(pieces, come, *waits):
        piece = pieces[0].astype(jnp.bfloat16) if come is None else add_piece(pieces[0], come)
        return send_all([(piece, layer[one])], *waits)[0]

    keep_0, send = mix(0, down_0, other_activ, *far_grads.values())
    come_0, down_2 = send_all([(send, side), (downs[2], twin)])
    grad_blocks = [grads[k] for k in range(layers)] + [far_grads[k] for k in range(layers)]
    own_grads = hidden_grads(grad_blocks, [down], [(0, width)], by=by)

    keep_1, send = mix(1, down_1, send, own_grads)
    own_0, *pieces = add_sides(after(keep_0, send), come_0, types)
    (come_1,) = send_all([(send, side)])
    far_0, next_0 = send_on(pieces)
    near_0 = send_last(pieces, next_0, far_0)
    grad_blocks = [after(grad_blocks[0], next_0), *grad_blocks[1:]]
    other_grad = hidden_grads(grad_blocks, [down_0, down_1], chunks[:2])

    keep_2, send = mix(2, down_2, other_grad, near_0)
    (come_2,) = send_all([(send, side)], own_0)

    other_by = after(other_by, send)
    other_grads = hidden_grads(grad_blocks, [down_2], chunks[2:], by=other_by, before=other_grad)
    weights = [gate_weight, up_weight, other_gate, other_up]

    def back(c, *waits):
        lo, hi = back_chunks[c]
        return back_columns(own_grads, after(other_grads, *waits), weights, lo // (hi - lo), hi - lo)

    keep_3, send = back(0)
    own_1, *pieces = add_sides(after(keep_1, send), come_1, types)
    (come_3,) = send_all([(send, side)], own_1)
    far_1, next_1 = send_on(pieces)
    near_1 = send_last(pieces, next_1, far_1)

    own_2, *pieces = add_sides(keep_2, after(come_2, next_1, far_1), types)
    far_2, next_2 = send_on(pieces)
    near_2 = send_last(pieces, next_2, far_2, near_1)
    keep_4, send = back(1, next_2, near_1)
    (come_4,) = send_all([(send, side)], own_2)

    keep_5, send = back(2, next_2)
    own_3, *pieces = add_sides(after(keep_3, send), come_3, types)
    (come_5,) = send_all([(send, side)], own_3)
    far_3, next_3 = send_on(pieces)
    near_3 = send_last(pieces, next_3, far_3, near_2)
    mixed = finish(chunks, [(own_0, far_0, near_0), (own_1, far_1, near_1), (own_2, far_2, near_2)], width)

    own_4, *pieces = add_sides(after(keep_4, mixed), after(come_4, next_3), types)
    far_4, next_4 = send_on(pieces)
    near_4 = send_last(pieces, next_4, far_4)

    types = [jnp.float32] + [jnp.bfloat16] * (layers - 1)
    own_5, *pieces = add_sides(keep_5, after(come_5, own_4), types)
    parts_5 = send_all([(piece, layer[k]) for k, piece in enumerate(pieces, 1)], near_3)
    back_parts = [(own_3, far_3, near_3), (own_4, far_4, near_4), (own_5, *parts_5)]
    return (mixed, finish(back_chunks, back_parts, width))


def route_slots(expert_ids, local_count, device_count, capacity):
    experts = local_count * device_count
    row_count = expert_ids.shape[0] * expert_ids.shape[1]
    flat_ids = expert_ids.reshape(row_count)
    sort_order = jnp.argsort(flat_ids, stable=True)
    labels = lax.broadcasted_iota(jnp.int32, (1, experts), 1)
    counts = jnp.sum((flat_ids[:, None] == labels).astype(jnp.int32), axis=0)
    starts = jnp.cumsum(counts) - counts
    sorted_ids = flat_ids[sort_order]
    rank_within = jnp.arange(row_count, dtype=jnp.int32) - starts[sorted_ids]
    owner = sorted_ids // local_count
    local_slot = sorted_ids % local_count
    target = local_slot * (device_count * capacity) + owner * capacity + rank_within
    source_of = jnp.full((experts * capacity,), row_count, jnp.int32).at[target].set(sort_order)
    target_of = jnp.zeros((row_count,), jnp.int32).at[sort_order].set(target)
    return (source_of, target_of)


def pack_rows(values, source_of, top_count, local_count):
    token_count = values.shape[0]
    with_zero = jnp.concatenate([values, jnp.zeros((1, values.shape[1]), values.dtype)], axis=0)
    token_index = jnp.minimum(source_of // top_count, token_count)
    picked = with_zero[token_index]
    return picked.reshape(local_count, -1, values.shape[1])


def forward_part(received, gate_weight, up_weight, down_weight):
    gate_pre = jnp.einsum("erd,edh->erh", received, gate_weight, preferred_element_type=jnp.float32)
    up_pre = jnp.einsum("erd,edh->erh", received, up_weight, preferred_element_type=jnp.float32)
    sigmoid_gate = jax.nn.sigmoid(gate_pre)
    activ = (gate_pre * sigmoid_gate * up_pre).astype(jnp.bfloat16)
    expert_out = jnp.einsum("erh,ehd->erd", activ, down_weight, preferred_element_type=jnp.float32)
    return (expert_out.astype(jnp.bfloat16), gate_pre, up_pre, sigmoid_gate)


def backward_part(grad_rows, gate_pre, up_pre, sigmoid_gate, gate_weight, up_weight, down_weight):
    grad_act = jnp.einsum(
        "erd,ehd->erh", grad_rows, down_weight, preferred_element_type=jnp.float32
    )
    grad_gate = (grad_act * up_pre * sigmoid_gate * (1.0 + gate_pre * (1.0 - sigmoid_gate))).astype(
        jnp.bfloat16
    )
    grad_up = (grad_act * gate_pre * sigmoid_gate).astype(jnp.bfloat16)
    joined_grad = jnp.concatenate([grad_gate, grad_up], axis=2)
    joined_weight = jnp.concatenate([gate_weight, up_weight], axis=2)
    expert_back = jnp.einsum(
        "erh,edh->erd", joined_grad, joined_weight, preferred_element_type=jnp.float32
    )
    return expert_back.astype(jnp.bfloat16)


def combine_rows(returned, target_of, probs):
    token_count, top_count = probs.shape
    flat_back = returned.reshape(-1, returned.shape[2])
    picked = flat_back[target_of].reshape(token_count, top_count, returned.shape[2])
    return jnp.sum(picked.astype(jnp.float32) * probs[:, :, None], axis=1)


def on_device_routed(tokens, cotangent, expert_ids, probs, gate_weight, up_weight, down_weight):
    local_count = gate_weight.shape[0]
    device_count = lax.axis_size("expert")
    experts = local_count * device_count
    token_count, top_count = expert_ids.shape
    row_count = token_count * top_count
    capacity = row_count * 6 // (5 * experts)
    source_of, target_of = route_slots(expert_ids, local_count, device_count, capacity)
    send_rows = pack_rows(tokens, source_of, top_count, local_count)
    send_grads = pack_rows(cotangent, source_of, top_count, local_count)
    received = lax.all_to_all(send_rows, "expert", split_axis=1, concat_axis=1, tiled=True)
    expert_out, gate_pre, up_pre, sigmoid_gate = forward_part(
        received, gate_weight, up_weight, down_weight
    )
    returned_out = lax.all_to_all(expert_out, "expert", split_axis=1, concat_axis=1, tiled=True)
    received_grads = lax.all_to_all(send_grads, "expert", split_axis=1, concat_axis=1, tiled=True)
    expert_back = backward_part(
        received_grads, gate_pre, up_pre, sigmoid_gate, gate_weight, up_weight, down_weight
    )
    returned_back = lax.all_to_all(expert_back, "expert", split_axis=1, concat_axis=1, tiled=True)
    mixed = combine_rows(returned_out, target_of, probs)
    input_grad = combine_rows(returned_back, target_of, probs)
    return (mixed, input_grad)


def on_device(tokens, cotangent, expert_ids, probs, gate_weight, up_weight, down_weight):
    devices = lax.axis_size("expert")
    dense = devices % 4 == 0 and 12 <= devices <= 2 * expert_ids.shape[1]
    body = on_device_dense if dense else on_device_routed
    return body(tokens, cotangent, expert_ids, probs, gate_weight, up_weight, down_weight)


def solution(mesh):
    in_specs = (
        P(("dp", "expert"), None),
        P(("dp", "expert"), None),
        P(("dp", "expert"), None),
        P(("dp", "expert"), None),
        P(("dp", "expert"), None, None),
        P(("dp", "expert"), None, None),
        P(("dp", "expert"), None, None),
    )
    out_specs = (P(("dp", "expert"), None), P(("dp", "expert"), None))
    return jax.shard_map(
        on_device, mesh=mesh, in_specs=in_specs, out_specs=out_specs, check_vma=False
    )
```
